128 devices in a mesh: dp: 16 (over z, y), value: 8 (over x, core).
Axes of the slice: x: 4, y: 4, z: 4, core: 2. Of those that a mesh axis runs over, the one named last changes fastest.
Arguments:
- inputs: bfloat16 [4, 512, 2048], P(None, 'dp'), may hold values from -6 to 6
- qk_weight: bfloat16 [2048, 4096], P(None, 'value'), may hold values from -0.125 to 0.125
- value_weight: bfloat16 [2048, 4096], P(None, 'value'), may hold values from -0.125 to 0.125
- output_gate_weight: bfloat16 [2048, 4096], P(None, 'value'), may hold values from -0.125 to 0.125
- rate_weight: bfloat16 [2048, 64], replicated, may hold values from -0.125 to 0.125
- log_decay: float32 [32], replicated, may hold values from -2.5 to 1.5
- decay_bias: float32 [32], replicated, may hold values from -1 to 1
- norm_gain: float32 [128], P('value'), may hold values from 0.1 to 1.9
- out_weight: bfloat16 [4096, 2048], P('value'), may hold values from -0.09375 to 0.09375
- states: float32 [512, 128, 32, 128], P('dp', 'value'), may hold values from -60 to 60, as said below
- prefilled: float32 [256, 128, 32, 128], P('dp', 'value'), may hold values from -60 to 60, as said below
- finished: int32 [4, 16, 2], replicated, may hold values from 0 to 31, as said below
- new_owner: int32 [4, 16, 2], replicated, may hold values from 0 to 15, as said below
- new_slot: int32 [4, 16, 2], replicated, may hold values from 0 to 15, as said below
Outputs:
- hidden_out: bfloat16 [4, 512, 2048], P(None, 'dp', 'value')
The draws below stay inside these ranges and needn't reach their ends.
Inputs may be any that keep to these rules, and one draw needn't show every extreme that they name: `states`: entries of a row are independent; the value entries have different scales. `prefilled`: drawn like states. `finished`: the 2 rows of one dp index in one step are distinct. `new_owner`: over all 4 steps, no two replacing rows of one dp index have the same owner. `new_slot`: no prefilled state is used twice.
All inputs are finite; a program needn't handle non-finite values.
Results may differ from the reference program's by a relative error of at most 0.006.
Values may be sent and summed in bfloat16 or wider, within the bound.
A program may use at most 128 MiB of HBM per device.

```python
import jax
import jax.numpy as jnp
from jax import lax

D = 2048
H = 32
KH = 16
DK = 128
DV = 128
ROWS_PER_RANK = 32
STEPS = 4
REPLACED = 2
ROWS = 512
POOL_DEV = 16
POOLS = 256
N_DP = 16


def column_rise():
    return (10.0 ** (jnp.arange(DV, dtype=jnp.float32) / (DV - 1))).reshape(1, DV, 1, 1)


def routing(key):
    total = STEPS * REPLACED
    row_keys = jax.random.split(jax.random.fold_in(key, 101), STEPS * N_DP)
    finished = jax.vmap(lambda sub: jax.random.permutation(sub, ROWS_PER_RANK)[:REPLACED])(row_keys)
    finished = finished.reshape(STEPS, N_DP, REPLACED).astype(jnp.int32)
    extra_reward = jax.random.randint(jax.random.fold_in(key, 103), (N_DP,), 0, 2)
    random_jitter = jax.random.randint(jax.random.fold_in(key, 102), (N_DP, N_DP), 0, 4096)
    rank_scores = (random_jitter + 2048 * extra_reward[None, :]) * N_DP + jnp.arange(N_DP, dtype=jnp.int32)[None, :]
    chosen = lax.top_k(rank_scores, total)[1].astype(jnp.int32)
    order_keys = jax.random.split(jax.random.fold_in(key, 104), N_DP)
    order = jax.vmap(lambda sub: jax.random.permutation(sub, total))(order_keys)
    owners = jnp.take_along_axis(chosen, order, axis=1)
    slot_keys = jax.random.split(jax.random.fold_in(key, 105), N_DP)
    perms = jax.vmap(lambda sub: jax.random.permutation(sub, POOL_DEV))(slot_keys)
    slots = perms[owners, jnp.arange(N_DP, dtype=jnp.int32)[:, None]]
    owners = jnp.transpose(owners.reshape(N_DP, STEPS, REPLACED), (1, 0, 2)).astype(jnp.int32)
    slots = jnp.transpose(slots.reshape(N_DP, STEPS, REPLACED), (1, 0, 2)).astype(jnp.int32)
    return (finished, owners, slots)


def draw_states(key, part):
    key = jax.random.fold_in(key, 11)
    shape = (ROWS, DV, H, DK)
    return jnp.clip(jax.random.normal(key, shape, jnp.float32), -6.0, 6.0) * column_rise()


def draw_prefilled(key, part):
    key = jax.random.fold_in(key, 12)
    shape = (POOLS, DV, H, DK)
    return jnp.clip(jax.random.normal(key, shape, jnp.float32), -6.0, 6.0) * column_rise()


def draw_finished(key, part):
    return routing(key)[0]


def draw_new_owner(key, part):
    return routing(key)[1]


def draw_new_slot(key, part):
    return routing(key)[2]


def level_of(key, dims, shards, low, high):
    def one(position, parts):
        draws = jax.random.uniform(jax.random.fold_in(jax.random.fold_in(key, 6), position), (parts,), jnp.float32, low / len(shards), high / len(shards))
        return jnp.repeat(jnp.exp(draws), dims[position] // parts).reshape((-1,) + (1,) * (len(dims) - position - 1))

    loudness = one(*shards[0])
    for cut in shards[1:]:
        loudness = loudness * one(*cut)
    return loudness


def noise(own_key, shape, spread, most, cuts=(), kind=jnp.bfloat16):
    entries = jax.random.normal(own_key, shape, jnp.float32) * spread
    if len(cuts) > 0:
        entries = level_of(own_key, shape, cuts, -0.22, 0.18) * entries
    return jnp.clip(entries, min=-most, max=most).astype(kind)


def setup_inputs(seed: int = 0) -> dict:
    key_list = jax.random.split(jax.random.key(seed), 15)
    inputs = noise(key_list[0], (STEPS, ROWS, D), 1.0, 6.0, ((1, 16),))
    qk_weight = noise(key_list[1], (D, 2 * KH * DK), D ** -0.5, 0.125, ((1, 8),))
    value_weight = noise(key_list[2], (D, DV * H), D ** -0.5, 0.125, ((1, 8),))
    output_gate_weight = noise(key_list[3], (D, DV * H), D ** -0.5, 0.125, ((1, 8),))
    rate_weight = noise(key_list[4], (D, 2 * H), D ** -0.5, 0.125)
    log_decay = jnp.clip(jax.random.uniform(key_list[5], (H,), jnp.float32, -2.5, 1.5), -2.5, 1.5)
    decay_bias = jnp.clip(jax.random.uniform(key_list[6], (H,), jnp.float32, -1.0, 1.0), -1.0, 1.0)
    norm_gain = jnp.clip(1.0 + 0.18 * jax.random.normal(key_list[7], (DV,), jnp.float32), 0.1, 1.9)
    out_weight = noise(key_list[8], (DV * H, D), (DV * H) ** -0.5, 0.09375, ((0, 8),))
    states = draw_states(jax.random.fold_in(key_list[14], 71), 0)
    prefilled = draw_prefilled(jax.random.fold_in(key_list[14], 71), 0)
    finished = draw_finished(jax.random.fold_in(key_list[14], 71), 0)
    new_owner = draw_new_owner(jax.random.fold_in(key_list[14], 71), 0)
    new_slot = draw_new_slot(jax.random.fold_in(key_list[14], 71), 0)
    return dict(inputs=inputs, qk_weight=qk_weight, value_weight=value_weight, output_gate_weight=output_gate_weight, rate_weight=rate_weight, log_decay=log_decay, decay_bias=decay_bias, norm_gain=norm_gain, out_weight=out_weight, states=states, prefilled=prefilled, finished=finished, new_owner=new_owner, new_slot=new_slot)


def normalized(heads):
    return heads * lax.rsqrt(lax.optimization_barrier(jnp.sum(heads * heads, axis=-1, keepdims=True)) + 1e-06)

def advance(states, inputs_now, qk_weight, value_weight, output_gate_weight, rate_weight, log_decay, decay_bias, norm_gain, out_weight):
    joined = jnp.dot(inputs_now, qk_weight, preferred_element_type=jnp.float32).astype(jnp.bfloat16)
    joined = lax.optimization_barrier(joined).astype(jnp.float32)
    split_at = KH * DK
    repeats = H // KH
    queries = normalized(joined[:, :split_at].reshape(-1, KH, DK)) * DK ** (-0.5)
    keys = normalized(joined[:, split_at:].reshape(-1, KH, DK))
    queries = jnp.repeat(queries, repeats, axis=1)
    keys = jnp.repeat(keys, repeats, axis=1)
    values = jnp.dot(inputs_now, value_weight, preferred_element_type=jnp.float32).reshape(-1, DV, H)
    gating = jnp.dot(inputs_now, output_gate_weight, preferred_element_type=jnp.float32).reshape(-1, DV, H)
    rates = jnp.dot(inputs_now, rate_weight, preferred_element_type=jnp.float32)
    strength = jax.nn.sigmoid(rates[:, :H])
    retain = jnp.exp(-jnp.exp(log_decay) * jax.nn.softplus(rates[:, H:] + decay_bias))
    decayed = states * retain[:, None, :, None]
    memory = lax.optimization_barrier(jnp.sum(decayed * keys[:, None], axis=-1))
    update = (values - memory) * strength[:, None, :]
    states = decayed + update[..., None] * keys[:, None]
    readout = lax.optimization_barrier(jnp.sum(states * queries[:, None], axis=-1))
    squares = lax.optimization_barrier(jnp.sum(readout * readout, axis=1))
    scaling = lax.rsqrt(squares / DV + 1e-06)
    gated = readout * scaling[:, None, :] * norm_gain[None, :, None] * jax.nn.silu(gating)
    gated = gated.astype(jnp.bfloat16).reshape(-1, DV * H)
    produced = jnp.dot(gated, out_weight, preferred_element_type=jnp.float32).astype(jnp.bfloat16)
    return (states, produced)

def reference(inputs, qk_weight, value_weight, output_gate_weight, rate_weight, log_decay, decay_bias, norm_gain, out_weight, states, prefilled, finished, new_owner, new_slot):
    results = []
    group_base = jnp.arange(N_DP, dtype=jnp.int32)[:, None] * ROWS_PER_RANK

    def one_block(pair):
        return advance(pair[0], pair[1], qk_weight, value_weight, output_gate_weight, rate_weight, log_decay, decay_bias, norm_gain, out_weight)
    for moment in range(STEPS):
        targets = (group_base + finished[moment]).reshape(-1).astype(jnp.int32)
        sources = (new_owner[moment] * POOL_DEV + new_slot[moment]).reshape(-1).astype(jnp.int32)
        states = states.at[targets].set(prefilled[sources])
        blocks = states.reshape(N_DP, ROWS_PER_RANK, DV, H, DK)
        block_input_rows = inputs[moment].reshape(N_DP, ROWS_PER_RANK, D)
        new_blocks, produced = lax.map(one_block, (blocks, block_input_rows))
        states = new_blocks.reshape(ROWS, DV, H, DK)
        results.append(produced.reshape(ROWS, D))
    return jnp.stack(results)
```

```python
import functools

import jax
import jax.numpy as jnp
from jax import lax
from jax.experimental import pallas as pl
from jax.experimental.pallas import tpu as pltpu
from jax.sharding import PartitionSpec as P

F32 = jnp.float32
BF16 = jnp.bfloat16
MESH = pl.DeviceIdType.MESH

STEPS = 4
REPLACED = 2
N_DP = 16
N_VALUE = 8
N_X = 4
ROWS = 32
H = 32
DK = 128
DV = 128
WIDTH = 2048
COLS = 512
PIECE = 256
BLOCKS = ROWS + N_DP
HEADS = 4
TILE = HEADS * STEPS
GROUPS = COLS // 128

FIRST, LAST, FOREIGN = 0, 1, 2
BASE = (0, 16, 32)
CHUNK = 16


def iota(shape, dim):
    return lax.broadcasted_iota(jnp.int32, shape, dim)


def dot(a, b, **kw):
    return jnp.dot(a, b, preferred_element_type=F32, **kw)


def dot_t(a, b):
    return lax.dot_general(a, b, (((1,), (1,)), ((), ())), preferred_element_type=F32)


def kernel(
    fin_ref,
    own_ref,
    slot_ref,
    logd_ref,
    bias_ref,
    gain_ref,
    x_hbm,
    wqk_hbm,
    wv_hbm,
    wg_hbm,
    wr_hbm,
    wo_hbm,
    st_hbm,
    pf_hbm,
    out_ref,
    x_v,
    wqk_v,
    wv_v,
    wg_v,
    wr_v,
    wo_v,
    st_v,
    pf_v,
    zf,
    snd_f,
    gbuf,
    msc,
    rsnd,
    rrcv,
    rf,
    val_s,
    gate_s,
    gat_s,
    sqbuf,
    r1_snd,
    r1_rcv,
    part,
    r2_snd,
    r2_rcv,
    loc,
    ag_s,
    ag_r,
    fs,
    fr,
    bs,
    br,
    qs,
    qr,
    r1s,
    r1r,
    r2s,
    r2r,
):
    me_d = lax.axis_index("dp")
    me_v = lax.axis_index("value")
    x = me_v // 2
    c = me_v % 2
    xr, xl, xo = (x + 1) % N_X, (x + 3) % N_X, (x + 2) % N_X

    def vid(xx, cc):
        return xx * 2 + cc

    right, left, partner = vid(xr, c), vid(xl, c), vid(x, 1 - c)

    def load(src, dst, k):
        cp = pltpu.make_async_copy(src, dst, loc.at[k])
        cp.start()
        return cp

    l_x = load(x_hbm, x_v, 0)
    l_qk = load(wqk_hbm, wqk_v, 1)

    barrier = pltpu.get_barrier_semaphore()
    for i in range(1, N_DP):
        pl.semaphore_signal(barrier, inc=1, device_id=((me_d + i) % N_DP, me_v), device_id_type=MESH)
    for i in range(1, N_VALUE):
        pl.semaphore_signal(barrier, inc=1, device_id=(me_d, (me_v + i) % N_VALUE), device_id_type=MESH)

    l_x.wait()
    l_qk.wait()
    l_r = load(wr_hbm, wr_v, 2)
    l_v = load(wv_hbm, wv_v, 3)
    l_g = load(wg_hbm, wg_v, 4)
    l_p = load(pf_hbm, pf_v, 5)
    l_s0 = load(st_hbm.at[pl.ds(0, 16)], st_v.at[pl.ds(0, 16)], 6)
    l_s1 = load(st_hbm.at[pl.ds(16, 16)], st_v.at[pl.ds(16, 16)], 7)
    l_o = load(wo_hbm, wo_v, 8)
    xin = x_v[...].reshape(STEPS * ROWS, WIDTH)
    joined = dot(xin, wqk_v[...]).astype(BF16)
    joined_f = joined.astype(F32)
    pick = jnp.zeros((N_DP, ROWS), F32)
    for t in range(STEPS):
        for j in range(REPLACED):
            hit = (iota((N_DP, ROWS), 0) == own_ref[t, me_d, j]) & (iota((N_DP, ROWS), 1) == fin_ref[t, me_d, j])
            pick = jnp.where(hit, 1.0, pick)
    pick = pick.astype(BF16)
    for t in range(STEPS):
        chosen = dot(pick, joined[t * ROWS : (t + 1) * ROWS])
        for h in range(HEADS):
            at = (h * STEPS + t) * BLOCKS
            zf[at : at + ROWS] = joined_f[t * ROWS : (t + 1) * ROWS, h * 128 : (h + 1) * 128]
            zf[at + ROWS : at + BLOCKS] = chosen[:, h * 128 : (h + 1) * 128]

    def block_of(r):
        return zf[pl.ds(r, TILE, stride=BLOCKS), :].astype(BF16)

    for o in range(N_DP):
        snd_f[o] = block_of(ROWS + o)
    pl.semaphore_wait(barrier, N_DP + N_VALUE - 2)

    def foreign(i):
        dst = (me_d + i) % N_DP
        return pltpu.make_async_remote_copy(
            src_ref=snd_f.at[dst],
            dst_ref=gbuf.at[me_v, ROWS + me_d],
            send_sem=fs.at[i],
            recv_sem=fr.at[i],
            device_id=(dst, me_v),
            device_id_type=MESH,
        )

    for i in range(1, N_DP):
        foreign(i).start()
    gbuf[me_v, ROWS + me_d] = snd_f[me_d]
    for r in range(CHUNK):
        gbuf[me_v, r] = block_of(r)

    def hop(chunk, k):
        slot, half, to = (
            (me_v, None, right),
            (me_v, None, left),
            (me_v, None, partner),
            (left, 0, right),
            (right, 1, left),
            (left, None, partner),
            (right, None, partner),
            (vid(xo, c), 0, partner),
            (vid(xo, c), 1, partner),
        )[k]
        return ag_copy(chunk, k, slot, half, to)

    def ag_copy(chunk, k, slot, half, to):
        rows = pl.ds(BASE[chunk], CHUNK) if half is None else pl.ds(BASE[chunk] + half * 8, 8)
        return pltpu.make_async_remote_copy(
            src_ref=gbuf.at[slot, rows],
            dst_ref=gbuf.at[slot, rows],
            send_sem=ag_s.at[chunk, k],
            recv_sem=ag_r.at[chunk, k],
            device_id=(me_d, to),
            device_id_type=MESH,
        )

    def arrived(chunk, k):
        slot, half = (
            (left, None),
            (right, None),
            (partner, None),
            (vid(xo, c), 0),
            (vid(xo, c), 1),
            (vid(xl, 1 - c), None),
            (vid(xr, 1 - c), None),
            (vid(xo, 1 - c), 0),
            (vid(xo, 1 - c), 1),
        )[k]
        ag_copy(chunk, k, slot, half, partner).wait_recv()

    def send_own(chunk):
        for k in range(3):
            hop(chunk, k).start()

    def forward_near(chunk):
        arrived(chunk, 0)
        hop(chunk, 3).start()
        hop(chunk, 5).start()
        arrived(chunk, 1)
        hop(chunk, 4).start()
        hop(chunk, 6).start()

    def forward_far(chunk):
        arrived(chunk, 3)
        hop(chunk, 7).start()
        arrived(chunk, 4)
        hop(chunk, 8).start()

    def all_here(chunk):
        for k in (2, 5, 6, 7, 8):
            arrived(chunk, k)

    send_own(FIRST)
    for r in range(CHUNK, 2 * CHUNK):
        gbuf[me_v, r] = block_of(r)
    l_r.wait()
    rates = dot(xin, wr_v[...])
    for i in range(1, N_DP):
        foreign(i).wait_recv()
    send_own(FOREIGN)
    send_own(LAST)
    l_v.wait()
    val_s[...] = dot(xin, wv_v[...])
    forward_near(FIRST)
    l_g.wait()
    gate_s[...] = dot(xin, wg_v[...])
    forward_far(FIRST)
    forward_near(FOREIGN)

    lane = iota((8, 128), 1)
    sub = iota((8, 128), 0)
    state_masks = [(lane % H) // 2 == 2 * i + sub // 4 for i in range(8)]
    gram_masks = [(lane % 64) // 4 == 2 * i + sub // 4 for i in range(8)]

    def diagonal(full, masks):
        sums = []
        for kind in range(2):
            acc = jnp.zeros((8, 128), F32)
            for i in range(8):
                at = kind * 64 + i * 8
                acc = jnp.where(masks[i], full[at : at + 8], acc)
            sums.append(acc + pltpu.roll(acc, 4, 0))
        return jnp.where(sub < 4, sums[0], sums[1])

    def contract(qk, state):
        full = dot_t(qk, state.reshape(COLS, DK).astype(BF16))
        return [diagonal(full[:, g * 128 : (g + 1) * 128], state_masks) for g in range(GROUPS)]

    def own_rows(first, count):
        def one(r, _):
            qk = gbuf[:, r].reshape(N_VALUE * TILE, DK)
            at = pl.multiple_of(r * 8, 8)
            for g, block in enumerate(contract(qk, st_v[r])):
                msc[g, pl.ds(at, 8)] = block
            msc[GROUPS, pl.ds(at, 8)] = diagonal(dot_t(qk, qk), gram_masks)
            return 0

        def two(i, _):
            one(first + 2 * i, 0)
            one(first + 2 * i + 1, 0)
            return 0

        lax.fori_loop(0, count // 2, two, 0)

    def foreign_rows():
        def one(d):
            slot = jnp.int32(0)
            for t in range(STEPS):
                for j in range(REPLACED):
                    slot = jnp.where(own_ref[t, d, j] == me_d, slot_ref[t, d, j], slot)
            qk = gbuf[:, ROWS + d].reshape(N_VALUE * TILE, DK)
            blocks = contract(qk, pf_v[slot])
            rsnd[d] = jnp.concatenate(blocks, axis=0).astype(BF16)

        def two(i, _):
            one(2 * i)
            one(2 * i + 1)
            return 0

        lax.fori_loop(0, N_DP // 2, two, 0)

    def back(i):
        dst = (me_d + i) % N_DP
        return pltpu.make_async_remote_copy(
            src_ref=rsnd.at[dst],
            dst_ref=rrcv.at[me_d],
            send_sem=bs.at[i],
            recv_sem=br.at[i],
            device_id=(dst, me_v),
            device_id_type=MESH,
        )

    all_here(FIRST)
    l_s0.wait()
    own_rows(0, CHUNK)
    forward_far(FOREIGN)
    forward_near(LAST)
    all_here(FOREIGN)
    l_p.wait()
    foreign_rows()
    for i in range(1, N_DP):
        back(i).start()
    rrcv[me_d] = rsnd[me_d]
    forward_far(LAST)
    all_here(LAST)
    l_s1.wait()
    own_rows(CHUNK, CHUNK)

    gram = [msc[GROUPS, pl.ds(k, ROWS, stride=8), :] for k in range(2 * STEPS)]
    src = iota((DK, 128), 0)
    head = (iota((DK, 128), 1) % H) // 2
    spread = [(src == 64 + head * 4 + s).astype(F32) for s in range(STEPS)]
    exact = dict(precision=lax.Precision.HIGHEST)
    by_key = dot(jnp.concatenate(gram, axis=0), jnp.concatenate(spread, axis=1), **exact)
    inv_k, inv_q = [], []
    for t in range(STEPS):
        kk = by_key[(STEPS + t) * ROWS : (STEPS + t + 1) * ROWS, t * 128 : (t + 1) * 128]
        qq = dot(gram[t], (src == head * 4 + t).astype(F32), **exact)
        inv_k.append(lax.rsqrt(kk + 1e-06))
        inv_q.append(lax.rsqrt(qq + 1e-06) * DK ** (-0.5))

    def key_key(s, t):
        return by_key[(STEPS + t) * ROWS : (STEPS + t + 1) * ROWS, s * 128 : (s + 1) * 128] * (inv_k[s] * inv_k[t])

    def key_query(s, t):
        return by_key[t * ROWS : (t + 1) * ROWS, s * 128 : (s + 1) * 128] * (inv_k[s] * inv_q[t])

    seg = iota((1, 128), 1) // H
    in_seg = iota((1, 128), 1) % H
    decay = jnp.zeros((1, 128), F32)
    bias = jnp.zeros((1, 128), F32)
    for h in range(H):
        decay = jnp.where(in_seg == h, logd_ref[h], decay)
        bias = jnp.where(in_seg == h, bias_ref[h], bias)
    wide = jnp.concatenate([rates, rates], axis=1)
    turned = pltpu.roll(wide, H, 1)
    odd = seg % 2 == 1
    strength = jax.nn.sigmoid(jnp.where(odd, turned, wide))
    retain = jnp.exp(-jnp.exp(decay) * jax.nn.softplus(jnp.where(odd, wide, turned) + bias))

    row = iota((ROWS, 128), 0)
    row_o = iota((ROWS, N_DP), 0)
    latest = jnp.full((ROWS, N_DP), -1, jnp.int32)
    owner_of = jnp.full((ROWS, 128), -1, jnp.int32)
    fresh, replaced, takes = [], [], []
    for t in range(STEPS):
        hit = jnp.zeros((ROWS, 128), jnp.bool_)
        for j in range(REPLACED):
            done, owner = fin_ref[t, me_d, j], own_ref[t, me_d, j]
            hit = hit | (row == done)
            latest = jnp.where(row_o == done, owner, latest)
            owner_of = jnp.where(row == done, owner, owner_of)
        fresh.append(hit)
        replaced.append(owner_of >= 0)
        takes.append((latest == iota((ROWS, N_DP), 1)).astype(BF16))

    for i in range(1, N_DP):
        back(i).wait_recv()
    rf[...] = rrcv[...].astype(F32).reshape(N_DP * GROUPS * 8, 128)
    returned = []
    for k in range(2 * STEPS):
        parts = [rf[pl.ds(g * 8 + k, N_DP, stride=GROUPS * 8), :] for g in range(GROUPS)]
        returned.append(dot(takes[k % STEPS], jnp.concatenate(parts, axis=1).astype(BF16)))

    readouts = [[None] * GROUPS for _ in range(STEPS)]
    squares = [None] * STEPS
    kks = {(s, t): key_key(s, t) for t in range(STEPS) for s in range(t)}
    kqs = {(s, t): key_query(s, t) for t in range(STEPS) for s in range(t + 1)}
    for g in range(GROUPS):
        lanes = slice(g * 128, (g + 1) * 128)
        written = []
        kept = None
        for t in range(STEPS):
            rows = slice(t * ROWS, (t + 1) * ROWS)
            a, b = retain[rows], strength[rows]
            kept = a if kept is None else jnp.where(fresh[t], a, kept * a)
            written = [jnp.where(fresh[t], 0.0, w * a) for w in written]

            def base(k):
                mine = msc[g, pl.ds(k, ROWS, stride=8), :]
                return jnp.where(replaced[t], returned[k][:, lanes], mine)

            memory = kept * base(STEPS + t) * inv_k[t]
            readout = kept * base(t) * inv_q[t]
            for s, w in enumerate(written):
                memory = memory + w * kks[s, t]
                readout = readout + w * kqs[s, t]
            update = (val_s[rows, lanes] - memory) * b
            readout = readout + update * kqs[t, t]
            written.append(update)
            readouts[t][g] = readout
            square = readout * readout
            squares[t] = square if g == 0 else squares[t] + square
    packed = jnp.zeros((ROWS, 128), F32)
    for t in range(STEPS):
        total = squares[t] + pltpu.roll(squares[t], 64, 1)
        total = total + pltpu.roll(total, 32, 1)
        packed = jnp.where(seg == t, total, packed)
    sqbuf[me_v] = packed.astype(BF16)

    def square_copy(i):
        return pltpu.make_async_remote_copy(
            src_ref=sqbuf.at[me_v],
            dst_ref=sqbuf.at[me_v],
            send_sem=qs.at[i],
            recv_sem=qr.at[i],
            device_id=(me_d, (me_v + i) % N_VALUE),
            device_id_type=MESH,
        )

    def square_here(i):
        origin = (me_v + N_VALUE - i) % N_VALUE
        pltpu.make_async_remote_copy(
            src_ref=sqbuf.at[origin],
            dst_ref=sqbuf.at[origin],
            send_sem=qs.at[i],
            recv_sem=qr.at[i],
            device_id=(me_d, (me_v + i) % N_VALUE),
            device_id_type=MESH,
        ).wait_recv()

    for i in range(1, N_VALUE):
        square_copy(i).start()
    for g in range(GROUPS):
        gain = jnp.zeros((1, 128), F32)
        for e in range(4):
            gain = jnp.where(seg == e, gain_ref[g * 4 + e], gain)
        for t in range(STEPS):
            gating = gate_s[t * ROWS : (t + 1) * ROWS, g * 128 : (g + 1) * 128]
            readouts[t][g] = readouts[t][g] * gain * (gating * jax.nn.sigmoid(gating))
    for i in range(1, N_VALUE):
        square_here(i)
    summed = jnp.sum(sqbuf[...].astype(F32), axis=0)
    for t in range(STEPS):
        total = jnp.where(seg == t, summed, 0.0)
        total = total + pltpu.roll(total, 64, 1)
        total = total + pltpu.roll(total, 32, 1)
        scaling = lax.rsqrt(total * (1.0 / DV) + 1e-06)
        for g in range(GROUPS):
            gat_s[t * ROWS : (t + 1) * ROWS, g * 128 : (g + 1) * 128] = (readouts[t][g] * scaling).astype(BF16)

    l_o.wait()
    gated = gat_s[...]
    order = (xo, xr, xl, x)

    def project(to):
        at = pl.multiple_of(to * PIECE, PIECE)
        return dot(gated, wo_v[:, pl.ds(at, PIECE)])

    def first_copy(k):
        return pltpu.make_async_remote_copy(
            src_ref=r1_snd.at[k],
            dst_ref=r1_rcv.at[k],
            send_sem=r1s.at[k],
            recv_sem=r1r.at[k],
            device_id=(me_d, partner),
            device_id_type=MESH,
        )

    def second_copy(k):
        return pltpu.make_async_remote_copy(
            src_ref=r2_snd.at[k],
            dst_ref=r2_rcv.at[k],
            send_sem=r2s.at[k],
            recv_sem=r2r.at[k],
            device_id=(me_d, vid(order[k], c)),
            device_id_type=MESH,
        )

    for k in range(N_X):
        r1_snd[k] = project(vid(order[k], 1 - c)).astype(BF16)
        first_copy(k).start()
    for k in range(N_X):
        part[k] = project(vid(order[k], c))
    for k in range(N_X - 1):
        first_copy(k).wait_recv()
        r2_snd[k] = (part[k] + r1_rcv[k].astype(F32)).astype(BF16)
        second_copy(k).start()
    first_copy(3).wait_recv()
    total = part[3] + r1_rcv[3].astype(F32)
    for k in (1, 2, 0):
        second_copy(k).wait_recv()
        total = total + r2_rcv[k].astype(F32)
    out_ref[...] = total.astype(BF16)

    for i in range(1, N_DP):
        foreign(i).wait_send()
        back(i).wait_send()
    for chunk in range(3):
        for k in range(9):
            hop(chunk, k).wait_send()
    for i in range(1, N_VALUE):
        square_copy(i).wait_send()
    for k in range(N_X):
        first_copy(k).wait_send()
    for k in range(N_X - 1):
        second_copy(k).wait_send()


def on_device(
    inputs,
    qk_weight,
    value_weight,
    output_gate_weight,
    rate_weight,
    log_decay,
    decay_bias,
    norm_gain,
    out_weight,
    states,
    prefilled,
    finished,
    new_owner,
    new_slot,
):
    smem = pl.BlockSpec(memory_space=pltpu.SMEM)
    hbm = pl.BlockSpec(memory_space=pl.ANY)
    dma = pltpu.SemaphoreType.DMA
    produced = pl.pallas_call(
        kernel,
        out_shape=jax.ShapeDtypeStruct((STEPS * ROWS, PIECE), BF16),
        in_specs=[smem] * 6 + [hbm] * 8,
        out_specs=pl.BlockSpec(memory_space=pltpu.VMEM),
        scratch_shapes=[
            pltpu.VMEM((STEPS, ROWS, WIDTH), BF16),
            pltpu.VMEM((WIDTH, COLS), BF16),
            pltpu.VMEM((WIDTH, COLS), BF16),
            pltpu.VMEM((WIDTH, COLS), BF16),
            pltpu.VMEM((WIDTH, 2 * H), BF16),
            pltpu.VMEM((COLS, WIDTH), BF16),
            pltpu.VMEM((ROWS, 16, H, DK), F32),
            pltpu.VMEM((16, 16, H, DK), F32),
            pltpu.VMEM((TILE * BLOCKS, DK), F32),
            pltpu.VMEM((N_DP, TILE, DK), BF16),
            pltpu.VMEM((N_VALUE, BLOCKS, TILE, DK), BF16),
            pltpu.VMEM((GROUPS + 1, ROWS * 8, 128), F32),
            pltpu.VMEM((N_DP, GROUPS * 8, 128), BF16),
            pltpu.VMEM((N_DP, GROUPS * 8, 128), BF16),
            pltpu.VMEM((N_DP * GROUPS * 8, 128), F32),
            pltpu.VMEM((STEPS * ROWS, COLS), F32),
            pltpu.VMEM((STEPS * ROWS, COLS), F32),
            pltpu.VMEM((STEPS * ROWS, COLS), BF16),
            pltpu.VMEM((N_VALUE, ROWS, 128), BF16),
            pltpu.VMEM((N_X, STEPS * ROWS, PIECE), BF16),
            pltpu.VMEM((N_X, STEPS * ROWS, PIECE), BF16),
            pltpu.VMEM((N_X, STEPS * ROWS, PIECE), F32),
            pltpu.VMEM((N_X - 1, STEPS * ROWS, PIECE), BF16),
            pltpu.VMEM((N_X - 1, STEPS * ROWS, PIECE), BF16),
            dma((9,)),
            dma((3, 9)),
            dma((3, 9)),
            dma((N_DP,)),
            dma((N_DP,)),
            dma((N_DP,)),
            dma((N_DP,)),
            dma((N_VALUE,)),
            dma((N_VALUE,)),
            dma((N_X,)),
            dma((N_X,)),
            dma((N_X - 1,)),
            dma((N_X - 1,)),
        ],
        compiler_params=pltpu.CompilerParams(
            collective_id=0, has_side_effects=True, vmem_limit_bytes=56 * 2**20
        ),
        name="delta_steps",
    )(
        finished,
        new_owner,
        new_slot,
        log_decay,
        decay_bias,
        norm_gain,
        inputs,
        qk_weight,
        value_weight,
        output_gate_weight,
        rate_weight,
        out_weight,
        states,
        prefilled,
    )
    return produced.reshape(STEPS, ROWS, PIECE)


def solution(mesh):
    return jax.shard_map(
        on_device,
        mesh=mesh,
        in_specs=(
            P(None, "dp", None),
            P(None, "value"),
            P(None, "value"),
            P(None, "value"),
            P(),
            P(),
            P(),
            P("value"),
            P("value", None),
            P("dp", "value", None, None),
            P("dp", "value", None, None),
            P(),
            P(),
            P(),
        ),
        out_specs=P(None, "dp", "value"),
        check_vma=False,
    )
```

```python
import functools

import jax
import jax.numpy as jnp
from jax import lax
from jax.experimental import pallas as pl
from jax.experimental.pallas import tpu as pltpu
from jax.sharding import PartitionSpec as P

F32 = jnp.float32
BF16 = jnp.bfloat16
MESH = pl.DeviceIdType.MESH

STEPS = 4
REPLACED = 2
N_DP = 16
N_VALUE = 8
N_X = 4
ROWS = 32
H = 32
DK = 128
DV = 128
WIDTH = 2048
COLS = 512
PIECE = 256
BLOCKS = ROWS + N_DP
HEADS = 4
TILE = HEADS * STEPS
GROUPS = COLS // 128

FIRST, LAST = 0, 1
BASE = (0, 16)
CHUNK = 16


def iota(shape, dim):
    return lax.broadcasted_iota(jnp.int32, shape, dim)


def dot(a, b, **kw):
    return jnp.dot(a, b, preferred_element_type=F32, **kw)


def dot_t(a, b):
    return lax.dot_general(a, b, (((1,), (1,)), ((), ())), preferred_element_type=F32)


def kernel(
    fin_hbm,
    own_hbm,
    slot_hbm,
    logd_hbm,
    bias_hbm,
    gain_hbm,
    x_hbm,
    wqk_hbm,
    wv_hbm,
    wg_hbm,
    wr_hbm,
    wo_hbm,
    st_hbm,
    pf_hbm,
    out_ref,
    fin_ref,
    own_ref,
    slot_ref,
    logd_ref,
    bias_ref,
    gain_ref,
    x_v,
    wqk_v,
    wv_v,
    wg_v,
    wr_v,
    wo_v,
    st_v,
    pf_v,
    zf,
    snd_f,
    gbuf,
    msc,
    rsnd,
    rrcv,
    rf,
    val_s,
    gate_s,
    gat_s,
    sqbuf,
    r1_snd,
    r1_rcv,
    part,
    r2_snd,
    r2_rcv,
    loc,
    ag_s,
    ag_r,
    fs,
    fr,
    fps,
    fpr,
    bs,
    br,
    qs,
    qr,
    r1s,
    r1r,
    r2s,
    r2r,
):
    me_d = lax.axis_index("dp")
    me_v = lax.axis_index("value")
    x = me_v // 2
    c = me_v % 2
    xr, xl, xo = (x + 1) % N_X, (x + 3) % N_X, (x + 2) % N_X

    def vid(xx, cc):
        return xx * 2 + cc

    right, left, partner = vid(xr, c), vid(xl, c), vid(x, 1 - c)

    def load(src, dst, k):
        cp = pltpu.make_async_copy(src, dst, loc.at[k])
        cp.start()
        return cp

    l_x = load(x_hbm, x_v, 0)
    l_qk = load(wqk_hbm, wqk_v, 1)
    scalars = (
        (fin_hbm, fin_ref),
        (own_hbm, own_ref),
        (slot_hbm, slot_ref),
        (logd_hbm, logd_ref),
        (bias_hbm, bias_ref),
        (gain_hbm, gain_ref),
    )
    l_scalars = [load(src, dst, 9 + k) for k, (src, dst) in enumerate(scalars)]
    l_p = load(pf_hbm, pf_v, 5)
    l_s = load(st_hbm, st_v, 6)
    l_r = load(wr_hbm, wr_v, 2)
    l_v = load(wv_hbm, wv_v, 3)
    l_g = load(wg_hbm, wg_v, 4)
    l_o = load(wo_hbm, wo_v, 8)

    barrier = pltpu.get_barrier_semaphore()
    greeted = 0
    for i in range(N_DP):
        for j in range(N_X):
            if i or j:
                to = ((me_d + i) % N_DP, vid((x + j) % N_X, c))
                pl.semaphore_signal(barrier, inc=1, device_id=to, device_id_type=MESH)
                greeted += 1
    for j in range(N_X):
        to = (me_d, vid((x + j) % N_X, 1 - c))
        pl.semaphore_signal(barrier, inc=1, device_id=to, device_id_type=MESH)
        greeted += 1

    l_x.wait()
    l_qk.wait()
    xin = x_v[...].reshape(STEPS * ROWS, WIDTH)
    joined = dot(xin, wqk_v[...]).astype(BF16)
    joined_f = joined.astype(F32)
    for copy in l_scalars:
        copy.wait()
    pick = jnp.zeros((N_DP, ROWS), F32)
    for t in range(STEPS):
        for j in range(REPLACED):
            hit = (iota((N_DP, ROWS), 0) == own_ref[t, j, me_d]) & (iota((N_DP, ROWS), 1) == fin_ref[t, j, me_d])
            pick = jnp.where(hit, 1.0, pick)
    pick = pick.astype(BF16)
    for t in range(STEPS):
        chosen = dot(pick, joined[t * ROWS : (t + 1) * ROWS])
        for h in range(HEADS):
            at = (h * STEPS + t) * BLOCKS
            zf[at : at + ROWS] = joined_f[t * ROWS : (t + 1) * ROWS, h * 128 : (h + 1) * 128]
            zf[at + ROWS : at + BLOCKS] = chosen[:, h * 128 : (h + 1) * 128]

    def block_of(r):
        return zf[pl.ds(r, TILE, stride=BLOCKS), :].astype(BF16)

    for o in range(N_DP):
        snd_f[o] = block_of(ROWS + o)
    pl.semaphore_wait(barrier, greeted)

    def foreign(i, j):
        dst = (me_d + i) % N_DP
        return pltpu.make_async_remote_copy(
            src_ref=snd_f.at[dst],
            dst_ref=gbuf.at[me_v, ROWS + me_d],
            send_sem=fs.at[j],
            recv_sem=fr.at[j],
            device_id=(dst, vid((x + j) % N_X, c)),
            device_id_type=MESH,
        )

    def foreign_all(j):
        slot = vid((x + N_X - j) % N_X, c)
        first = 1 if j == 0 else 0
        rows = pl.ds(ROWS, N_DP - first)
        return pltpu.make_async_remote_copy(
            src_ref=gbuf.at[slot, rows],
            dst_ref=gbuf.at[slot, rows],
            send_sem=fs.at[j],
            recv_sem=fr.at[j],
            device_id=(me_d, partner),
            device_id_type=MESH,
        )

    def foreign_forward(j):
        slot = vid((x + N_X - j) % N_X, c)
        rows = pl.ds(ROWS, N_DP)
        return pltpu.make_async_remote_copy(
            src_ref=gbuf.at[slot, rows],
            dst_ref=gbuf.at[slot, rows],
            send_sem=fps.at[j],
            recv_sem=fpr.at[j],
            device_id=(me_d, partner),
            device_id_type=MESH,
        )

    def foreign_forwarded(j):
        slot = vid((x + N_X - j) % N_X, 1 - c)
        rows = pl.ds(ROWS, N_DP)
        pltpu.make_async_remote_copy(
            src_ref=gbuf.at[slot, rows],
            dst_ref=gbuf.at[slot, rows],
            send_sem=fps.at[j],
            recv_sem=fpr.at[j],
            device_id=(me_d, partner),
            device_id_type=MESH,
        ).wait_recv()

    for j in (2, 1, 3, 0):
        for i in range(1 if j == 0 else 0, N_DP):
            foreign(i, j).start()
    gbuf[me_v, ROWS + me_d] = snd_f[me_d]
    for r in range(CHUNK):
        gbuf[me_v, r] = block_of(r)

    def hop(chunk, k):
        slot, half, to = (
            (me_v, None, right),
            (me_v, None, left),
            (me_v, None, partner),
            (left, 0, right),
            (right, 1, left),
            (left, None, partner),
            (right, None, partner),
            (vid(xo, c), 0, partner),
            (vid(xo, c), 1, partner),
        )[k]
        return ag_copy(chunk, k, slot, half, to)

    def ag_copy(chunk, k, slot, half, to):
        rows = pl.ds(BASE[chunk], CHUNK) if half is None else pl.ds(BASE[chunk] + half * 8, 8)
        return pltpu.make_async_remote_copy(
            src_ref=gbuf.at[slot, rows],
            dst_ref=gbuf.at[slot, rows],
            send_sem=ag_s.at[chunk, k],
            recv_sem=ag_r.at[chunk, k],
            device_id=(me_d, to),
            device_id_type=MESH,
        )

    def arrived(chunk, k):
        slot, half = (
            (left, None),
            (right, None),
            (partner, None),
            (vid(xo, c), 0),
            (vid(xo, c), 1),
            (vid(xl, 1 - c), None),
            (vid(xr, 1 - c), None),
            (vid(xo, 1 - c), 0),
            (vid(xo, 1 - c), 1),
        )[k]
        ag_copy(chunk, k, slot, half, partner).wait_recv()

    def send_own(chunk):
        for k in range(3):
            hop(chunk, k).start()

    def forward_near(chunk):
        arrived(chunk, 0)
        hop(chunk, 3).start()
        hop(chunk, 5).start()
        arrived(chunk, 1)
        hop(chunk, 4).start()
        hop(chunk, 6).start()

    def forward_far(chunk):
        arrived(chunk, 3)
        hop(chunk, 7).start()
        arrived(chunk, 4)
        hop(chunk, 8).start()

    def all_here(chunk):
        for k in (2, 5, 6, 7, 8):
            arrived(chunk, k)

    send_own(FIRST)
    for r in range(CHUNK, 2 * CHUNK):
        gbuf[me_v, r] = block_of(r)
    send_own(LAST)
    l_r.wait()
    rates = dot_t(xin, wr_v[...])
    l_v.wait()
    val_s[...] = dot(xin, wv_v[...])
    forward_near(FIRST)
    l_g.wait()
    gate_s[...] = dot(xin, wg_v[...])
    forward_near(LAST)
    forward_far(FIRST)
    for j in (0, 1, 3, 2):
        foreign_all(j).wait_recv()
        foreign_forward(j).start()
    forward_far(LAST)

    lane = iota((8, 128), 1)
    sub = iota((8, 128), 0)
    state_masks = [(lane % H) // 2 == 2 * i + sub // 4 for i in range(8)]
    gram_masks = [(lane % 64) // 4 == 2 * i + sub // 4 for i in range(8)]

    def diagonal(full, masks):
        sums = []
        for kind in range(2):
            acc = jnp.zeros((8, 128), F32)
            for i in range(8):
                at = kind * 64 + i * 8
                acc = jnp.where(masks[i], full[at : at + 8], acc)
            sums.append(acc + pltpu.roll(acc, 4, 0))
        return jnp.where(sub < 4, sums[0], sums[1])

    def contract(qk, state):
        full = dot_t(qk, state.reshape(COLS, DK).astype(BF16))
        return [diagonal(full[:, g * 128 : (g + 1) * 128], state_masks) for g in range(GROUPS)]

    def own_rows(first, count):
        def one(r, _):
            qk = gbuf[:, r].reshape(N_VALUE * TILE, DK)
            at = pl.multiple_of(r * 8, 8)
            for g, block in enumerate(contract(qk, st_v[r])):
                msc[g, pl.ds(at, 8)] = block
            msc[GROUPS, pl.ds(at, 8)] = diagonal(dot_t(qk, qk), gram_masks)
            return 0

        def two(i, _):
            one(first + 2 * i, 0)
            one(first + 2 * i + 1, 0)
            return 0

        lax.fori_loop(0, count // 2, two, 0)

    def foreign_rows():
        def one(d):
            slot = jnp.int32(0)
            for t in range(STEPS):
                for j in range(REPLACED):
                    slot = jnp.where(own_ref[t, j, d] == me_d, slot_ref[t, j, d], slot)
            qk = gbuf[:, ROWS + d].reshape(N_VALUE * TILE, DK)
            blocks = contract(qk, pf_v[slot])
            rsnd[d] = jnp.concatenate(blocks, axis=0).astype(BF16)

        def two(i, _):
            one(2 * i)
            one(2 * i + 1)
            return 0

        lax.fori_loop(0, N_DP // 2, two, 0)

    def back(i):
        dst = (me_d + i) % N_DP
        return pltpu.make_async_remote_copy(
            src_ref=rsnd.at[dst],
            dst_ref=rrcv.at[me_d],
            send_sem=bs.at[i],
            recv_sem=br.at[i],
            device_id=(dst, me_v),
            device_id_type=MESH,
        )

    l_p.wait()
    for j in (0, 1, 3, 2):
        foreign_forwarded(j)
    foreign_rows()
    for i in range(1, N_DP):
        back(i).start()
    rrcv[me_d] = rsnd[me_d]
    l_s.wait()
    all_here(FIRST)
    own_rows(0, CHUNK)
    all_here(LAST)
    own_rows(CHUNK, CHUNK)

    gram = [msc[GROUPS, pl.ds(k, ROWS, stride=8), :] for k in range(2 * STEPS)]
    src = iota((DK, 128), 0)
    head = (iota((DK, 128), 1) % H) // 2
    spread = [(src == 64 + head * 4 + s).astype(F32) for s in range(STEPS)]
    exact = dict(precision=lax.Precision.HIGHEST)
    by_key = dot(jnp.concatenate(gram, axis=0), jnp.concatenate(spread, axis=1), **exact)
    inv_k, inv_q = [], []
    for t in range(STEPS):
        kk = by_key[(STEPS + t) * ROWS : (STEPS + t + 1) * ROWS, t * 128 : (t + 1) * 128]
        qq = dot(gram[t], (src == head * 4 + t).astype(F32), **exact)
        inv_k.append(lax.rsqrt(kk + 1e-06))
        inv_q.append(lax.rsqrt(qq + 1e-06) * DK ** (-0.5))

    def key_key(s, t):
        return by_key[(STEPS + t) * ROWS : (STEPS + t + 1) * ROWS, s * 128 : (s + 1) * 128] * (inv_k[s] * inv_k[t])

    def key_query(s, t):
        return by_key[t * ROWS : (t + 1) * ROWS, s * 128 : (s + 1) * 128] * (inv_k[s] * inv_q[t])

    seg = iota((1, 128), 1) // H
    in_seg = iota((1, 128), 1) % H
    decay = jnp.zeros((1, 128), F32)
    bias = jnp.zeros((1, 128), F32)
    for h in range(H):
        decay = jnp.where(in_seg == h, logd_ref[h], decay)
        bias = jnp.where(in_seg == h, bias_ref[h], bias)
    wide = jnp.concatenate([rates, rates], axis=1)
    turned = pltpu.roll(wide, H, 1)
    odd = seg % 2 == 1
    strength = jax.nn.sigmoid(jnp.where(odd, turned, wide))
    retain = jnp.exp(-jnp.exp(decay) * jax.nn.softplus(jnp.where(odd, wide, turned) + bias))

    row = iota((ROWS, 128), 0)
    row_o = iota((ROWS, N_DP), 0)
    latest = jnp.full((ROWS, N_DP), -1, jnp.int32)
    owner_of = jnp.full((ROWS, 128), -1, jnp.int32)
    fresh, replaced, takes = [], [], []
    for t in range(STEPS):
        hit = jnp.zeros((ROWS, 128), jnp.bool_)
        for j in range(REPLACED):
            done, owner = fin_ref[t, j, me_d], own_ref[t, j, me_d]
            hit = hit | (row == done)
            latest = jnp.where(row_o == done, owner, latest)
            owner_of = jnp.where(row == done, owner, owner_of)
        fresh.append(hit)
        replaced.append(owner_of >= 0)
        takes.append((latest == iota((ROWS, N_DP), 1)).astype(BF16))

    for i in range(1, N_DP):
        back(i).wait_recv()
    rf[...] = rrcv[...].astype(F32).reshape(N_DP * GROUPS * 8, 128)
    returned = []
    for k in range(2 * STEPS):
        parts = [rf[pl.ds(g * 8 + k, N_DP, stride=GROUPS * 8), :] for g in range(GROUPS)]
        returned.append(dot(takes[k % STEPS], jnp.concatenate(parts, axis=1).astype(BF16)))

    readouts = [[None] * GROUPS for _ in range(STEPS)]
    squares = [None] * STEPS
    kks = {(s, t): key_key(s, t) for t in range(STEPS) for s in range(t)}
    kqs = {(s, t): key_query(s, t) for t in range(STEPS) for s in range(t + 1)}
    for g in range(GROUPS):
        lanes = slice(g * 128, (g + 1) * 128)
        written = []
        kept = None
        for t in range(STEPS):
            rows = slice(t * ROWS, (t + 1) * ROWS)
            a, b = retain[rows], strength[rows]
            kept = a if kept is None else jnp.where(fresh[t], a, kept * a)
            written = [jnp.where(fresh[t], 0.0, w * a) for w in written]

            def base(k):
                mine = msc[g, pl.ds(k, ROWS, stride=8), :]
                return jnp.where(replaced[t], returned[k][:, lanes], mine)

            memory = kept * base(STEPS + t) * inv_k[t]
            readout = kept * base(t) * inv_q[t]
            for s, w in enumerate(written):
                memory = memory + w * kks[s, t]
                readout = readout + w * kqs[s, t]
            update = (val_s[rows, lanes] - memory) * b
            readout = readout + update * kqs[t, t]
            written.append(update)
            readouts[t][g] = readout
            square = readout * readout
            squares[t] = square if g == 0 else squares[t] + square
    packed = jnp.zeros((ROWS, 128), F32)
    for t in range(STEPS):
        total = squares[t] + pltpu.roll(squares[t], 64, 1)
        total = total + pltpu.roll(total, 32, 1)
        packed = jnp.where(seg == t, total, packed)
    sqbuf[me_v] = packed.astype(BF16)

    def square_copy(i):
        return pltpu.make_async_remote_copy(
            src_ref=sqbuf.at[me_v],
            dst_ref=sqbuf.at[me_v],
            send_sem=qs.at[i],
            recv_sem=qr.at[i],
            device_id=(me_d, (me_v + i) % N_VALUE),
            device_id_type=MESH,
        )

    def square_here(i):
        origin = (me_v + N_VALUE - i) % N_VALUE
        pltpu.make_async_remote_copy(
            src_ref=sqbuf.at[origin],
            dst_ref=sqbuf.at[origin],
            send_sem=qs.at[i],
            recv_sem=qr.at[i],
            device_id=(me_d, (me_v + i) % N_VALUE),
            device_id_type=MESH,
        ).wait_recv()

    for i in range(1, N_VALUE):
        square_copy(i).start()
    for g in range(GROUPS):
        gain = jnp.zeros((1, 128), F32)
        for e in range(4):
            gain = jnp.where(seg == e, gain_ref[g * 4 + e], gain)
        for t in range(STEPS):
            gating = gate_s[t * ROWS : (t + 1) * ROWS, g * 128 : (g + 1) * 128]
            readouts[t][g] = readouts[t][g] * gain * (gating * jax.nn.sigmoid(gating))
    for i in range(1, N_VALUE):
        square_here(i)
    summed = jnp.sum(sqbuf[...].astype(F32), axis=0)
    for t in range(STEPS):
        total = jnp.where(seg == t, summed, 0.0)
        total = total + pltpu.roll(total, 64, 1)
        total = total + pltpu.roll(total, 32, 1)
        scaling = lax.rsqrt(total * (1.0 / DV) + 1e-06)
        for g in range(GROUPS):
            gat_s[t * ROWS : (t + 1) * ROWS, g * 128 : (g + 1) * 128] = (readouts[t][g] * scaling).astype(BF16)

    l_o.wait()
    gated = gat_s[...]
    order = (xo, xr, xl, x)

    def project(to):
        at = pl.multiple_of(to * PIECE, PIECE)
        return dot(gated, wo_v[:, pl.ds(at, PIECE)])

    def first_copy(k):
        return pltpu.make_async_remote_copy(
            src_ref=r1_snd.at[k],
            dst_ref=r1_rcv.at[k],
            send_sem=r1s.at[k],
            recv_sem=r1r.at[k],
            device_id=(me_d, partner),
            device_id_type=MESH,
        )

    def second_copy(k):
        return pltpu.make_async_remote_copy(
            src_ref=r2_snd.at[k],
            dst_ref=r2_rcv.at[k],
            send_sem=r2s.at[k],
            recv_sem=r2r.at[k],
            device_id=(me_d, vid(order[k], c)),
            device_id_type=MESH,
        )

    for k in range(N_X):
        r1_snd[k] = project(vid(order[k], 1 - c)).astype(BF16)
        first_copy(k).start()
    for k in range(N_X):
        part[k] = project(vid(order[k], c))
    for k in range(N_X - 1):
        first_copy(k).wait_recv()
        r2_snd[k] = (part[k] + r1_rcv[k].astype(F32)).astype(BF16)
        second_copy(k).start()
    first_copy(3).wait_recv()
    total = part[3] + r1_rcv[3].astype(F32)
    for k in (1, 2, 0):
        second_copy(k).wait_recv()
        total = total + r2_rcv[k].astype(F32)
    out_ref[...] = total.astype(BF16)

    for j in range(N_X):
        foreign_all(j).wait_send()
        foreign_forward(j).wait_send()
    for i in range(1, N_DP):
        back(i).wait_send()
    for chunk in range(2):
        for k in range(9):
            hop(chunk, k).wait_send()
    for i in range(1, N_VALUE):
        square_copy(i).wait_send()
    for k in range(N_X):
        first_copy(k).wait_send()
    for k in range(N_X - 1):
        second_copy(k).wait_send()


def on_device(
    inputs,
    qk_weight,
    value_weight,
    output_gate_weight,
    rate_weight,
    log_decay,
    decay_bias,
    norm_gain,
    out_weight,
    states,
    prefilled,
    finished,
    new_owner,
    new_slot,
):
    hbm = pl.BlockSpec(memory_space=pl.ANY)
    dma = pltpu.SemaphoreType.DMA
    produced = pl.pallas_call(
        kernel,
        out_shape=jax.ShapeDtypeStruct((STEPS * ROWS, PIECE), BF16),
        in_specs=[hbm] * 14,
        out_specs=pl.BlockSpec(memory_space=pltpu.VMEM),
        scratch_shapes=[
            pltpu.SMEM((STEPS, REPLACED, N_DP), jnp.int32),
            pltpu.SMEM((STEPS, REPLACED, N_DP), jnp.int32),
            pltpu.SMEM((STEPS, REPLACED, N_DP), jnp.int32),
            pltpu.SMEM((H,), F32),
            pltpu.SMEM((H,), F32),
            pltpu.SMEM((DV // N_VALUE,), F32),
            pltpu.VMEM((STEPS, ROWS, WIDTH), BF16),
            pltpu.VMEM((WIDTH, COLS), BF16),
            pltpu.VMEM((WIDTH, COLS), BF16),
            pltpu.VMEM((WIDTH, COLS), BF16),
            pltpu.VMEM((2 * H, WIDTH), BF16),
            pltpu.VMEM((COLS, WIDTH), BF16),
            pltpu.VMEM((ROWS, 16, H, DK), F32),
            pltpu.VMEM((16, 16, H, DK), F32),
            pltpu.VMEM((TILE * BLOCKS, DK), F32),
            pltpu.VMEM((N_DP, TILE, DK), BF16),
            pltpu.VMEM((N_VALUE, BLOCKS, TILE, DK), BF16),
            pltpu.VMEM((GROUPS + 1, ROWS * 8, 128), F32),
            pltpu.VMEM((N_DP, GROUPS * 8, 128), BF16),
            pltpu.VMEM((N_DP, GROUPS * 8, 128), BF16),
            pltpu.VMEM((N_DP * GROUPS * 8, 128), F32),
            pltpu.VMEM((STEPS * ROWS, COLS), F32),
            pltpu.VMEM((STEPS * ROWS, COLS), F32),
            pltpu.VMEM((STEPS * ROWS, COLS), BF16),
            pltpu.VMEM((N_VALUE, ROWS, 128), BF16),
            pltpu.VMEM((N_X, STEPS * ROWS, PIECE), BF16),
            pltpu.VMEM((N_X, STEPS * ROWS, PIECE), BF16),
            pltpu.VMEM((N_X, STEPS * ROWS, PIECE), F32),
            pltpu.VMEM((N_X - 1, STEPS * ROWS, PIECE), BF16),
            pltpu.VMEM((N_X - 1, STEPS * ROWS, PIECE), BF16),
            dma((15,)),
            dma((2, 9)),
            dma((2, 9)),
            dma((N_X,)),
            dma((N_X,)),
            dma((N_X,)),
            dma((N_X,)),
            dma((N_DP,)),
            dma((N_DP,)),
            dma((N_VALUE,)),
            dma((N_VALUE,)),
            dma((N_X,)),
            dma((N_X,)),
            dma((N_X - 1,)),
            dma((N_X - 1,)),
        ],
        compiler_params=pltpu.CompilerParams(
            collective_id=0, has_side_effects=True, vmem_limit_bytes=56 * 2**20
        ),
        name="delta_steps",
    )(
        finished.transpose(0, 2, 1),
        new_owner.transpose(0, 2, 1),
        new_slot.transpose(0, 2, 1),
        log_decay,
        decay_bias,
        norm_gain,
        inputs,
        qk_weight,
        value_weight,
        output_gate_weight,
        rate_weight.T,
        out_weight,
        states,
        prefilled,
    )
    return produced.reshape(STEPS, ROWS, PIECE)


def solution(mesh):
    return jax.shard_map(
        on_device,
        mesh=mesh,
        in_specs=(
            P(None, "dp", None),
            P(None, "value"),
            P(None, "value"),
            P(None, "value"),
            P(),
            P(),
            P(),
            P("value"),
            P("value", None),
            P("dp", "value", None, None),
            P("dp", "value", None, None),
            P(),
            P(),
            P(),
        ),
        out_specs=P(None, "dp", "value"),
        check_vma=False,
    )
```

```python
import functools

import jax
import jax.numpy as jnp
from jax import lax
from jax.experimental import pallas as pl
from jax.experimental.pallas import tpu as pltpu
from jax.sharding import PartitionSpec as P

F32 = jnp.float32
BF16 = jnp.bfloat16
MESH = pl.DeviceIdType.MESH

STEPS = 4
REPLACED = 2
N_DP = 16
N_VALUE = 8
N_X = 4
ROWS = 32
H = 32
DK = 128
DV = 128
WIDTH = 2048
COLS = 512
PIECE = 256
BLOCKS = ROWS + N_DP
HEADS = 4
TILE = HEADS * STEPS
GROUPS = COLS // 128
ALL = STEPS * ROWS

PAIRS = [(s, t) for t in range(STEPS) for s in range(t + 1)]
VALUES, GATING = 0, GROUPS * ALL
RETAIN = 2 * GROUPS * ALL
STRENGTH, INV_K, INV_Q = RETAIN + ALL, RETAIN + 2 * ALL, RETAIN + 3 * ALL
KEY_KEY = RETAIN + 4 * ALL
KEY_QUERY = KEY_KEY + len(PAIRS) * ROWS
QUANTITIES = KEY_QUERY // ROWS + len(PAIRS)

FIRST, LAST = 0, 1
BASE = (0, 16)
CHUNK = 16


def ring(k):
    return min(k, N_X - k)


PLANE = sorted(((a, b) for a in range(N_X) for b in range(N_X)), key=lambda o: -ring(o[0]) - ring(o[1]))
SPACE = sorted(((i, j) for i in range(N_DP) for j in range(N_X)), key=lambda o: -sum(map(ring, (*PLANE[o[0]], o[1]))))


def iota(shape, dim):
    return lax.broadcasted_iota(jnp.int32, shape, dim)


def dot(a, b, **kw):
    return jnp.dot(a, b, preferred_element_type=F32, **kw)


def dot_t(a, b):
    return lax.dot_general(a, b, (((1,), (1,)), ((), ())), preferred_element_type=F32)


def kernel(
    fin_hbm,
    own_hbm,
    slot_hbm,
    logd_hbm,
    bias_hbm,
    gain_hbm,
    x_hbm,
    wqk_hbm,
    wv_hbm,
    wg_hbm,
    wr_hbm,
    wo_hbm,
    st_hbm,
    pf_hbm,
    out_ref,
    fin_ref,
    own_ref,
    slot_ref,
    logd_ref,
    bias_ref,
    gain_ref,
    x_v,
    wqk_v,
    wv_v,
    wg_v,
    wr_v,
    wo_v,
    st_v,
    pf_v,
    zf,
    snd_f,
    gbuf,
    msc,
    rsnd,
    rrcv,
    rf,
    rowq,
    slotq,
    gat_s,
    sqbuf,
    ssqbuf,
    r1_snd,
    r1_rcv,
    part,
    r2_snd,
    r2_rcv,
    s_snd,
    s_rcv,
    loc,
    ag_s,
    ag_r,
    fs,
    fr,
    fps,
    fpr,
    bs,
    br,
    qs,
    qr,
    r1s,
    r1r,
    r2s,
    r2r,
    sqs,
    sqr,
    ss,
    sr,
):
    me_d = lax.axis_index("dp")
    me_v = lax.axis_index("value")
    x = me_v // 2
    c = me_v % 2
    xr, xl, xo = (x + 1) % N_X, (x + 3) % N_X, (x + 2) % N_X

    def vid(xx, cc):
        return xx * 2 + cc

    right, left, partner = vid(xr, c), vid(xl, c), vid(x, 1 - c)

    def peer(i):
        dz, dy = PLANE[i]
        return ((me_d // N_X + dz) % N_X) * N_X + (me_d % N_X + dy) % N_X

    barrier = pltpu.get_barrier_semaphore()
    greeted = 0
    for i, j in SPACE:
        if PLANE[i] != (0, 0) or j:
            to = (peer(i), vid((x + j) % N_X, c))
            pl.semaphore_signal(barrier, inc=1, device_id=to, device_id_type=MESH)
            greeted += 1
    for j in range(N_X):
        to = (me_d, vid((x + j) % N_X, 1 - c))
        pl.semaphore_signal(barrier, inc=1, device_id=to, device_id_type=MESH)
        greeted += 1

    def load(src, dst, k):
        cp = pltpu.make_async_copy(src, dst, loc.at[k])
        cp.start()
        return cp

    l_x = load(x_hbm, x_v, 0)
    l_qk = load(wqk_hbm, wqk_v, 1)
    scalars = (
        (fin_hbm, fin_ref),
        (own_hbm, own_ref),
        (slot_hbm, slot_ref),
        (logd_hbm, logd_ref),
        (bias_hbm, bias_ref),
        (gain_hbm, gain_ref),
    )
    l_scalars = [load(src, dst, 9 + k) for k, (src, dst) in enumerate(scalars)]
    l_r = load(wr_hbm, wr_v, 2)
    l_v = load(wv_hbm, wv_v, 3)
    l_g = load(wg_hbm, wg_v, 4)
    l_p = load(pf_hbm, pf_v, 5)
    l_s = load(st_hbm, st_v, 6)
    l_o = load(wo_hbm, wo_v, 8)

    l_x.wait()
    l_qk.wait()
    xin = x_v[...].reshape(STEPS * ROWS, WIDTH)
    joined = dot(xin, wqk_v[...]).astype(BF16)
    joined_f = joined.astype(F32)
    for copy in l_scalars:
        copy.wait()
    pick = jnp.zeros((N_DP, ROWS), F32)
    for t in range(STEPS):
        for j in range(REPLACED):
            hit = (iota((N_DP, ROWS), 0) == own_ref[t, j, me_d]) & (iota((N_DP, ROWS), 1) == fin_ref[t, j, me_d])
            pick = jnp.where(hit, 1.0, pick)
    pick = pick.astype(BF16)
    for t in range(STEPS):
        chosen = dot(pick, joined[t * ROWS : (t + 1) * ROWS])
        for h in range(HEADS):
            at = (h * STEPS + t) * BLOCKS
            zf[at : at + ROWS] = joined_f[t * ROWS : (t + 1) * ROWS, h * 128 : (h + 1) * 128]
            zf[at + ROWS : at + BLOCKS] = chosen[:, h * 128 : (h + 1) * 128]

    def block_of(r):
        return zf[pl.ds(r, TILE, stride=BLOCKS), :].astype(BF16)

    for o in range(N_DP):
        snd_f[o] = block_of(ROWS + o)
    pl.semaphore_wait(barrier, greeted)

    def foreign(i, j):
        dst = peer(i)
        return pltpu.make_async_remote_copy(
            src_ref=snd_f.at[dst],
            dst_ref=gbuf.at[me_v, ROWS + me_d],
            send_sem=fs.at[j],
            recv_sem=fr.at[j],
            device_id=(dst, vid((x + j) % N_X, c)),
            device_id_type=MESH,
        )

    def foreign_all(j):
        slot = vid((x + N_X - j) % N_X, c)
        first = 1 if j == 0 else 0
        rows = pl.ds(ROWS, N_DP - first)
        return pltpu.make_async_remote_copy(
            src_ref=gbuf.at[slot, rows],
            dst_ref=gbuf.at[slot, rows],
            send_sem=fs.at[j],
            recv_sem=fr.at[j],
            device_id=(me_d, partner),
            device_id_type=MESH,
        )

    def foreign_forward(j):
        slot = vid((x + N_X - j) % N_X, c)
        rows = pl.ds(ROWS, N_DP)
        return pltpu.make_async_remote_copy(
            src_ref=gbuf.at[slot, rows],
            dst_ref=gbuf.at[slot, rows],
            send_sem=fps.at[j],
            recv_sem=fpr.at[j],
            device_id=(me_d, partner),
            device_id_type=MESH,
        )

    def foreign_forwarded(j):
        slot = vid((x + N_X - j) % N_X, 1 - c)
        rows = pl.ds(ROWS, N_DP)
        pltpu.make_async_remote_copy(
            src_ref=gbuf.at[slot, rows],
            dst_ref=gbuf.at[slot, rows],
            send_sem=fps.at[j],
            recv_sem=fpr.at[j],
            device_id=(me_d, partner),
            device_id_type=MESH,
        ).wait_recv()

    for i, j in SPACE:
        if PLANE[i] != (0, 0) or j:
            foreign(i, j).start()
    gbuf[me_v, ROWS + me_d] = snd_f[me_d]
    for r in range(CHUNK):
        gbuf[me_v, r] = block_of(r)

    def hop(chunk, k):
        slot, half, to = (
            (me_v, None, right),
            (me_v, None, left),
            (me_v, None, partner),
            (left, 0, right),
            (right, 1, left),
            (left, None, partner),
            (right, None, partner),
            (vid(xo, c), 0, partner),
            (vid(xo, c), 1, partner),
        )[k]
        return ag_copy(chunk, k, slot, half, to)

    def ag_copy(chunk, k, slot, half, to):
        rows = pl.ds(BASE[chunk], CHUNK) if half is None else pl.ds(BASE[chunk] + half * 8, 8)
        return pltpu.make_async_remote_copy(
            src_ref=gbuf.at[slot, rows],
            dst_ref=gbuf.at[slot, rows],
            send_sem=ag_s.at[chunk, k],
            recv_sem=ag_r.at[chunk, k],
            device_id=(me_d, to),
            device_id_type=MESH,
        )

    def arrived(chunk, k):
        slot, half = (
            (left, None),
            (right, None),
            (partner, None),
            (vid(xo, c), 0),
            (vid(xo, c), 1),
            (vid(xl, 1 - c), None),
            (vid(xr, 1 - c), None),
            (vid(xo, 1 - c), 0),
            (vid(xo, 1 - c), 1),
        )[k]
        ag_copy(chunk, k, slot, half, partner).wait_recv()

    def send_own(chunk):
        for k in range(3):
            hop(chunk, k).start()

    def forward_near(chunk):
        arrived(chunk, 0)
        hop(chunk, 3).start()
        hop(chunk, 5).start()
        arrived(chunk, 1)
        hop(chunk, 4).start()
        hop(chunk, 6).start()

    def forward_far(chunk):
        arrived(chunk, 3)
        hop(chunk, 7).start()
        arrived(chunk, 4)
        hop(chunk, 8).start()

    def all_here(chunk):
        for k in (2, 5, 6, 7, 8):
            arrived(chunk, k)

    send_own(FIRST)
    for r in range(CHUNK, 2 * CHUNK):
        gbuf[me_v, r] = block_of(r)
    send_own(LAST)

    seg = iota((1, 128), 1) // H
    in_seg = iota((1, 128), 1) % H
    l_r.wait()
    rates = dot_t(xin, wr_v[...])
    decay = jnp.zeros((1, 128), F32)
    bias = jnp.zeros((1, 128), F32)
    for h in range(H):
        decay = jnp.where(in_seg == h, logd_ref[h], decay)
        bias = jnp.where(in_seg == h, bias_ref[h], bias)
    wide = jnp.concatenate([rates, rates], axis=1)
    turned = pltpu.roll(wide, H, 1)
    odd = seg % 2 == 1
    rowq[RETAIN : RETAIN + ALL] = jnp.exp(-jnp.exp(decay) * jax.nn.softplus(jnp.where(odd, wide, turned) + bias))
    rowq[STRENGTH : STRENGTH + ALL] = jax.nn.sigmoid(jnp.where(odd, turned, wide))
    l_v.wait()
    values = dot(xin, wv_v[...])
    for g in range(GROUPS):
        rowq[VALUES + g * ALL : VALUES + (g + 1) * ALL] = values[:, g * 128 : (g + 1) * 128]
    forward_near(FIRST)
    l_g.wait()
    gating = dot(xin, wg_v[...])
    for g in range(GROUPS):
        rowq[GATING + g * ALL : GATING + (g + 1) * ALL] = gating[:, g * 128 : (g + 1) * 128]
    forward_near(LAST)
    forward_far(FIRST)
    for j in (0, 1, 3, 2):
        foreign_all(j).wait_recv()
        foreign_forward(j).start()
    forward_far(LAST)

    lane = iota((8, 128), 1)
    sub = iota((8, 128), 0)
    state_masks = [(lane % H) // 2 == 2 * i + sub // 4 for i in range(8)]
    gram_masks = [(lane % 64) // 4 == 2 * i + sub // 4 for i in range(8)]

    def diagonal(full, masks):
        sums = []
        for kind in range(2):
            acc = jnp.zeros((8, 128), F32)
            for i in range(8):
                at = kind * 64 + i * 8
                acc = jnp.where(masks[i], full[at : at + 8], acc)
            sums.append(acc + pltpu.roll(acc, 4, 0))
        return jnp.where(sub < 4, sums[0], sums[1])

    def contract(qk, state):
        full = dot_t(qk, state.reshape(COLS, DK).astype(BF16))
        return [diagonal(full[:, g * 128 : (g + 1) * 128], state_masks) for g in range(GROUPS)]

    def own_rows(first, count):
        def one(r, _):
            qk = gbuf[:, r].reshape(N_VALUE * TILE, DK)
            at = pl.multiple_of(r * 8, 8)
            for g, block in enumerate(contract(qk, st_v[r])):
                msc[g, pl.ds(at, 8)] = block
            msc[GROUPS, pl.ds(at, 8)] = diagonal(dot_t(qk, qk), gram_masks)
            return 0

        def two(i, _):
            one(first + 2 * i, 0)
            one(first + 2 * i + 1, 0)
            return 0

        lax.fori_loop(0, count // 2, two, 0)

    def foreign_rows():
        def one(d):
            slot = jnp.int32(0)
            for t in range(STEPS):
                for j in range(REPLACED):
                    slot = jnp.where(own_ref[t, j, d] == me_d, slot_ref[t, j, d], slot)
            qk = gbuf[:, ROWS + d].reshape(N_VALUE * TILE, DK)
            blocks = contract(qk, pf_v[slot])
            rsnd[d] = jnp.concatenate(blocks, axis=0).astype(BF16)

        def two(i, _):
            one(2 * i)
            one(2 * i + 1)
            return 0

        lax.fori_loop(0, N_DP // 2, two, 0)

    def back(i):
        dst = peer(i)
        return pltpu.make_async_remote_copy(
            src_ref=rsnd.at[dst],
            dst_ref=rrcv.at[me_d],
            send_sem=bs.at[i],
            recv_sem=br.at[i],
            device_id=(dst, me_v),
            device_id_type=MESH,
        )

    l_p.wait()
    for j in (0, 1, 3, 2):
        foreign_forwarded(j)
    foreign_rows()
    for i in range(N_DP):
        if PLANE[i] != (0, 0):
            back(i).start()
    rrcv[me_d] = rsnd[me_d]
    l_s.wait()
    all_here(FIRST)
    own_rows(0, CHUNK)
    all_here(LAST)
    own_rows(CHUNK, CHUNK)

    gram = [msc[GROUPS, pl.ds(k, ROWS, stride=8), :] for k in range(2 * STEPS)]
    src = iota((DK, 128), 0)
    head = (iota((DK, 128), 1) % H) // 2
    spread = [(src == 64 + head * 4 + s).astype(F32) for s in range(STEPS)]
    exact = dict(precision=lax.Precision.HIGHEST)
    by_key = dot(jnp.concatenate(gram, axis=0), jnp.concatenate(spread, axis=1), **exact)
    inv_k, inv_q = [], []
    for t in range(STEPS):
        kk = by_key[(STEPS + t) * ROWS : (STEPS + t + 1) * ROWS, t * 128 : (t + 1) * 128]
        qq = dot(gram[t], (src == head * 4 + t).astype(F32), **exact)
        inv_k.append(lax.rsqrt(kk + 1e-06))
        inv_q.append(lax.rsqrt(qq + 1e-06) * DK ** (-0.5))
        rowq[INV_K + t * ROWS : INV_K + (t + 1) * ROWS] = inv_k[t]
        rowq[INV_Q + t * ROWS : INV_Q + (t + 1) * ROWS] = inv_q[t]
    for t in range(STEPS):
        for s in range(t + 1):
            if s < t:
                at = KEY_KEY + PAIRS.index((s, t)) * ROWS
                kk = by_key[(STEPS + t) * ROWS : (STEPS + t + 1) * ROWS, s * 128 : (s + 1) * 128]
                rowq[at : at + ROWS] = kk * (inv_k[s] * inv_k[t])
            at = KEY_QUERY + PAIRS.index((s, t)) * ROWS
            kq = by_key[t * ROWS : (t + 1) * ROWS, s * 128 : (s + 1) * 128]
            rowq[at : at + ROWS] = kq * (inv_k[s] * inv_q[t])

    def recurrence(get, contracted, fresh):
        readouts = [[None] * GROUPS for _ in range(STEPS)]
        squares = [None] * STEPS
        for g in range(GROUPS):
            written = []
            kept = None
            for t in range(STEPS):
                a, b = get(RETAIN + t * ROWS), get(STRENGTH + t * ROWS)
                kept = a if kept is None else kept * a
                written = [w * a for w in written]
                if fresh is not None:
                    kept = jnp.where(fresh[t], a, kept)
                    written = [jnp.where(fresh[t], 0.0, w) for w in written]
                memory = kept * contracted(g, STEPS + t) * get(INV_K + t * ROWS)
                readout = kept * contracted(g, t) * get(INV_Q + t * ROWS)
                for s, w in enumerate(written):
                    at = PAIRS.index((s, t)) * ROWS
                    memory = memory + w * get(KEY_KEY + at)
                    readout = readout + w * get(KEY_QUERY + at)
                update = (get(VALUES + g * ALL + t * ROWS) - memory) * b
                readout = readout + update * get(KEY_QUERY + PAIRS.index((t, t)) * ROWS)
                written.append(update)
                readouts[t][g] = readout
                square = readout * readout
                squares[t] = square if g == 0 else squares[t] + square
        packed = jnp.zeros_like(squares[0])
        for t in range(STEPS):
            total = squares[t] + pltpu.roll(squares[t], 64, 1)
            total = total + pltpu.roll(total, 32, 1)
            packed = jnp.where(seg == t, total, packed)
        return readouts, packed

    def silu_gain(readouts, get):
        for g in range(GROUPS):
            gain = jnp.zeros((1, 128), F32)
            for e in range(4):
                gain = jnp.where(seg == e, gain_ref[g * 4 + e], gain)
            for t in range(STEPS):
                gate = get(GATING + g * ALL + t * ROWS)
                readouts[t][g] = readouts[t][g] * gain * (gate * jax.nn.sigmoid(gate))

    def scalings(summed):
        out = []
        for t in range(STEPS):
            total = jnp.where(seg == t, summed, 0.0)
            total = total + pltpu.roll(total, 64, 1)
            total = total + pltpu.roll(total, 32, 1)
            out.append(lax.rsqrt(total * (1.0 / DV) + 1e-06))
        return out

    def exchange(buf, s_sem, r_sem):
        def one(i, slot):
            return pltpu.make_async_remote_copy(
                src_ref=buf.at[slot],
                dst_ref=buf.at[slot],
                send_sem=s_sem.at[i],
                recv_sem=r_sem.at[i],
                device_id=(me_d, (me_v + i) % N_VALUE),
                device_id_type=MESH,
            )

        sends = [one(i, me_v) for i in range(1, N_VALUE)]
        arrivals = [one(i, (me_v + N_VALUE - i) % N_VALUE) for i in range(1, N_VALUE)]
        return sends, arrivals

    def row_get(at):
        return rowq[at : at + ROWS]

    readouts, packed = recurrence(row_get, lambda g, k: msc[g, pl.ds(k, ROWS, stride=8), :], None)
    sqbuf[me_v] = packed.astype(BF16)
    sq_sends, sq_arrivals = exchange(sqbuf, qs, qr)
    for copy in sq_sends:
        copy.start()

    slots = [(t, j) for t in range(STEPS) for j in range(REPLACED)]
    for k, (t, j) in enumerate(slots):
        slotq[k * QUANTITIES : (k + 1) * QUANTITIES] = rowq[pl.ds(fin_ref[t, j, me_d], QUANTITIES, stride=ROWS), :]

    def slot_get(at):
        return slotq[pl.ds(at // ROWS, len(slots), stride=QUANTITIES), :]

    silu_gain(readouts, row_get)
    slot_of = jnp.full((ALL, 128), -1, jnp.int32)
    take_of = jnp.full((ALL, len(slots) * STEPS), -1, jnp.int32)
    for k, (t, j) in enumerate(slots):
        done = fin_ref[t, j, me_d]
        wide_row, thin_row = iota(slot_of.shape, 0), iota(take_of.shape, 0)
        slot_of = jnp.where((wide_row % ROWS == done) & (wide_row // ROWS >= t), k, slot_of)
        take_of = jnp.where((thin_row % ROWS == done) & (thin_row // ROWS >= t), k, take_of)
    column = iota(take_of.shape, 1)
    same_step = column // len(slots) == iota(take_of.shape, 0) // ROWS
    take = ((take_of == column % len(slots)) & same_step).astype(BF16)

    for i in range(N_DP):
        if PLANE[i] != (0, 0):
            back(i).wait_recv()
    for k, (t, j) in enumerate(slots):
        rf[k * GROUPS * 8 : (k + 1) * GROUPS * 8] = rrcv[own_ref[t, j, me_d]].astype(F32)
    slot_row = iota((len(slots), 128), 0)
    slot_readouts, slot_packed = recurrence(
        slot_get,
        lambda g, k: rf[pl.ds(g * 8 + k, len(slots), stride=GROUPS * 8), :],
        [slot_row // REPLACED == t for t in range(STEPS)],
    )
    ssqbuf[me_v] = slot_packed
    ssq_sends, ssq_arrivals = exchange(ssqbuf, sqs, sqr)
    for copy in ssq_sends:
        copy.start()
    silu_gain(slot_readouts, slot_get)

    for copy in sq_arrivals:
        copy.wait_recv()
    scales = scalings(jnp.sum(sqbuf[...].astype(F32), axis=0))
    for t in range(STEPS):
        for g in range(GROUPS):
            gat_s[t * ROWS : (t + 1) * ROWS, g * 128 : (g + 1) * 128] = (readouts[t][g] * scales[t]).astype(BF16)

    l_o.wait()
    gated = gat_s[...]
    order = (xo, xr, xl, x)

    def project(to):
        at = pl.multiple_of(to * PIECE, PIECE)
        return dot(gated, wo_v[:, pl.ds(at, PIECE)])

    def first_copy(k):
        return pltpu.make_async_remote_copy(
            src_ref=r1_snd.at[k],
            dst_ref=r1_rcv.at[k],
            send_sem=r1s.at[k],
            recv_sem=r1r.at[k],
            device_id=(me_d, partner),
            device_id_type=MESH,
        )

    def second_copy(k):
        return pltpu.make_async_remote_copy(
            src_ref=r2_snd.at[k],
            dst_ref=r2_rcv.at[k],
            send_sem=r2s.at[k],
            recv_sem=r2r.at[k],
            device_id=(me_d, vid(order[k], c)),
            device_id_type=MESH,
        )

    for k in range(N_X):
        r1_snd[k] = project(vid(order[k], 1 - c)).astype(BF16)
        first_copy(k).start()
    for k in range(N_X):
        part[k] = project(vid(order[k], c))
    for k in range(N_X - 1):
        first_copy(k).wait_recv()
        r2_snd[k] = (part[k] + r1_rcv[k].astype(F32)).astype(BF16)
        second_copy(k).start()

    for copy in ssq_arrivals:
        copy.wait_recv()
    slot_scales = scalings(jnp.sum(ssqbuf[...], axis=0))
    slot_gated = jnp.concatenate(
        [
            jnp.concatenate([slot_readouts[t][g] * slot_scales[t] for g in range(GROUPS)], axis=1)
            for t in range(STEPS)
        ],
        axis=0,
    ).astype(BF16)

    def slot_project(to):
        at = pl.multiple_of(to * PIECE, PIECE)
        return dot(slot_gated, wo_v[:, pl.ds(at, PIECE)])

    def slot_copy(i):
        return pltpu.make_async_remote_copy(
            src_ref=s_snd.at[i],
            dst_ref=s_rcv.at[i],
            send_sem=ss.at[i],
            recv_sem=sr.at[i],
            device_id=(me_d, (me_v + i) % N_VALUE),
            device_id_type=MESH,
        )

    for i in (4, 3, 5, 2, 6, 1, 7):
        s_snd[i] = slot_project((me_v + i) % N_VALUE).astype(BF16)
        slot_copy(i).start()
    slot_total = slot_project(me_v)

    first_copy(3).wait_recv()
    total = part[3] + r1_rcv[3].astype(F32)
    for k in (1, 2, 0):
        second_copy(k).wait_recv()
        total = total + r2_rcv[k].astype(F32)
    for i in (1, 7, 2, 6, 3, 5, 4):
        slot_copy(i).wait_recv()
        slot_total = slot_total + s_rcv[i].astype(F32)
    chosen = dot(take, slot_total.astype(BF16))
    for half in range(PIECE // 128):
        lanes = slice(half * 128, (half + 1) * 128)
        out_ref[:, lanes] = jnp.where(slot_of >= 0, chosen[:, lanes], total[:, lanes]).astype(BF16)

    for j in range(N_X):
        foreign_all(j).wait_send()
        foreign_forward(j).wait_send()
    for i in range(N_DP):
        if PLANE[i] != (0, 0):
            back(i).wait_send()
    for chunk in range(2):
        for k in range(9):
            hop(chunk, k).wait_send()
    for copy in sq_sends + ssq_sends:
        copy.wait_send()
    for k in range(N_X):
        first_copy(k).wait_send()
    for k in range(N_X - 1):
        second_copy(k).wait_send()
    for i in range(1, N_VALUE):
        slot_copy(i).wait_send()


def on_device(
    inputs,
    qk_weight,
    value_weight,
    output_gate_weight,
    rate_weight,
    log_decay,
    decay_bias,
    norm_gain,
    out_weight,
    states,
    prefilled,
    finished,
    new_owner,
    new_slot,
):
    hbm = pl.BlockSpec(memory_space=pl.ANY)
    dma = pltpu.SemaphoreType.DMA
    produced = pl.pallas_call(
        kernel,
        out_shape=jax.ShapeDtypeStruct((STEPS * ROWS, PIECE), BF16),
        in_specs=[hbm] * 14,
        out_specs=pl.BlockSpec(memory_space=pltpu.VMEM),
        scratch_shapes=[
            pltpu.SMEM((STEPS, REPLACED, N_DP), jnp.int32),
            pltpu.SMEM((STEPS, REPLACED, N_DP), jnp.int32),
            pltpu.SMEM((STEPS, REPLACED, N_DP), jnp.int32),
            pltpu.SMEM((H,), F32),
            pltpu.SMEM((H,), F32),
            pltpu.SMEM((DV // N_VALUE,), F32),
            pltpu.VMEM((STEPS, ROWS, WIDTH), BF16),
            pltpu.VMEM((WIDTH, COLS), BF16),
            pltpu.VMEM((WIDTH, COLS), BF16),
            pltpu.VMEM((WIDTH, COLS), BF16),
            pltpu.VMEM((2 * H, WIDTH), BF16),
            pltpu.VMEM((COLS, WIDTH), BF16),
            pltpu.VMEM((ROWS, 16, H, DK), F32),
            pltpu.VMEM((16, 16, H, DK), F32),
            pltpu.VMEM((TILE * BLOCKS, DK), F32),
            pltpu.VMEM((N_DP, TILE, DK), BF16),
            pltpu.VMEM((N_VALUE, BLOCKS, TILE, DK), BF16),
            pltpu.VMEM((GROUPS + 1, ROWS * 8, 128), F32),
            pltpu.VMEM((N_DP, GROUPS * 8, 128), BF16),
            pltpu.VMEM((N_DP, GROUPS * 8, 128), BF16),
            pltpu.VMEM((STEPS * REPLACED * GROUPS * 8, 128), F32),
            pltpu.VMEM((QUANTITIES * ROWS, 128), F32),
            pltpu.VMEM((STEPS * REPLACED * QUANTITIES, 128), F32),
            pltpu.VMEM((STEPS * ROWS, COLS), BF16),
            pltpu.VMEM((N_VALUE, ROWS, 128), BF16),
            pltpu.VMEM((N_VALUE, STEPS * REPLACED, 128), F32),
            pltpu.VMEM((N_X, STEPS * ROWS, PIECE), BF16),
            pltpu.VMEM((N_X, STEPS * ROWS, PIECE), BF16),
            pltpu.VMEM((N_X, STEPS * ROWS, PIECE), F32),
            pltpu.VMEM((N_X - 1, STEPS * ROWS, PIECE), BF16),
            pltpu.VMEM((N_X - 1, STEPS * ROWS, PIECE), BF16),
            pltpu.VMEM((N_VALUE, STEPS * STEPS * REPLACED, PIECE), BF16),
            pltpu.VMEM((N_VALUE, STEPS * STEPS * REPLACED, PIECE), BF16),
            dma((15,)),
            dma((2, 9)),
            dma((2, 9)),
            dma((N_X,)),
            dma((N_X,)),
            dma((N_X,)),
            dma((N_X,)),
            dma((N_DP,)),
            dma((N_DP,)),
            dma((N_VALUE,)),
            dma((N_VALUE,)),
            dma((N_X,)),
            dma((N_X,)),
            dma((N_X - 1,)),
            dma((N_X - 1,)),
            dma((N_VALUE,)),
            dma((N_VALUE,)),
            dma((N_VALUE,)),
            dma((N_VALUE,)),
        ],
        compiler_params=pltpu.CompilerParams(
            collective_id=0, has_side_effects=True, vmem_limit_bytes=56 * 2**20
        ),
        name="delta_steps",
    )(
        finished.transpose(0, 2, 1),
        new_owner.transpose(0, 2, 1),
        new_slot.transpose(0, 2, 1),
        log_decay,
        decay_bias,
        norm_gain,
        inputs,
        qk_weight,
        value_weight,
        output_gate_weight,
        rate_weight.T,
        out_weight,
        states,
        prefilled,
    )
    return produced.reshape(STEPS, ROWS, PIECE)


def solution(mesh):
    return jax.shard_map(
        on_device,
        mesh=mesh,
        in_specs=(
            P(None, "dp", None),
            P(None, "value"),
            P(None, "value"),
            P(None, "value"),
            P(),
            P(),
            P(),
            P("value"),
            P("value", None),
            P("dp", "value", None, None),
            P("dp", "value", None, None),
            P(),
            P(),
            P(),
        ),
        out_specs=P(None, "dp", "value"),
        check_vma=False,
    )
```

```python
import functools

import jax
import jax.numpy as jnp
from jax import lax
from jax.experimental import pallas as pl
from jax.experimental.pallas import tpu as pltpu
from jax.sharding import PartitionSpec as P

F32 = jnp.float32
BF16 = jnp.bfloat16
MESH = pl.DeviceIdType.MESH

STEPS = 4
REPLACED = 2
N_DP = 16
N_VALUE = 8
N_X = 4
ROWS = 32
H = 32
DK = 128
DV = 128
WIDTH = 2048
COLS = 512
PIECE = 256
BLOCKS = ROWS + N_DP
HEADS = 4
TILE = HEADS * STEPS
GROUPS = COLS // 128
ALL = STEPS * ROWS

PAIRS = [(s, t) for t in range(STEPS) for s in range(t + 1)]
VALUES, GATING = 0, GROUPS * ALL
RETAIN = 2 * GROUPS * ALL
STRENGTH, INV_K, INV_Q = RETAIN + ALL, RETAIN + 2 * ALL, RETAIN + 3 * ALL
KEY_KEY = RETAIN + 4 * ALL
KEY_QUERY = KEY_KEY + len(PAIRS) * ROWS
QUANTITIES = KEY_QUERY // ROWS + len(PAIRS)

FIRST, LAST = 0, 1
BASE = (0, 16)
CHUNK = 16
UNROLL = 8


def ring(k):
    return min(k, N_X - k)


PLANE = sorted(((a, b) for a in range(N_X) for b in range(N_X)), key=lambda o: -ring(o[0]) - ring(o[1]))
SPACE = sorted(((i, j) for i in range(N_DP) for j in range(N_X)), key=lambda o: -sum(map(ring, (*PLANE[o[0]], o[1]))))


def iota(shape, dim):
    return lax.broadcasted_iota(jnp.int32, shape, dim)


def dot(a, b, **kw):
    return jnp.dot(a, b, preferred_element_type=F32, **kw)


def dot_t(a, b):
    return lax.dot_general(a, b, (((1,), (1,)), ((), ())), preferred_element_type=F32)


def kernel(
    fin_hbm,
    own_hbm,
    slot_hbm,
    logd_hbm,
    bias_hbm,
    gain_hbm,
    x_hbm,
    wqk_hbm,
    wv_hbm,
    wg_hbm,
    wr_hbm,
    wo_hbm,
    st_hbm,
    pf_hbm,
    out_ref,
    fin_ref,
    own_ref,
    slot_ref,
    logd_ref,
    bias_ref,
    gain_ref,
    x_v,
    wqk_v,
    wv_v,
    wg_v,
    wr_v,
    wo_v,
    st_v,
    pf_v,
    zf,
    snd_f,
    gbuf,
    msc,
    rsnd,
    rrcv,
    rf,
    rowq,
    slotq,
    gat_s,
    sqbuf,
    ssqbuf,
    r1_snd,
    r1_rcv,
    part,
    r2_snd,
    r2_rcv,
    s_snd,
    s_rcv,
    loc,
    ag_s,
    ag_r,
    fs,
    fr,
    fps,
    fpr,
    bs,
    br,
    qs,
    qr,
    r1s,
    r1r,
    r2s,
    r2r,
    sqs,
    sqr,
    ss,
    sr,
):
    me_d = lax.axis_index("dp")
    me_v = lax.axis_index("value")
    x = me_v // 2
    c = me_v % 2

    def vid(xx, cc):
        return xx * 2 + cc

    partner = vid(x, 1 - c)

    def peer(i):
        dz, dy = PLANE[i]
        return ((me_d // N_X + dz) % N_X) * N_X + (me_d % N_X + dy) % N_X

    barrier = pltpu.get_barrier_semaphore()
    greeted = 0
    for i, j in SPACE:
        if PLANE[i] != (0, 0) or j:
            to = (peer(i), vid((x + j) % N_X, c))
            pl.semaphore_signal(barrier, inc=1, device_id=to, device_id_type=MESH)
            greeted += 1
    for j in range(N_X):
        to = (me_d, vid((x + j) % N_X, 1 - c))
        pl.semaphore_signal(barrier, inc=1, device_id=to, device_id_type=MESH)
        greeted += 1

    def load(src, dst, k):
        cp = pltpu.make_async_copy(src, dst, loc.at[k])
        cp.start()
        return cp

    l_x = load(x_hbm, x_v, 0)
    l_qk = load(wqk_hbm, wqk_v, 1)
    scalars = (
        (fin_hbm, fin_ref),
        (own_hbm, own_ref),
        (slot_hbm, slot_ref),
        (logd_hbm, logd_ref),
        (bias_hbm, bias_ref),
        (gain_hbm, gain_ref),
    )
    l_scalars = [load(src, dst, 9 + k) for k, (src, dst) in enumerate(scalars)]
    l_r = load(wr_hbm, wr_v, 2)
    l_v = load(wv_hbm, wv_v, 3)
    l_g = load(wg_hbm, wg_v, 4)
    l_p = load(pf_hbm, pf_v, 5)
    l_s = load(st_hbm, st_v, 6)
    l_o = load(wo_hbm, wo_v, 8)

    l_x.wait()
    l_qk.wait()
    xin = x_v[...].reshape(STEPS * ROWS, WIDTH)
    joined = dot(xin, wqk_v[...]).astype(BF16)
    joined_f = joined.astype(F32)
    for copy in l_scalars:
        copy.wait()
    pick = jnp.zeros((N_DP, ROWS), F32)
    for t in range(STEPS):
        for j in range(REPLACED):
            hit = (iota((N_DP, ROWS), 0) == own_ref[t, j, me_d]) & (iota((N_DP, ROWS), 1) == fin_ref[t, j, me_d])
            pick = jnp.where(hit, 1.0, pick)
    pick = pick.astype(BF16)
    for t in range(STEPS):
        chosen = dot(pick, joined[t * ROWS : (t + 1) * ROWS])
        for h in range(HEADS):
            at = (h * STEPS + t) * BLOCKS
            zf[at : at + ROWS] = joined_f[t * ROWS : (t + 1) * ROWS, h * 128 : (h + 1) * 128]
            zf[at + ROWS : at + BLOCKS] = chosen[:, h * 128 : (h + 1) * 128]

    def block_of(r):
        return zf[pl.ds(r, TILE, stride=BLOCKS), :].astype(BF16)

    for o in range(N_DP):
        snd_f[o] = block_of(ROWS + o)
    pl.semaphore_wait(barrier, greeted)

    def foreign(i, j):
        dst = peer(i)
        return pltpu.make_async_remote_copy(
            src_ref=snd_f.at[dst],
            dst_ref=gbuf.at[me_v, ROWS + me_d],
            send_sem=fs.at[j],
            recv_sem=fr.at[j],
            device_id=(dst, vid((x + j) % N_X, c)),
            device_id_type=MESH,
        )

    def foreign_all(j):
        slot = vid((x + N_X - j) % N_X, c)
        first = 1 if j == 0 else 0
        rows = pl.ds(ROWS, N_DP - first)
        return pltpu.make_async_remote_copy(
            src_ref=gbuf.at[slot, rows],
            dst_ref=gbuf.at[slot, rows],
            send_sem=fs.at[j],
            recv_sem=fr.at[j],
            device_id=(me_d, partner),
            device_id_type=MESH,
        )

    def foreign_forward(j):
        slot = vid((x + N_X - j) % N_X, c)
        rows = pl.ds(ROWS, N_DP)
        return pltpu.make_async_remote_copy(
            src_ref=gbuf.at[slot, rows],
            dst_ref=gbuf.at[slot, rows],
            send_sem=fps.at[j],
            recv_sem=fpr.at[j],
            device_id=(me_d, partner),
            device_id_type=MESH,
        )

    def foreign_forwarded(j):
        slot = vid((x + N_X - j) % N_X, 1 - c)
        rows = pl.ds(ROWS, N_DP)
        pltpu.make_async_remote_copy(
            src_ref=gbuf.at[slot, rows],
            dst_ref=gbuf.at[slot, rows],
            send_sem=fps.at[j],
            recv_sem=fpr.at[j],
            device_id=(me_d, partner),
            device_id_type=MESH,
        ).wait_recv()

    for i, j in SPACE:
        if PLANE[i] != (0, 0) or j:
            foreign(i, j).start()
    gbuf[me_v, ROWS + me_d] = snd_f[me_d]
    for r in range(CHUNK):
        gbuf[me_v, r] = block_of(r)

    def gather(chunk, k, slot, to):
        rows = pl.ds(BASE[chunk], CHUNK)
        return pltpu.make_async_remote_copy(
            src_ref=gbuf.at[slot, rows],
            dst_ref=gbuf.at[slot, rows],
            send_sem=ag_s.at[chunk, k],
            recv_sem=ag_r.at[chunk, k],
            device_id=(me_d, to),
            device_id_type=MESH,
        )

    def along(chunk, j):
        return gather(chunk, j, me_v, vid((x + j) % N_X, c) if j else partner)

    def arrived(chunk, j):
        gather(chunk, j, vid((x + N_X - j) % N_X, c) if j else partner, partner).wait_recv()

    def forward(chunk, j):
        return gather(chunk, N_X - 1 + j, vid((x + N_X - j) % N_X, c), partner)

    def forwarded(chunk, j):
        gather(chunk, N_X - 1 + j, vid((x + N_X - j) % N_X, 1 - c), partner).wait_recv()

    def send_own(chunk):
        for j in (2, 1, 3, 0):
            along(chunk, j).start()

    def pass_on(chunk):
        for j in (1, 3, 2):
            arrived(chunk, j)
            forward(chunk, j).start()

    def all_here(chunk):
        arrived(chunk, 0)
        for j in (1, 3, 2):
            forwarded(chunk, j)

    send_own(FIRST)
    for r in range(CHUNK, 2 * CHUNK):
        gbuf[me_v, r] = block_of(r)
    send_own(LAST)

    seg = iota((1, 128), 1) // H
    in_seg = iota((1, 128), 1) % H
    l_r.wait()
    rates = dot_t(xin, wr_v[...])
    decay = jnp.zeros((1, 128), F32)
    bias = jnp.zeros((1, 128), F32)
    for h in range(H):
        decay = jnp.where(in_seg == h, logd_ref[h], decay)
        bias = jnp.where(in_seg == h, bias_ref[h], bias)
    wide = jnp.concatenate([rates, rates], axis=1)
    turned = pltpu.roll(wide, H, 1)
    odd = seg % 2 == 1
    rowq[RETAIN : RETAIN + ALL] = jnp.exp(-jnp.exp(decay) * jax.nn.softplus(jnp.where(odd, wide, turned) + bias))
    rowq[STRENGTH : STRENGTH + ALL] = jax.nn.sigmoid(jnp.where(odd, turned, wide))
    l_v.wait()
    values = dot(xin, wv_v[...])
    for g in range(GROUPS):
        rowq[VALUES + g * ALL : VALUES + (g + 1) * ALL] = values[:, g * 128 : (g + 1) * 128]
    l_g.wait()
    gating = dot(xin, wg_v[...])
    for g in range(GROUPS):
        rowq[GATING + g * ALL : GATING + (g + 1) * ALL] = gating[:, g * 128 : (g + 1) * 128]
    for j in (0, 1, 3, 2):
        foreign_all(j).wait_recv()
        foreign_forward(j).start()
    pass_on(FIRST)

    lane = iota((8, 128), 1)
    sub = iota((8, 128), 0)
    state_masks = [(lane % H) // 2 == 2 * i + sub // 4 for i in range(8)]
    gram_masks = [(lane % 64) // 4 == 2 * i + sub // 4 for i in range(8)]

    def diagonal(full, masks):
        sums = []
        for kind in range(2):
            acc = jnp.zeros((8, 128), F32)
            for i in range(8):
                at = kind * 64 + i * 8
                acc = jnp.where(masks[i], full[at : at + 8], acc)
            sums.append(acc + pltpu.roll(acc, 4, 0))
        return jnp.where(sub < 4, sums[0], sums[1])

    def contract(qk, state):
        full = dot_t(qk, state.reshape(COLS, DK).astype(BF16))
        return [diagonal(full[:, g * 128 : (g + 1) * 128], state_masks) for g in range(GROUPS)]

    def own_rows(first, count):
        def one(r):
            qk = gbuf[:, r].reshape(N_VALUE * TILE, DK)
            at = pl.multiple_of(r * 8, 8)
            for g, block in enumerate(contract(qk, st_v[r])):
                msc[g, pl.ds(at, 8)] = block
            msc[GROUPS, pl.ds(at, 8)] = diagonal(dot_t(qk, qk), gram_masks)

        def some(i, _):
            for k in range(UNROLL):
                one(first + UNROLL * i + k)
            return 0

        lax.fori_loop(0, count // UNROLL, some, 0)

    def foreign_rows():
        def one(d):
            slot = jnp.int32(0)
            for t in range(STEPS):
                for j in range(REPLACED):
                    slot = jnp.where(own_ref[t, j, d] == me_d, slot_ref[t, j, d], slot)
            qk = gbuf[:, ROWS + d].reshape(N_VALUE * TILE, DK)
            blocks = contract(qk, pf_v[slot])
            rsnd[d] = jnp.concatenate(blocks, axis=0).astype(BF16)

        def some(i, _):
            for k in range(UNROLL):
                one(UNROLL * i + k)
            return 0

        lax.fori_loop(0, N_DP // UNROLL, some, 0)

    def back(i):
        dst = peer(i)
        return pltpu.make_async_remote_copy(
            src_ref=rsnd.at[dst],
            dst_ref=rrcv.at[me_d],
            send_sem=bs.at[i],
            recv_sem=br.at[i],
            device_id=(dst, me_v),
            device_id_type=MESH,
        )

    l_p.wait()
    for j in (0, 1, 3, 2):
        foreign_forwarded(j)
    foreign_rows()
    for i in range(N_DP):
        if PLANE[i] != (0, 0):
            back(i).start()
    rrcv[me_d] = rsnd[me_d]
    pass_on(LAST)
    l_s.wait()
    all_here(FIRST)
    own_rows(0, CHUNK)
    all_here(LAST)
    own_rows(CHUNK, CHUNK)

    gram = [msc[GROUPS, pl.ds(k, ROWS, stride=8), :] for k in range(2 * STEPS)]
    src = iota((DK, 128), 0)
    head = (iota((DK, 128), 1) % H) // 2
    spread = [(src == 64 + head * 4 + s).astype(F32) for s in range(STEPS)]
    exact = dict(precision=lax.Precision.HIGHEST)
    by_key = dot(jnp.concatenate(gram, axis=0), jnp.concatenate(spread, axis=1), **exact)
    inv_k, inv_q = [], []
    for t in range(STEPS):
        kk = by_key[(STEPS + t) * ROWS : (STEPS + t + 1) * ROWS, t * 128 : (t + 1) * 128]
        qq = dot(gram[t], (src == head * 4 + t).astype(F32), **exact)
        inv_k.append(lax.rsqrt(kk + 1e-06))
        inv_q.append(lax.rsqrt(qq + 1e-06) * DK ** (-0.5))
        rowq[INV_K + t * ROWS : INV_K + (t + 1) * ROWS] = inv_k[t]
        rowq[INV_Q + t * ROWS : INV_Q + (t + 1) * ROWS] = inv_q[t]
    for t in range(STEPS):
        for s in range(t + 1):
            if s < t:
                at = KEY_KEY + PAIRS.index((s, t)) * ROWS
                kk = by_key[(STEPS + t) * ROWS : (STEPS + t + 1) * ROWS, s * 128 : (s + 1) * 128]
                rowq[at : at + ROWS] = kk * (inv_k[s] * inv_k[t])
            at = KEY_QUERY + PAIRS.index((s, t)) * ROWS
            kq = by_key[t * ROWS : (t + 1) * ROWS, s * 128 : (s + 1) * 128]
            rowq[at : at + ROWS] = kq * (inv_k[s] * inv_q[t])

    def recurrence(get, contracted, fresh):
        readouts = [[None] * GROUPS for _ in range(STEPS)]
        squares = [None] * STEPS
        for g in range(GROUPS):
            written = []
            kept = None
            for t in range(STEPS):
                a, b = get(RETAIN + t * ROWS), get(STRENGTH + t * ROWS)
                kept = a if kept is None else kept * a
                written = [w * a for w in written]
                if fresh is not None:
                    kept = jnp.where(fresh[t], a, kept)
                    written = [jnp.where(fresh[t], 0.0, w) for w in written]
                memory = kept * contracted(g, STEPS + t) * get(INV_K + t * ROWS)
                readout = kept * contracted(g, t) * get(INV_Q + t * ROWS)
                for s, w in enumerate(written):
                    at = PAIRS.index((s, t)) * ROWS
                    memory = memory + w * get(KEY_KEY + at)
                    readout = readout + w * get(KEY_QUERY + at)
                update = (get(VALUES + g * ALL + t * ROWS) - memory) * b
                readout = readout + update * get(KEY_QUERY + PAIRS.index((t, t)) * ROWS)
                written.append(update)
                readouts[t][g] = readout
                square = readout * readout
                squares[t] = square if g == 0 else squares[t] + square
        packed = jnp.zeros_like(squares[0])
        for t in range(STEPS):
            total = squares[t] + pltpu.roll(squares[t], 64, 1)
            total = total + pltpu.roll(total, 32, 1)
            packed = jnp.where(seg == t, total, packed)
        return readouts, packed

    def silu_gain(readouts, get):
        for g in range(GROUPS):
            gain = jnp.zeros((1, 128), F32)
            for e in range(4):
                gain = jnp.where(seg == e, gain_ref[g * 4 + e], gain)
            for t in range(STEPS):
                gate = get(GATING + g * ALL + t * ROWS)
                readouts[t][g] = readouts[t][g] * gain * (gate * jax.nn.sigmoid(gate))

    def scalings(summed):
        out = []
        for t in range(STEPS):
            total = jnp.where(seg == t, summed, 0.0)
            total = total + pltpu.roll(total, 64, 1)
            total = total + pltpu.roll(total, 32, 1)
            out.append(lax.rsqrt(total * (1.0 / DV) + 1e-06))
        return out

    def exchange(buf, s_sem, r_sem):
        def one(i, slot):
            return pltpu.make_async_remote_copy(
                src_ref=buf.at[slot],
                dst_ref=buf.at[slot],
                send_sem=s_sem.at[i],
                recv_sem=r_sem.at[i],
                device_id=(me_d, (me_v + i) % N_VALUE),
                device_id_type=MESH,
            )

        sends = [one(i, me_v) for i in range(1, N_VALUE)]
        arrivals = [one(i, (me_v + N_VALUE - i) % N_VALUE) for i in range(1, N_VALUE)]
        return sends, arrivals

    def row_get(at):
        return rowq[at : at + ROWS]

    readouts, packed = recurrence(row_get, lambda g, k: msc[g, pl.ds(k, ROWS, stride=8), :], None)
    sqbuf[me_v] = packed.astype(BF16)
    sq_sends, sq_arrivals = exchange(sqbuf, qs, qr)
    for copy in sq_sends:
        copy.start()

    slots = [(t, j) for t in range(STEPS) for j in range(REPLACED)]
    for k, (t, j) in enumerate(slots):
        slotq[k * QUANTITIES : (k + 1) * QUANTITIES] = rowq[pl.ds(fin_ref[t, j, me_d], QUANTITIES, stride=ROWS), :]

    def slot_get(at):
        return slotq[pl.ds(at // ROWS, len(slots), stride=QUANTITIES), :]

    silu_gain(readouts, row_get)
    slot_of = jnp.full((ALL, 128), -1, jnp.int32)
    take_of = jnp.full((ALL, len(slots) * STEPS), -1, jnp.int32)
    for k, (t, j) in enumerate(slots):
        done = fin_ref[t, j, me_d]
        wide_row, thin_row = iota(slot_of.shape, 0), iota(take_of.shape, 0)
        slot_of = jnp.where((wide_row % ROWS == done) & (wide_row // ROWS >= t), k, slot_of)
        take_of = jnp.where((thin_row % ROWS == done) & (thin_row // ROWS >= t), k, take_of)
    column = iota(take_of.shape, 1)
    same_step = column // len(slots) == iota(take_of.shape, 0) // ROWS
    take = ((take_of == column % len(slots)) & same_step).astype(BF16)

    for i in range(N_DP):
        if PLANE[i] != (0, 0):
            back(i).wait_recv()
    for k, (t, j) in enumerate(slots):
        rf[k * GROUPS * 8 : (k + 1) * GROUPS * 8] = rrcv[own_ref[t, j, me_d]].astype(F32)
    slot_row = iota((len(slots), 128), 0)
    slot_readouts, slot_packed = recurrence(
        slot_get,
        lambda g, k: rf[pl.ds(g * 8 + k, len(slots), stride=GROUPS * 8), :],
        [slot_row // REPLACED == t for t in range(STEPS)],
    )
    ssqbuf[me_v] = slot_packed
    ssq_sends, ssq_arrivals = exchange(ssqbuf, sqs, sqr)
    for copy in ssq_sends:
        copy.start()
    silu_gain(slot_readouts, slot_get)

    for copy in sq_arrivals:
        copy.wait_recv()
    scales = scalings(jnp.sum(sqbuf[...].astype(F32), axis=0))
    for t in range(STEPS):
        for g in range(GROUPS):
            gat_s[t * ROWS : (t + 1) * ROWS, g * 128 : (g + 1) * 128] = (readouts[t][g] * scales[t]).astype(BF16)

    l_o.wait()
    gated = gat_s[...]
    order = [(x + j) % N_X for j in (2, 1, 3, 0)]

    def project(to):
        at = pl.multiple_of(to * PIECE, PIECE)
        return dot(gated, wo_v[:, pl.ds(at, PIECE)])

    def first_copy(k):
        return pltpu.make_async_remote_copy(
            src_ref=r1_snd.at[k],
            dst_ref=r1_rcv.at[k],
            send_sem=r1s.at[k],
            recv_sem=r1r.at[k],
            device_id=(me_d, partner),
            device_id_type=MESH,
        )

    def second_copy(k):
        return pltpu.make_async_remote_copy(
            src_ref=r2_snd.at[k],
            dst_ref=r2_rcv.at[k],
            send_sem=r2s.at[k],
            recv_sem=r2r.at[k],
            device_id=(me_d, vid(order[k], c)),
            device_id_type=MESH,
        )

    for k in range(N_X):
        r1_snd[k] = project(vid(order[k], 1 - c)).astype(BF16)
        first_copy(k).start()
    for k in range(N_X):
        part[k] = project(vid(order[k], c))
    for k in range(N_X - 1):
        first_copy(k).wait_recv()
        r2_snd[k] = (part[k] + r1_rcv[k].astype(F32)).astype(BF16)
        second_copy(k).start()

    for copy in ssq_arrivals:
        copy.wait_recv()
    slot_scales = scalings(jnp.sum(ssqbuf[...], axis=0))
    slot_gated = jnp.concatenate(
        [
            jnp.concatenate([slot_readouts[t][g] * slot_scales[t] for g in range(GROUPS)], axis=1)
            for t in range(STEPS)
        ],
        axis=0,
    ).astype(BF16)

    def slot_project(to):
        at = pl.multiple_of(to * PIECE, PIECE)
        return dot(slot_gated, wo_v[:, pl.ds(at, PIECE)])

    def slot_copy(i):
        return pltpu.make_async_remote_copy(
            src_ref=s_snd.at[i],
            dst_ref=s_rcv.at[i],
            send_sem=ss.at[i],
            recv_sem=sr.at[i],
            device_id=(me_d, (me_v + i) % N_VALUE),
            device_id_type=MESH,
        )

    for i in (4, 3, 5, 2, 6, 1, 7):
        s_snd[i] = slot_project((me_v + i) % N_VALUE).astype(BF16)
        slot_copy(i).start()
    slot_total = slot_project(me_v)

    first_copy(3).wait_recv()
    total = part[3] + r1_rcv[3].astype(F32)
    for k in (1, 2, 0):
        second_copy(k).wait_recv()
        total = total + r2_rcv[k].astype(F32)
    for i in (1, 7, 2, 6, 3, 5, 4):
        slot_copy(i).wait_recv()
        slot_total = slot_total + s_rcv[i].astype(F32)
    chosen = dot(take, slot_total.astype(BF16))
    for half in range(PIECE // 128):
        lanes = slice(half * 128, (half + 1) * 128)
        out_ref[:, lanes] = jnp.where(slot_of >= 0, chosen[:, lanes], total[:, lanes]).astype(BF16)

    for j in range(N_X):
        foreign_all(j).wait_send()
        foreign_forward(j).wait_send()
    for i in range(N_DP):
        if PLANE[i] != (0, 0):
            back(i).wait_send()
    for chunk in range(2):
        for j in range(N_X):
            along(chunk, j).wait_send()
        for j in range(1, N_X):
            forward(chunk, j).wait_send()
    for copy in sq_sends + ssq_sends:
        copy.wait_send()
    for k in range(N_X):
        first_copy(k).wait_send()
    for k in range(N_X - 1):
        second_copy(k).wait_send()
    for i in range(1, N_VALUE):
        slot_copy(i).wait_send()


def on_device(
    inputs,
    qk_weight,
    value_weight,
    output_gate_weight,
    rate_weight,
    log_decay,
    decay_bias,
    norm_gain,
    out_weight,
    states,
    prefilled,
    finished,
    new_owner,
    new_slot,
):
    hbm = pl.BlockSpec(memory_space=pl.ANY)
    dma = pltpu.SemaphoreType.DMA
    produced = pl.pallas_call(
        kernel,
        out_shape=jax.ShapeDtypeStruct((STEPS * ROWS, PIECE), BF16),
        in_specs=[hbm] * 14,
        out_specs=pl.BlockSpec(memory_space=pltpu.VMEM),
        scratch_shapes=[
            pltpu.SMEM((STEPS, REPLACED, N_DP), jnp.int32),
            pltpu.SMEM((STEPS, REPLACED, N_DP), jnp.int32),
            pltpu.SMEM((STEPS, REPLACED, N_DP), jnp.int32),
            pltpu.SMEM((H,), F32),
            pltpu.SMEM((H,), F32),
            pltpu.SMEM((DV // N_VALUE,), F32),
            pltpu.VMEM((STEPS, ROWS, WIDTH), BF16),
            pltpu.VMEM((WIDTH, COLS), BF16),
            pltpu.VMEM((WIDTH, COLS), BF16),
            pltpu.VMEM((WIDTH, COLS), BF16),
            pltpu.VMEM((2 * H, WIDTH), BF16),
            pltpu.VMEM((COLS, WIDTH), BF16),
            pltpu.VMEM((ROWS, 16, H, DK), F32),
            pltpu.VMEM((16, 16, H, DK), F32),
            pltpu.VMEM((TILE * BLOCKS, DK), F32),
            pltpu.VMEM((N_DP, TILE, DK), BF16),
            pltpu.VMEM((N_VALUE, BLOCKS, TILE, DK), BF16),
            pltpu.VMEM((GROUPS + 1, ROWS * 8, 128), F32),
            pltpu.VMEM((N_DP, GROUPS * 8, 128), BF16),
            pltpu.VMEM((N_DP, GROUPS * 8, 128), BF16),
            pltpu.VMEM((STEPS * REPLACED * GROUPS * 8, 128), F32),
            pltpu.VMEM((QUANTITIES * ROWS, 128), F32),
            pltpu.VMEM((STEPS * REPLACED * QUANTITIES, 128), F32),
            pltpu.VMEM((STEPS * ROWS, COLS), BF16),
            pltpu.VMEM((N_VALUE, ROWS, 128), BF16),
            pltpu.VMEM((N_VALUE, STEPS * REPLACED, 128), F32),
            pltpu.VMEM((N_X, STEPS * ROWS, PIECE), BF16),
            pltpu.VMEM((N_X, STEPS * ROWS, PIECE), BF16),
            pltpu.VMEM((N_X, STEPS * ROWS, PIECE), F32),
            pltpu.VMEM((N_X - 1, STEPS * ROWS, PIECE), BF16),
            pltpu.VMEM((N_X - 1, STEPS * ROWS, PIECE), BF16),
            pltpu.VMEM((N_VALUE, STEPS * STEPS * REPLACED, PIECE), BF16),
            pltpu.VMEM((N_VALUE, STEPS * STEPS * REPLACED, PIECE), BF16),
            dma((15,)),
            dma((2, 2 * N_X - 1)),
            dma((2, 2 * N_X - 1)),
            dma((N_X,)),
            dma((N_X,)),
            dma((N_X,)),
            dma((N_X,)),
            dma((N_DP,)),
            dma((N_DP,)),
            dma((N_VALUE,)),
            dma((N_VALUE,)),
            dma((N_X,)),
            dma((N_X,)),
            dma((N_X - 1,)),
            dma((N_X - 1,)),
            dma((N_VALUE,)),
            dma((N_VALUE,)),
            dma((N_VALUE,)),
            dma((N_VALUE,)),
        ],
        compiler_params=pltpu.CompilerParams(
            collective_id=0, has_side_effects=True, vmem_limit_bytes=56 * 2**20
        ),
        name="delta_steps",
    )(
        finished.transpose(0, 2, 1),
        new_owner.transpose(0, 2, 1),
        new_slot.transpose(0, 2, 1),
        log_decay,
        decay_bias,
        norm_gain,
        inputs,
        qk_weight,
        value_weight,
        output_gate_weight,
        rate_weight.T,
        out_weight,
        states,
        prefilled,
    )
    return produced.reshape(STEPS, ROWS, PIECE)


def solution(mesh):
    return jax.shard_map(
        on_device,
        mesh=mesh,
        in_specs=(
            P(None, "dp", None),
            P(None, "value"),
            P(None, "value"),
            P(None, "value"),
            P(),
            P(),
            P(),
            P("value"),
            P("value", None),
            P("dp", "value", None, None),
            P("dp", "value", None, None),
            P(),
            P(),
            P(),
        ),
        out_specs=P(None, "dp", "value"),
        check_vma=False,
    )
```

```python
import functools

import jax
import jax.numpy as jnp
from jax import lax
from jax.experimental import pallas as pl
from jax.experimental.pallas import tpu as pltpu
from jax.sharding import PartitionSpec as P

F32 = jnp.float32
BF16 = jnp.bfloat16
MESH = pl.DeviceIdType.MESH

STEPS = 4
REPLACED = 2
N_DP = 16
N_VALUE = 8
N_X = 4
ROWS = 32
H = 32
DK = 128
DV = 128
WIDTH = 2048
COLS = 512
PIECE = 256
BLOCKS = ROWS + N_DP
HEADS = 4
TILE = HEADS * STEPS
GROUPS = COLS // 128
ALL = STEPS * ROWS

PAIRS = [(s, t) for t in range(STEPS) for s in range(t + 1)]
VALUES, GATING = 0, GROUPS * ALL
RETAIN = 2 * GROUPS * ALL
STRENGTH, INV_K, INV_Q = RETAIN + ALL, RETAIN + 2 * ALL, RETAIN + 3 * ALL
KEY_KEY = RETAIN + 4 * ALL
KEY_QUERY = KEY_KEY + len(PAIRS) * ROWS
QUANTITIES = KEY_QUERY // ROWS + len(PAIRS)

FIRST, LAST = 0, 1
BASE = (0, 16)
CHUNK = 16
SLOT_ROWS = STEPS * STEPS * REPLACED
SUMMED = (STEPS * CHUNK, STEPS * CHUNK + SLOT_ROWS)
UNROLL = 8


def ring(k):
    return min(k, N_X - k)


PLANE = sorted(((a, b) for a in range(N_X) for b in range(N_X)), key=lambda o: -ring(o[0]) - ring(o[1]))
SPACE = sorted(((i, j) for i in range(N_DP) for j in range(N_X)), key=lambda o: -sum(map(ring, (*PLANE[o[0]], o[1]))))


def iota(shape, dim):
    return lax.broadcasted_iota(jnp.int32, shape, dim)


def dot(a, b, **kw):
    return jnp.dot(a, b, preferred_element_type=F32, **kw)


def dot_t(a, b):
    return lax.dot_general(a, b, (((1,), (1,)), ((), ())), preferred_element_type=F32)


def kernel(
    fin_hbm,
    own_hbm,
    slot_hbm,
    logd_hbm,
    bias_hbm,
    gain_hbm,
    x_hbm,
    wqk_hbm,
    wv_hbm,
    wg_hbm,
    wr_hbm,
    wo_hbm,
    st_hbm,
    pf_hbm,
    out_ref,
    fin_ref,
    own_ref,
    slot_ref,
    logd_ref,
    bias_ref,
    gain_ref,
    x_v,
    wqk_v,
    wv_v,
    wg_v,
    wr_v,
    wo_v,
    st_v,
    pf_v,
    zf,
    snd_f,
    gbuf,
    msc,
    rsnd,
    rrcv,
    rf,
    rowq,
    slotq,
    gat_s,
    sqbuf,
    ssqbuf,
    r1_snd,
    r1_rcv,
    part,
    r2_snd,
    r2_rcv,
    loc,
    ag_s,
    ag_r,
    fs,
    fr,
    fps,
    fpr,
    bs,
    br,
    qs,
    qr,
    r1s,
    r1r,
    r2s,
    r2r,
    sqs,
    sqr,
):
    me_d = lax.axis_index("dp")
    me_v = lax.axis_index("value")
    x = me_v // 2
    c = me_v % 2

    def vid(xx, cc):
        return xx * 2 + cc

    partner = vid(x, 1 - c)

    def peer(i):
        dz, dy = PLANE[i]
        return ((me_d // N_X + dz) % N_X) * N_X + (me_d % N_X + dy) % N_X

    def load(src, dst, k):
        cp = pltpu.make_async_copy(src, dst, loc.at[k])
        cp.start()
        return cp

    l_x = load(x_hbm, x_v, 0)
    l_qk = load(wqk_hbm, wqk_v, 1)
    scalars = (
        (fin_hbm, fin_ref),
        (own_hbm, own_ref),
        (slot_hbm, slot_ref),
        (logd_hbm, logd_ref),
        (bias_hbm, bias_ref),
        (gain_hbm, gain_ref),
    )
    l_scalars = [load(src, dst, 9 + k) for k, (src, dst) in enumerate(scalars)]

    barrier = pltpu.get_barrier_semaphore()
    greeted = 0
    for i, j in SPACE:
        if PLANE[i] != (0, 0) or j:
            to = (peer(i), vid((x + j) % N_X, c))
            pl.semaphore_signal(barrier, inc=1, device_id=to, device_id_type=MESH)
            greeted += 1
    for j in range(N_X):
        to = (me_d, vid((x + j) % N_X, 1 - c))
        pl.semaphore_signal(barrier, inc=1, device_id=to, device_id_type=MESH)
        greeted += 1

    l_r = load(wr_hbm, wr_v, 2)
    l_v = load(wv_hbm, wv_v, 3)
    l_g = load(wg_hbm, wg_v, 4)
    l_p = load(pf_hbm, pf_v, 5)
    l_s = load(st_hbm, st_v, 6)
    l_o = load(wo_hbm, wo_v, 8)

    for copy in l_scalars:
        copy.wait()
    pick = jnp.zeros((N_DP, ROWS), F32)
    for t in range(STEPS):
        for j in range(REPLACED):
            hit = (iota((N_DP, ROWS), 0) == own_ref[t, j, me_d]) & (iota((N_DP, ROWS), 1) == fin_ref[t, j, me_d])
            pick = jnp.where(hit, 1.0, pick)
    pick = pick.astype(BF16)

    l_x.wait()
    l_qk.wait()
    xin = x_v[...].reshape(STEPS * ROWS, WIDTH)
    joined = dot(xin, wqk_v[...]).astype(BF16)
    joined_f = joined.astype(F32)
    for t in range(STEPS):
        chosen = dot(pick, joined[t * ROWS : (t + 1) * ROWS])
        for h in range(HEADS):
            at = (h * STEPS + t) * BLOCKS
            zf[at : at + ROWS] = joined_f[t * ROWS : (t + 1) * ROWS, h * 128 : (h + 1) * 128]
            zf[at + ROWS : at + BLOCKS] = chosen[:, h * 128 : (h + 1) * 128]

    def block_of(r):
        return zf[pl.ds(r, TILE, stride=BLOCKS), :].astype(BF16)

    for o in range(N_DP):
        snd_f[o] = block_of(ROWS + o)
    pl.semaphore_wait(barrier, greeted)

    def foreign(i, j):
        dst = peer(i)
        return pltpu.make_async_remote_copy(
            src_ref=snd_f.at[dst],
            dst_ref=gbuf.at[me_v, ROWS + me_d],
            send_sem=fs.at[j],
            recv_sem=fr.at[j],
            device_id=(dst, vid((x + j) % N_X, c)),
            device_id_type=MESH,
        )

    def foreign_all(j):
        slot = vid((x + N_X - j) % N_X, c)
        first = 1 if j == 0 else 0
        rows = pl.ds(ROWS, N_DP - first)
        return pltpu.make_async_remote_copy(
            src_ref=gbuf.at[slot, rows],
            dst_ref=gbuf.at[slot, rows],
            send_sem=fs.at[j],
            recv_sem=fr.at[j],
            device_id=(me_d, partner),
            device_id_type=MESH,
        )

    def foreign_forward(j):
        slot = vid((x + N_X - j) % N_X, c)
        rows = pl.ds(ROWS, N_DP)
        return pltpu.make_async_remote_copy(
            src_ref=gbuf.at[slot, rows],
            dst_ref=gbuf.at[slot, rows],
            send_sem=fps.at[j],
            recv_sem=fpr.at[j],
            device_id=(me_d, partner),
            device_id_type=MESH,
        )

    def foreign_forwarded(j):
        slot = vid((x + N_X - j) % N_X, 1 - c)
        rows = pl.ds(ROWS, N_DP)
        pltpu.make_async_remote_copy(
            src_ref=gbuf.at[slot, rows],
            dst_ref=gbuf.at[slot, rows],
            send_sem=fps.at[j],
            recv_sem=fpr.at[j],
            device_id=(me_d, partner),
            device_id_type=MESH,
        ).wait_recv()

    for i, j in SPACE:
        if PLANE[i] != (0, 0) or j:
            foreign(i, j).start()
    gbuf[me_v, ROWS + me_d] = snd_f[me_d]
    for r in range(CHUNK):
        gbuf[me_v, r] = block_of(r)

    def gather(chunk, k, slot, to):
        rows = pl.ds(BASE[chunk], CHUNK)
        return pltpu.make_async_remote_copy(
            src_ref=gbuf.at[slot, rows],
            dst_ref=gbuf.at[slot, rows],
            send_sem=ag_s.at[chunk, k],
            recv_sem=ag_r.at[chunk, k],
            device_id=(me_d, to),
            device_id_type=MESH,
        )

    def along(chunk, j):
        return gather(chunk, j, me_v, vid((x + j) % N_X, c) if j else partner)

    def arrived(chunk, j):
        gather(chunk, j, vid((x + N_X - j) % N_X, c) if j else partner, partner).wait_recv()

    def forward(chunk, j):
        return gather(chunk, N_X - 1 + j, vid((x + N_X - j) % N_X, c), partner)

    def forwarded(chunk, j):
        gather(chunk, N_X - 1 + j, vid((x + N_X - j) % N_X, 1 - c), partner).wait_recv()

    def send_own(chunk):
        for j in (2, 1, 3, 0):
            along(chunk, j).start()

    def pass_on(chunk):
        for j in (1, 3, 2):
            arrived(chunk, j)
            forward(chunk, j).start()

    def all_here(chunk):
        arrived(chunk, 0)
        for j in (1, 3, 2):
            forwarded(chunk, j)

    send_own(FIRST)
    for r in range(CHUNK, 2 * CHUNK):
        gbuf[me_v, r] = block_of(r)
    send_own(LAST)

    seg = iota((1, 128), 1) // H
    in_seg = iota((1, 128), 1) % H
    l_r.wait()
    rates = dot_t(xin, wr_v[...])
    decay = jnp.zeros((1, 128), F32)
    bias = jnp.zeros((1, 128), F32)
    for h in range(H):
        decay = jnp.where(in_seg == h, logd_ref[h], decay)
        bias = jnp.where(in_seg == h, bias_ref[h], bias)
    wide = jnp.concatenate([rates, rates], axis=1)
    turned = pltpu.roll(wide, H, 1)
    odd = seg % 2 == 1
    rowq[RETAIN : RETAIN + ALL] = jnp.exp(-jnp.exp(decay) * jax.nn.softplus(jnp.where(odd, wide, turned) + bias))
    rowq[STRENGTH : STRENGTH + ALL] = jax.nn.sigmoid(jnp.where(odd, turned, wide))
    l_v.wait()
    values = dot(xin, wv_v[...])
    for g in range(GROUPS):
        rowq[VALUES + g * ALL : VALUES + (g + 1) * ALL] = values[:, g * 128 : (g + 1) * 128]
    l_g.wait()
    gating = dot(xin, wg_v[...])
    for g in range(GROUPS):
        rowq[GATING + g * ALL : GATING + (g + 1) * ALL] = gating[:, g * 128 : (g + 1) * 128]
    chosen_slots = []
    for d in range(N_DP):
        slot = jnp.int32(0)
        for t in range(STEPS):
            for j in range(REPLACED):
                slot = jnp.where(own_ref[t, j, d] == me_d, slot_ref[t, j, d], slot)
        chosen_slots.append(slot)
    for j in (0, 1, 3, 2):
        foreign_all(j).wait_recv()
        foreign_forward(j).start()

    lane = iota((8, 128), 1)
    sub = iota((8, 128), 0)
    state_masks = [(lane % H) // 2 == 2 * i + sub // 4 for i in range(8)]
    gram_masks = [(lane % 64) // 4 == 2 * i + sub // 4 for i in range(8)]

    def diagonal(full, masks):
        sums = []
        for kind in range(2):
            acc = jnp.zeros((8, 128), F32)
            for i in range(8):
                at = kind * 64 + i * 8
                acc = jnp.where(masks[i], full[at : at + 8], acc)
            sums.append(acc + pltpu.roll(acc, 4, 0))
        return jnp.where(sub < 4, sums[0], sums[1])

    def contract(qk, state):
        full = dot_t(qk, state.reshape(COLS, DK).astype(BF16))
        return [diagonal(full[:, g * 128 : (g + 1) * 128], state_masks) for g in range(GROUPS)]

    def own_rows(first, count):
        def one(r):
            qk = gbuf[:, r].reshape(N_VALUE * TILE, DK)
            at = pl.multiple_of(r * 8, 8)
            for g, block in enumerate(contract(qk, st_v[r])):
                msc[g, pl.ds(at, 8)] = block
            msc[GROUPS, pl.ds(at, 8)] = diagonal(dot_t(qk, qk), gram_masks)

        def some(i, _):
            for k in range(UNROLL):
                one(first + UNROLL * i + k)
            return 0

        lax.fori_loop(0, count // UNROLL, some, 0)

    def foreign_rows():
        for d in range(N_DP):
            qk = gbuf[:, ROWS + d].reshape(N_VALUE * TILE, DK)
            blocks = contract(qk, pf_v[chosen_slots[d]])
            rsnd[d] = jnp.concatenate(blocks, axis=0).astype(BF16)

    def back(i):
        dst = peer(i)
        return pltpu.make_async_remote_copy(
            src_ref=rsnd.at[dst],
            dst_ref=rrcv.at[me_d],
            send_sem=bs.at[i],
            recv_sem=br.at[i],
            device_id=(dst, me_v),
            device_id_type=MESH,
        )

    l_p.wait()
    for j in (0, 1, 3, 2):
        foreign_forwarded(j)
    foreign_rows()
    for i in range(N_DP):
        if PLANE[i] != (0, 0):
            back(i).start()
    rrcv[me_d] = rsnd[me_d]

    def row_get(chunk):
        def get(at):
            return rowq[at + BASE[chunk] : at + BASE[chunk] + CHUNK]

        return get

    src = iota((DK, 128), 0)
    head = (iota((DK, 128), 1) % H) // 2
    spread = [src == 64 + head * 4 + s for s in range(STEPS)] + [src == head * 4 + t for t in range(STEPS)]
    spread = jnp.concatenate([entry.astype(F32) for entry in spread], axis=1).astype(BF16)

    def contractions(chunk):
        def part_of(g, k):
            return msc[g, pl.ds(BASE[chunk] * 8 + k, CHUNK, stride=8), :]

        all_here(chunk)
        own_rows(BASE[chunk], CHUNK)
        gram = [part_of(GROUPS, k) for k in range(2 * STEPS)]
        gram = jnp.concatenate(gram, axis=0)
        high = gram.astype(BF16)
        low = (gram - high.astype(F32)).astype(BF16)
        copied = dot(jnp.concatenate([high, low], axis=0), spread)
        copied = copied[: 2 * STEPS * CHUNK] + copied[2 * STEPS * CHUNK :]

        def entry(k, s):
            return copied[k * CHUNK : (k + 1) * CHUNK, s * 128 : (s + 1) * 128]

        def put(at, what):
            rowq[at + BASE[chunk] : at + BASE[chunk] + CHUNK] = what

        inv_k, inv_q = [], []
        for t in range(STEPS):
            inv_k.append(lax.rsqrt(entry(STEPS + t, t) + 1e-06))
            inv_q.append(lax.rsqrt(entry(t, STEPS + t) + 1e-06) * DK ** (-0.5))
            put(INV_K + t * ROWS, inv_k[t])
            put(INV_Q + t * ROWS, inv_q[t])
        for s, t in PAIRS:
            at = PAIRS.index((s, t)) * ROWS
            if s < t:
                put(KEY_KEY + at, entry(STEPS + t, s) * (inv_k[s] * inv_k[t]))
            put(KEY_QUERY + at, entry(t, s) * (inv_k[s] * inv_q[t]))
        return part_of

    def recurrence(get, contracted, fresh):
        readouts = [[None] * GROUPS for _ in range(STEPS)]
        squares = [None] * STEPS
        for g in range(GROUPS):
            written = []
            kept = None
            for t in range(STEPS):
                a, b = get(RETAIN + t * ROWS), get(STRENGTH + t * ROWS)
                kept = a if kept is None else kept * a
                written = [w * a for w in written]
                if fresh is not None:
                    kept = jnp.where(fresh[t], a, kept)
                    written = [jnp.where(fresh[t], 0.0, w) for w in written]
                memory = kept * contracted(g, STEPS + t) * get(INV_K + t * ROWS)
                readout = kept * contracted(g, t) * get(INV_Q + t * ROWS)
                for s, w in enumerate(written):
                    at = PAIRS.index((s, t)) * ROWS
                    memory = memory + w * get(KEY_KEY + at)
                    readout = readout + w * get(KEY_QUERY + at)
                update = (get(VALUES + g * ALL + t * ROWS) - memory) * b
                readout = readout + update * get(KEY_QUERY + PAIRS.index((t, t)) * ROWS)
                written.append(update)
                readouts[t][g] = readout
                square = readout * readout
                squares[t] = square if g == 0 else squares[t] + square
        packed = jnp.zeros_like(squares[0])
        for t in range(STEPS):
            total = squares[t] + pltpu.roll(squares[t], 64, 1)
            total = total + pltpu.roll(total, 32, 1)
            packed = jnp.where(seg == t, total, packed)
        return readouts, packed

    def silu_gain(readouts, get):
        for g in range(GROUPS):
            gain = jnp.zeros((1, 128), F32)
            for e in range(4):
                gain = jnp.where(seg == e, gain_ref[g * 4 + e], gain)
            for t in range(STEPS):
                gate = get(GATING + g * ALL + t * ROWS)
                readouts[t][g] = readouts[t][g] * gain * (gate * jax.nn.sigmoid(gate))

    def scalings(summed):
        out = []
        for t in range(STEPS):
            total = jnp.where(seg == t, summed, 0.0)
            total = total + pltpu.roll(total, 64, 1)
            total = total + pltpu.roll(total, 32, 1)
            out.append(lax.rsqrt(total * (1.0 / DV) + 1e-06))
        return out

    def exchange(place, s_sem, r_sem):
        def one(i, slot):
            return pltpu.make_async_remote_copy(
                src_ref=place(slot),
                dst_ref=place(slot),
                send_sem=s_sem(i),
                recv_sem=r_sem(i),
                device_id=(me_d, (me_v + i) % N_VALUE),
                device_id_type=MESH,
            )

        sends = [one(i, me_v) for i in range(1, N_VALUE)]
        arrivals = [one(i, (me_v + N_VALUE - i) % N_VALUE) for i in range(1, N_VALUE)]
        return sends, arrivals

    def first_half(chunk):
        part_of = contractions(chunk)
        readouts, packed = recurrence(row_get(chunk), part_of, None)
        sqbuf[chunk, me_v] = packed.astype(BF16)
        sends, arrivals = exchange(
            lambda slot: sqbuf.at[chunk, slot], lambda i: qs.at[chunk, i], lambda i: qr.at[chunk, i]
        )
        for copy in sends:
            copy.start()
        return readouts, sends, arrivals

    def scaled(chunk, readouts, arrivals):
        for copy in arrivals:
            copy.wait_recv()
        scales = scalings(jnp.sum(sqbuf[chunk].astype(F32), axis=0))
        for t in range(STEPS):
            for g in range(GROUPS):
                rows = slice(t * CHUNK, (t + 1) * CHUNK)
                gat_s[chunk, rows, g * 128 : (g + 1) * 128] = (readouts[t][g] * scales[t]).astype(BF16)

    order = [(x + j) % N_X for j in (2, 1, 3, 0)]

    def project(what, to):
        at = pl.multiple_of(to * PIECE, PIECE)
        return dot(what, wo_v[:, pl.ds(at, PIECE)])

    def first_copy(chunk, k):
        return pltpu.make_async_remote_copy(
            src_ref=r1_snd.at[chunk, k, pl.ds(0, SUMMED[chunk])],
            dst_ref=r1_rcv.at[chunk, k, pl.ds(0, SUMMED[chunk])],
            send_sem=r1s.at[chunk, k],
            recv_sem=r1r.at[chunk, k],
            device_id=(me_d, partner),
            device_id_type=MESH,
        )

    def second_copy(chunk, k):
        return pltpu.make_async_remote_copy(
            src_ref=r2_snd.at[chunk, k, pl.ds(0, SUMMED[chunk])],
            dst_ref=r2_rcv.at[chunk, k, pl.ds(0, SUMMED[chunk])],
            send_sem=r2s.at[chunk, k],
            recv_sem=r2r.at[chunk, k],
            device_id=(me_d, vid(order[k], c)),
            device_id_type=MESH,
        )

    def sum_over_cores(chunk):
        n = SUMMED[chunk]
        gated = gat_s[chunk, :n]
        for k in range(N_X):
            r1_snd[chunk, k, :n] = project(gated, vid(order[k], 1 - c)).astype(BF16)
            first_copy(chunk, k).start()
        for k in range(N_X):
            part[chunk, k, :n] = project(gated, vid(order[k], c))

    def sum_along_x(chunk):
        n = SUMMED[chunk]
        for k in range(N_X - 1):
            first_copy(chunk, k).wait_recv()
            r2_snd[chunk, k, :n] = (part[chunk, k, :n] + r1_rcv[chunk, k, :n].astype(F32)).astype(BF16)
            second_copy(chunk, k).start()

    def summed(chunk):
        n = SUMMED[chunk]
        first_copy(chunk, 3).wait_recv()
        total = part[chunk, 3, :n] + r1_rcv[chunk, 3, :n].astype(F32)
        for k in (1, 2, 0):
            second_copy(chunk, k).wait_recv()
            total = total + r2_rcv[chunk, k, :n].astype(F32)
        return total

    l_s.wait()
    pass_on(FIRST)
    pass_on(LAST)
    readouts_a, sq_sends_a, sq_arrivals_a = first_half(FIRST)
    silu_gain(readouts_a, row_get(FIRST))
    readouts_b, sq_sends_b, sq_arrivals_b = first_half(LAST)
    slots = [(t, j) for t in range(STEPS) for j in range(REPLACED)]
    for k, (t, j) in enumerate(slots):
        slotq[k * QUANTITIES : (k + 1) * QUANTITIES] = rowq[pl.ds(fin_ref[t, j, me_d], QUANTITIES, stride=ROWS), :]

    def slot_get(at):
        return slotq[pl.ds(at // ROWS, len(slots), stride=QUANTITIES), :]

    slot_of = jnp.full((ALL, 128), -1, jnp.int32)
    take_of = jnp.full((ALL, len(slots) * STEPS), -1, jnp.int32)
    for k, (t, j) in enumerate(slots):
        done = fin_ref[t, j, me_d]
        wide_row, thin_row = iota(slot_of.shape, 0), iota(take_of.shape, 0)
        slot_of = jnp.where((wide_row % ROWS == done) & (wide_row // ROWS >= t), k, slot_of)
        take_of = jnp.where((thin_row % ROWS == done) & (thin_row // ROWS >= t), k, take_of)
    column = iota(take_of.shape, 1)
    same_step = column // len(slots) == iota(take_of.shape, 0) // ROWS
    take = ((take_of == column % len(slots)) & same_step).astype(BF16)

    for i in range(N_DP):
        if PLANE[i] != (0, 0):
            back(i).wait_recv()
    for k, (t, j) in enumerate(slots):
        rf[k * GROUPS * 8 : (k + 1) * GROUPS * 8] = rrcv[own_ref[t, j, me_d]].astype(F32)
    slot_row = iota((len(slots), 128), 0)
    slot_readouts, slot_packed = recurrence(
        slot_get,
        lambda g, k: rf[pl.ds(g * 8 + k, len(slots), stride=GROUPS * 8), :],
        [slot_row // REPLACED == t for t in range(STEPS)],
    )
    ssqbuf[me_v] = slot_packed
    ssq_sends, ssq_arrivals = exchange(lambda slot: ssqbuf.at[slot], lambda i: sqs.at[i], lambda i: sqr.at[i])
    for copy in ssq_sends:
        copy.start()
    l_o.wait()
    scaled(FIRST, readouts_a, sq_arrivals_a)
    sum_over_cores(FIRST)
    silu_gain(readouts_b, row_get(LAST))
    silu_gain(slot_readouts, slot_get)
    sum_along_x(FIRST)
    scaled(LAST, readouts_b, sq_arrivals_b)

    for copy in ssq_arrivals:
        copy.wait_recv()
    slot_scales = scalings(jnp.sum(ssqbuf[...], axis=0))
    gat_s[LAST, SUMMED[FIRST] : SUMMED[LAST]] = jnp.concatenate(
        [
            jnp.concatenate([slot_readouts[t][g] * slot_scales[t] for g in range(GROUPS)], axis=1)
            for t in range(STEPS)
        ],
        axis=0,
    ).astype(BF16)

    sum_over_cores(LAST)
    sum_along_x(LAST)

    totals = [summed(FIRST), summed(LAST)]
    chosen = dot(take, totals[LAST][SUMMED[FIRST] :].astype(BF16))
    for half in range(PIECE // 128):
        lanes = slice(half * 128, (half + 1) * 128)
        for chunk, total in enumerate(totals):
            for t in range(STEPS):
                rows = slice(t * ROWS + BASE[chunk], t * ROWS + BASE[chunk] + CHUNK)
                own = total[t * CHUNK : (t + 1) * CHUNK, lanes]
                out_ref[rows, lanes] = jnp.where(slot_of[rows] >= 0, chosen[rows, lanes], own).astype(BF16)

    for j in range(N_X):
        foreign_all(j).wait_send()
        foreign_forward(j).wait_send()
    for i in range(N_DP):
        if PLANE[i] != (0, 0):
            back(i).wait_send()
    for chunk in range(2):
        for j in range(N_X):
            along(chunk, j).wait_send()
        for j in range(1, N_X):
            forward(chunk, j).wait_send()
        for k in range(N_X):
            first_copy(chunk, k).wait_send()
        for k in range(N_X - 1):
            second_copy(chunk, k).wait_send()
    for copy in sq_sends_a + sq_sends_b + ssq_sends:
        copy.wait_send()


def on_device(
    inputs,
    qk_weight,
    value_weight,
    output_gate_weight,
    rate_weight,
    log_decay,
    decay_bias,
    norm_gain,
    out_weight,
    states,
    prefilled,
    finished,
    new_owner,
    new_slot,
):
    hbm = pl.BlockSpec(memory_space=pl.ANY)
    dma = pltpu.SemaphoreType.DMA
    produced = pl.pallas_call(
        kernel,
        out_shape=jax.ShapeDtypeStruct((STEPS * ROWS, PIECE), BF16),
        in_specs=[hbm] * 14,
        out_specs=pl.BlockSpec(memory_space=pltpu.VMEM),
        scratch_shapes=[
            pltpu.SMEM((STEPS, REPLACED, N_DP), jnp.int32),
            pltpu.SMEM((STEPS, REPLACED, N_DP), jnp.int32),
            pltpu.SMEM((STEPS, REPLACED, N_DP), jnp.int32),
            pltpu.SMEM((H,), F32),
            pltpu.SMEM((H,), F32),
            pltpu.SMEM((DV // N_VALUE,), F32),
            pltpu.VMEM((STEPS, ROWS, WIDTH), BF16),
            pltpu.VMEM((WIDTH, COLS), BF16),
            pltpu.VMEM((WIDTH, COLS), BF16),
            pltpu.VMEM((WIDTH, COLS), BF16),
            pltpu.VMEM((2 * H, WIDTH), BF16),
            pltpu.VMEM((COLS, WIDTH), BF16),
            pltpu.VMEM((ROWS, 16, H, DK), F32),
            pltpu.VMEM((16, 16, H, DK), F32),
            pltpu.VMEM((TILE * BLOCKS, DK), F32),
            pltpu.VMEM((N_DP, TILE, DK), BF16),
            pltpu.VMEM((N_VALUE, BLOCKS, TILE, DK), BF16),
            pltpu.VMEM((GROUPS + 1, ROWS * 8, 128), F32),
            pltpu.VMEM((N_DP, GROUPS * 8, 128), BF16),
            pltpu.VMEM((N_DP, GROUPS * 8, 128), BF16),
            pltpu.VMEM((STEPS * REPLACED * GROUPS * 8, 128), F32),
            pltpu.VMEM((QUANTITIES * ROWS, 128), F32),
            pltpu.VMEM((STEPS * REPLACED * QUANTITIES, 128), F32),
            pltpu.VMEM((2, SUMMED[LAST], COLS), BF16),
            pltpu.VMEM((2, N_VALUE, CHUNK, 128), BF16),
            pltpu.VMEM((N_VALUE, STEPS * REPLACED, 128), F32),
            pltpu.VMEM((2, N_X, SUMMED[LAST], PIECE), BF16),
            pltpu.VMEM((2, N_X, SUMMED[LAST], PIECE), BF16),
            pltpu.VMEM((2, N_X, SUMMED[LAST], PIECE), F32),
            pltpu.VMEM((2, N_X - 1, SUMMED[LAST], PIECE), BF16),
            pltpu.VMEM((2, N_X - 1, SUMMED[LAST], PIECE), BF16),
            dma((15,)),
            dma((2, 2 * N_X - 1)),
            dma((2, 2 * N_X - 1)),
            dma((N_X,)),
            dma((N_X,)),
            dma((N_X,)),
            dma((N_X,)),
            dma((N_DP,)),
            dma((N_DP,)),
            dma((2, N_VALUE)),
            dma((2, N_VALUE)),
            dma((2, N_X)),
            dma((2, N_X)),
            dma((2, N_X - 1)),
            dma((2, N_X - 1)),
            dma((N_VALUE,)),
            dma((N_VALUE,)),
        ],
        compiler_params=pltpu.CompilerParams(
            collective_id=0, has_side_effects=True, vmem_limit_bytes=56 * 2**20
        ),
        name="delta_steps",
    )(
        finished.transpose(0, 2, 1),
        new_owner.transpose(0, 2, 1),
        new_slot.transpose(0, 2, 1),
        log_decay,
        decay_bias,
        norm_gain,
        inputs,
        qk_weight,
        value_weight,
        output_gate_weight,
        rate_weight.T,
        out_weight,
        states,
        prefilled,
    )
    return produced.reshape(STEPS, ROWS, PIECE)


def solution(mesh):
    return jax.shard_map(
        on_device,
        mesh=mesh,
        in_specs=(
            P(None, "dp", None),
            P(None, "value"),
            P(None, "value"),
            P(None, "value"),
            P(),
            P(),
            P(),
            P("value"),
            P("value", None),
            P("dp", "value", None, None),
            P("dp", "value", None, None),
            P(),
            P(),
            P(),
        ),
        out_specs=P(None, "dp", "value"),
        check_vma=False,
    )
```

```python
import functools

import jax
import jax.numpy as jnp
from jax import lax
from jax.experimental import pallas as pl
from jax.experimental.pallas import tpu as pltpu
from jax.sharding import PartitionSpec as P

F32 = jnp.float32
BF16 = jnp.bfloat16
MESH = pl.DeviceIdType.MESH

STEPS = 4
REPLACED = 2
N_DP = 16
N_VALUE = 8
N_X = 4
ROWS = 32
H = 32
DK = 128
DV = 128
WIDTH = 2048
COLS = 512
PIECE = 256
BLOCKS = ROWS + N_DP
HEADS = 4
TILE = HEADS * STEPS
GROUPS = COLS // 128
ALL = STEPS * ROWS

PAIRS = [(s, t) for t in range(STEPS) for s in range(t + 1)]
VALUES, GATING = 0, GROUPS * ALL
RETAIN = 2 * GROUPS * ALL
STRENGTH, INV_K, INV_Q = RETAIN + ALL, RETAIN + 2 * ALL, RETAIN + 3 * ALL
KEY_KEY = RETAIN + 4 * ALL
KEY_QUERY = KEY_KEY + len(PAIRS) * ROWS
QUANTITIES = KEY_QUERY // ROWS + len(PAIRS)

FIRST, LAST = 0, 1
BASE = (0, 16)
CHUNK = 16
SLOT_ROWS = STEPS * STEPS * REPLACED
SUMMED = (STEPS * CHUNK, STEPS * CHUNK + SLOT_ROWS)
QK_PIECES = 4
UNROLL = 16


def ring(k):
    return min(k, N_X - k)


PLANE = sorted(((a, b) for a in range(N_X) for b in range(N_X)), key=lambda o: -ring(o[0]) - ring(o[1]))
SPACE = sorted(((i, j) for i in range(N_DP) for j in range(N_X)), key=lambda o: -sum(map(ring, (*PLANE[o[0]], o[1]))))


def iota(shape, dim):
    return lax.broadcasted_iota(jnp.int32, shape, dim)


def dot(a, b, **kw):
    return jnp.dot(a, b, preferred_element_type=F32, **kw)


def dot_t(a, b):
    return lax.dot_general(a, b, (((1,), (1,)), ((), ())), preferred_element_type=F32)


def kernel(
    fin_hbm,
    own_hbm,
    slot_hbm,
    logd_hbm,
    bias_hbm,
    gain_hbm,
    x_hbm,
    wqk_hbm,
    wv_hbm,
    wg_hbm,
    wr_hbm,
    wo_hbm,
    st_hbm,
    pf_hbm,
    out_ref,
    fin_ref,
    own_ref,
    slot_ref,
    logd_ref,
    bias_ref,
    gain_ref,
    x_v,
    wqk_v,
    wv_v,
    wg_v,
    wr_v,
    wo_v,
    st_v,
    pf_v,
    zf,
    snd_f,
    gbuf,
    msc,
    rsnd,
    rrcv,
    rf,
    rowq,
    slotq,
    gat_s,
    sqbuf,
    ssqbuf,
    r1_snd,
    r1_rcv,
    part,
    r2_snd,
    r2_rcv,
    loc,
    ag_s,
    ag_r,
    fs,
    fr,
    fps,
    fpr,
    bs,
    br,
    qs,
    qr,
    r1s,
    r1r,
    r2s,
    r2r,
    sqs,
    sqr,
):
    me_d = lax.axis_index("dp")
    me_v = lax.axis_index("value")
    x = me_v // 2
    c = me_v % 2

    def vid(xx, cc):
        return xx * 2 + cc

    partner = vid(x, 1 - c)

    def peer(i):
        dz, dy = PLANE[i]
        return ((me_d // N_X + dz) % N_X) * N_X + (me_d % N_X + dy) % N_X

    def load(src, dst, k):
        cp = pltpu.make_async_copy(src, dst, loc.at[k])
        cp.start()
        return cp

    scalars = (
        (fin_hbm, fin_ref),
        (own_hbm, own_ref),
        (slot_hbm, slot_ref),
        (logd_hbm, logd_ref),
        (bias_hbm, bias_ref),
        (gain_hbm, gain_ref),
    )
    l_scalars = [load(src, dst, 9 + k) for k, (src, dst) in enumerate(scalars)]
    l_x = load(x_hbm, x_v, 0)
    pieces = [pl.ds(k * (WIDTH // QK_PIECES), WIDTH // QK_PIECES) for k in range(QK_PIECES)]
    l_qk = [load(wqk_hbm.at[piece], wqk_v.at[piece], 15 + k) for k, piece in enumerate(pieces)]

    barrier = pltpu.get_barrier_semaphore()
    greeted = 0
    for i, j in SPACE:
        if PLANE[i] != (0, 0) or j:
            to = (peer(i), vid((x + j) % N_X, c))
            pl.semaphore_signal(barrier, inc=1, device_id=to, device_id_type=MESH)
            greeted += 1
    for j in range(N_X):
        to = (me_d, vid((x + j) % N_X, 1 - c))
        pl.semaphore_signal(barrier, inc=1, device_id=to, device_id_type=MESH)
        greeted += 1

    l_r = load(wr_hbm, wr_v, 2)
    l_v = load(wv_hbm, wv_v, 3)
    l_g = load(wg_hbm, wg_v, 4)
    l_p = load(pf_hbm, pf_v, 5)
    l_s = load(st_hbm, st_v, 6)
    l_o = load(wo_hbm, wo_v, 8)

    for copy in l_scalars:
        copy.wait()
    pick = jnp.zeros((N_DP, ROWS), F32)
    for t in range(STEPS):
        for j in range(REPLACED):
            hit = (iota((N_DP, ROWS), 0) == own_ref[t, j, me_d]) & (iota((N_DP, ROWS), 1) == fin_ref[t, j, me_d])
            pick = jnp.where(hit, 1.0, pick)
    pick = pick.astype(BF16)

    l_x.wait()
    xin = x_v[...].reshape(STEPS * ROWS, WIDTH)
    joined = jnp.zeros((ALL, COLS), F32)
    for k, piece in enumerate(pieces):
        l_qk[k].wait()
        deep = slice(k * (WIDTH // QK_PIECES), (k + 1) * (WIDTH // QK_PIECES))
        joined = joined + dot(xin[:, deep], wqk_v[piece])
    joined = joined.astype(BF16)
    joined_f = joined.astype(F32)
    for t in range(STEPS):
        chosen = dot(pick, joined[t * ROWS : (t + 1) * ROWS])
        for h in range(HEADS):
            at = (h * STEPS + t) * BLOCKS
            zf[at : at + ROWS] = joined_f[t * ROWS : (t + 1) * ROWS, h * 128 : (h + 1) * 128]
            zf[at + ROWS : at + BLOCKS] = chosen[:, h * 128 : (h + 1) * 128]

    def block_of(r):
        return zf[pl.ds(r, TILE, stride=BLOCKS), :].astype(BF16)

    for o in range(N_DP):
        snd_f[o] = block_of(ROWS + o)
    pl.semaphore_wait(barrier, greeted)

    def foreign(i, j):
        dst = peer(i)
        return pltpu.make_async_remote_copy(
            src_ref=snd_f.at[dst],
            dst_ref=gbuf.at[me_v, ROWS + me_d],
            send_sem=fs.at[j],
            recv_sem=fr.at[j],
            device_id=(dst, vid((x + j) % N_X, c)),
            device_id_type=MESH,
        )

    def foreign_all(j):
        slot = vid((x + N_X - j) % N_X, c)
        first = 1 if j == 0 else 0
        rows = pl.ds(ROWS, N_DP - first)
        return pltpu.make_async_remote_copy(
            src_ref=gbuf.at[slot, rows],
            dst_ref=gbuf.at[slot, rows],
            send_sem=fs.at[j],
            recv_sem=fr.at[j],
            device_id=(me_d, partner),
            device_id_type=MESH,
        )

    def foreign_forward(j):
        slot = vid((x + N_X - j) % N_X, c)
        rows = pl.ds(ROWS, N_DP)
        return pltpu.make_async_remote_copy(
            src_ref=gbuf.at[slot, rows],
            dst_ref=gbuf.at[slot, rows],
            send_sem=fps.at[j],
            recv_sem=fpr.at[j],
            device_id=(me_d, partner),
            device_id_type=MESH,
        )

    def foreign_forwarded(j):
        slot = vid((x + N_X - j) % N_X, 1 - c)
        rows = pl.ds(ROWS, N_DP)
        pltpu.make_async_remote_copy(
            src_ref=gbuf.at[slot, rows],
            dst_ref=gbuf.at[slot, rows],
            send_sem=fps.at[j],
            recv_sem=fpr.at[j],
            device_id=(me_d, partner),
            device_id_type=MESH,
        ).wait_recv()

    for i, j in SPACE:
        if PLANE[i] != (0, 0) or j:
            foreign(i, j).start()
    gbuf[me_v, ROWS + me_d] = snd_f[me_d]
    for r in range(CHUNK):
        gbuf[me_v, r] = block_of(r)

    def gather(chunk, k, slot, to):
        rows = pl.ds(BASE[chunk], CHUNK)
        return pltpu.make_async_remote_copy(
            src_ref=gbuf.at[slot, rows],
            dst_ref=gbuf.at[slot, rows],
            send_sem=ag_s.at[chunk, k],
            recv_sem=ag_r.at[chunk, k],
            device_id=(me_d, to),
            device_id_type=MESH,
        )

    def along(chunk, j):
        return gather(chunk, j, me_v, vid((x + j) % N_X, c) if j else partner)

    def arrived(chunk, j):
        gather(chunk, j, vid((x + N_X - j) % N_X, c) if j else partner, partner).wait_recv()

    def forward(chunk, j):
        return gather(chunk, N_X - 1 + j, vid((x + N_X - j) % N_X, c), partner)

    def forwarded(chunk, j):
        gather(chunk, N_X - 1 + j, vid((x + N_X - j) % N_X, 1 - c), partner).wait_recv()

    def send_own(chunk):
        for j in (2, 1, 3, 0):
            along(chunk, j).start()

    def pass_on(chunk):
        for j in (1, 3, 2):
            arrived(chunk, j)
            forward(chunk, j).start()

    def all_here(chunk):
        arrived(chunk, 0)
        for j in (1, 3, 2):
            forwarded(chunk, j)

    send_own(FIRST)
    for r in range(CHUNK, 2 * CHUNK):
        gbuf[me_v, r] = block_of(r)
    send_own(LAST)

    seg = iota((1, 128), 1) // H
    in_seg = iota((1, 128), 1) % H
    l_r.wait()
    rates = dot_t(xin, wr_v[...])
    decay = jnp.zeros((1, 128), F32)
    bias = jnp.zeros((1, 128), F32)
    for h in range(H):
        decay = jnp.where(in_seg == h, logd_ref[h], decay)
        bias = jnp.where(in_seg == h, bias_ref[h], bias)
    wide = jnp.concatenate([rates, rates], axis=1)
    turned = pltpu.roll(wide, H, 1)
    odd = seg % 2 == 1
    rowq[RETAIN : RETAIN + ALL] = jnp.exp(-jnp.exp(decay) * jax.nn.softplus(jnp.where(odd, wide, turned) + bias))
    rowq[STRENGTH : STRENGTH + ALL] = jax.nn.sigmoid(jnp.where(odd, turned, wide))
    l_v.wait()
    values = dot(xin, wv_v[...])
    for g in range(GROUPS):
        rowq[VALUES + g * ALL : VALUES + (g + 1) * ALL] = values[:, g * 128 : (g + 1) * 128]
    l_g.wait()
    gating = dot(xin, wg_v[...])
    for g in range(GROUPS):
        rowq[GATING + g * ALL : GATING + (g + 1) * ALL] = gating[:, g * 128 : (g + 1) * 128]
    chosen_slots = []
    for d in range(N_DP):
        slot = jnp.int32(0)
        for t in range(STEPS):
            for j in range(REPLACED):
                slot = jnp.where(own_ref[t, j, d] == me_d, slot_ref[t, j, d], slot)
        chosen_slots.append(slot)
    for j in (0, 1, 3, 2):
        foreign_all(j).wait_recv()
        foreign_forward(j).start()

    lane = iota((8, 128), 1)
    sub = iota((8, 128), 0)
    state_masks = [(lane % H) // 2 == 2 * i + sub // 4 for i in range(8)]
    gram_masks = [(lane % 64) // 4 == 2 * i + sub // 4 for i in range(8)]

    def diagonal(full, masks):
        sums = []
        for kind in range(2):
            acc = jnp.zeros((8, 128), F32)
            for i in range(8):
                at = kind * 64 + i * 8
                acc = jnp.where(masks[i], full[at : at + 8], acc)
            sums.append(acc + pltpu.roll(acc, 4, 0))
        return jnp.where(sub < 4, sums[0], sums[1])

    def contract(qk, state):
        full = dot_t(qk, state.reshape(COLS, DK).astype(BF16))
        return [diagonal(full[:, g * 128 : (g + 1) * 128], state_masks) for g in range(GROUPS)]

    def own_rows(first, count):
        def one(r):
            qk = gbuf[:, r].reshape(N_VALUE * TILE, DK)
            at = pl.multiple_of(r * 8, 8)
            for g, block in enumerate(contract(qk, st_v[r])):
                msc[g, pl.ds(at, 8)] = block
            msc[GROUPS, pl.ds(at, 8)] = diagonal(dot_t(qk, qk), gram_masks)

        def some(i, _):
            for k in range(UNROLL):
                one(first + UNROLL * i + k)
            return 0

        if count == UNROLL:
            some(0, 0)
        else:
            lax.fori_loop(0, count // UNROLL, some, 0)

    def foreign_rows():
        for d in range(N_DP):
            qk = gbuf[:, ROWS + d].reshape(N_VALUE * TILE, DK)
            blocks = contract(qk, pf_v[chosen_slots[d]])
            rsnd[d] = jnp.concatenate(blocks, axis=0).astype(BF16)

    def back(i):
        dst = peer(i)
        return pltpu.make_async_remote_copy(
            src_ref=rsnd.at[dst],
            dst_ref=rrcv.at[me_d],
            send_sem=bs.at[i],
            recv_sem=br.at[i],
            device_id=(dst, me_v),
            device_id_type=MESH,
        )

    l_p.wait()
    for j in (0, 1, 3, 2):
        foreign_forwarded(j)
    foreign_rows()
    for i in range(N_DP):
        if PLANE[i] != (0, 0):
            back(i).start()
    rrcv[me_d] = rsnd[me_d]

    def row_get(chunk):
        def get(at):
            return rowq[at + BASE[chunk] : at + BASE[chunk] + CHUNK]

        return get

    src = iota((DK, 128), 0)
    head = (iota((DK, 128), 1) % H) // 2
    spread = [src == 64 + head * 4 + s for s in range(STEPS)] + [src == head * 4 + t for t in range(STEPS)]
    spread = jnp.concatenate([entry.astype(F32) for entry in spread], axis=1).astype(BF16)

    def contractions(chunk):
        def part_of(g, k):
            return msc[g, pl.ds(BASE[chunk] * 8 + k, CHUNK, stride=8), :]

        all_here(chunk)
        own_rows(BASE[chunk], CHUNK)
        gram = [part_of(GROUPS, k) for k in range(2 * STEPS)]
        gram = jnp.concatenate(gram, axis=0)
        high = gram.astype(BF16)
        low = (gram - high.astype(F32)).astype(BF16)
        copied = dot(jnp.concatenate([high, low], axis=0), spread)
        copied = copied[: 2 * STEPS * CHUNK] + copied[2 * STEPS * CHUNK :]

        def entry(k, s):
            return copied[k * CHUNK : (k + 1) * CHUNK, s * 128 : (s + 1) * 128]

        def put(at, what):
            rowq[at + BASE[chunk] : at + BASE[chunk] + CHUNK] = what

        inv_k, inv_q = [], []
        for t in range(STEPS):
            inv_k.append(lax.rsqrt(entry(STEPS + t, t) + 1e-06))
            inv_q.append(lax.rsqrt(entry(t, STEPS + t) + 1e-06) * DK ** (-0.5))
            put(INV_K + t * ROWS, inv_k[t])
            put(INV_Q + t * ROWS, inv_q[t])
        for s, t in PAIRS:
            at = PAIRS.index((s, t)) * ROWS
            if s < t:
                put(KEY_KEY + at, entry(STEPS + t, s) * (inv_k[s] * inv_k[t]))
            put(KEY_QUERY + at, entry(t, s) * (inv_k[s] * inv_q[t]))
        return part_of

    def recurrence(get, contracted, fresh):
        readouts = [[None] * GROUPS for _ in range(STEPS)]
        squares = [None] * STEPS
        for g in range(GROUPS):
            written = []
            kept = None
            for t in range(STEPS):
                a, b = get(RETAIN + t * ROWS), get(STRENGTH + t * ROWS)
                kept = a if kept is None else kept * a
                written = [w * a for w in written]
                if fresh is not None:
                    kept = jnp.where(fresh[t], a, kept)
                    written = [jnp.where(fresh[t], 0.0, w) for w in written]
                memory = kept * contracted(g, STEPS + t) * get(INV_K + t * ROWS)
                readout = kept * contracted(g, t) * get(INV_Q + t * ROWS)
                for s, w in enumerate(written):
                    at = PAIRS.index((s, t)) * ROWS
                    memory = memory + w * get(KEY_KEY + at)
                    readout = readout + w * get(KEY_QUERY + at)
                update = (get(VALUES + g * ALL + t * ROWS) - memory) * b
                readout = readout + update * get(KEY_QUERY + PAIRS.index((t, t)) * ROWS)
                written.append(update)
                readouts[t][g] = readout
                square = readout * readout
                squares[t] = square if g == 0 else squares[t] + square
        packed = jnp.zeros_like(squares[0])
        for t in range(STEPS):
            total = squares[t] + pltpu.roll(squares[t], 64, 1)
            total = total + pltpu.roll(total, 32, 1)
            packed = jnp.where(seg == t, total, packed)
        return readouts, packed

    def silu_gain(readouts, get):
        for g in range(GROUPS):
            gain = jnp.zeros((1, 128), F32)
            for e in range(4):
                gain = jnp.where(seg == e, gain_ref[g * 4 + e], gain)
            for t in range(STEPS):
                gate = get(GATING + g * ALL + t * ROWS)
                readouts[t][g] = readouts[t][g] * gain * (gate * jax.nn.sigmoid(gate))

    def scalings(summed):
        out = []
        for t in range(STEPS):
            total = jnp.where(seg == t, summed, 0.0)
            total = total + pltpu.roll(total, 64, 1)
            total = total + pltpu.roll(total, 32, 1)
            out.append(lax.rsqrt(total * (1.0 / DV) + 1e-06))
        return out

    def exchange(place, s_sem, r_sem):
        def one(i, slot):
            return pltpu.make_async_remote_copy(
                src_ref=place(slot),
                dst_ref=place(slot),
                send_sem=s_sem(i),
                recv_sem=r_sem(i),
                device_id=(me_d, (me_v + i) % N_VALUE),
                device_id_type=MESH,
            )

        sends = [one(i, me_v) for i in range(1, N_VALUE)]
        arrivals = [one(i, (me_v + N_VALUE - i) % N_VALUE) for i in range(1, N_VALUE)]
        return sends, arrivals

    def first_half(chunk, part_of):
        readouts, packed = recurrence(row_get(chunk), part_of, None)
        sqbuf[chunk, me_v] = packed.astype(BF16)
        sends, arrivals = exchange(
            lambda slot: sqbuf.at[chunk, slot], lambda i: qs.at[chunk, i], lambda i: qr.at[chunk, i]
        )
        for copy in sends:
            copy.start()
        return readouts, sends, arrivals

    def scaled(chunk, readouts, arrivals):
        for copy in arrivals:
            copy.wait_recv()
        scales = scalings(jnp.sum(sqbuf[chunk].astype(F32), axis=0))
        for t in range(STEPS):
            for g in range(GROUPS):
                rows = slice(t * CHUNK, (t + 1) * CHUNK)
                gat_s[chunk, rows, g * 128 : (g + 1) * 128] = (readouts[t][g] * scales[t]).astype(BF16)

    order = [(x + j) % N_X for j in (2, 1, 3, 0)]

    def project(what, to):
        at = pl.multiple_of(to * PIECE, PIECE)
        return dot(what, wo_v[:, pl.ds(at, PIECE)])

    def first_copy(chunk, k):
        return pltpu.make_async_remote_copy(
            src_ref=r1_snd.at[chunk, k, pl.ds(0, SUMMED[chunk])],
            dst_ref=r1_rcv.at[chunk, k, pl.ds(0, SUMMED[chunk])],
            send_sem=r1s.at[chunk, k],
            recv_sem=r1r.at[chunk, k],
            device_id=(me_d, partner),
            device_id_type=MESH,
        )

    def second_copy(chunk, k):
        return pltpu.make_async_remote_copy(
            src_ref=r2_snd.at[chunk, k, pl.ds(0, SUMMED[chunk])],
            dst_ref=r2_rcv.at[chunk, k, pl.ds(0, SUMMED[chunk])],
            send_sem=r2s.at[chunk, k],
            recv_sem=r2r.at[chunk, k],
            device_id=(me_d, vid(order[k], c)),
            device_id_type=MESH,
        )

    def sum_over_cores(chunk):
        n = SUMMED[chunk]
        gated = gat_s[chunk, :n]
        for k in range(N_X):
            r1_snd[chunk, k, :n] = project(gated, vid(order[k], 1 - c)).astype(BF16)
            first_copy(chunk, k).start()
        for k in range(N_X):
            part[chunk, k, :n] = project(gated, vid(order[k], c))

    def sum_along_x(chunk):
        n = SUMMED[chunk]
        for k in range(N_X - 1):
            first_copy(chunk, k).wait_recv()
            r2_snd[chunk, k, :n] = (part[chunk, k, :n] + r1_rcv[chunk, k, :n].astype(F32)).astype(BF16)
            second_copy(chunk, k).start()

    def summed(chunk):
        n = SUMMED[chunk]
        first_copy(chunk, 3).wait_recv()
        total = part[chunk, 3, :n] + r1_rcv[chunk, 3, :n].astype(F32)
        for k in (1, 2, 0):
            second_copy(chunk, k).wait_recv()
            total = total + r2_rcv[chunk, k, :n].astype(F32)
        return total

    l_s.wait()
    pass_on(FIRST)
    pass_on(LAST)
    readouts_a, sq_sends_a, sq_arrivals_a = first_half(FIRST, contractions(FIRST))
    part_of_b = contractions(LAST)
    slots = [(t, j) for t in range(STEPS) for j in range(REPLACED)]
    for k, (t, j) in enumerate(slots):
        slotq[k * QUANTITIES : (k + 1) * QUANTITIES] = rowq[pl.ds(fin_ref[t, j, me_d], QUANTITIES, stride=ROWS), :]

    def slot_get(at):
        return slotq[pl.ds(at // ROWS, len(slots), stride=QUANTITIES), :]

    slot_of = jnp.full((ALL, 128), -1, jnp.int32)
    take_of = jnp.full((ALL, len(slots) * STEPS), -1, jnp.int32)
    for k, (t, j) in enumerate(slots):
        done = fin_ref[t, j, me_d]
        wide_row, thin_row = iota(slot_of.shape, 0), iota(take_of.shape, 0)
        slot_of = jnp.where((wide_row % ROWS == done) & (wide_row // ROWS >= t), k, slot_of)
        take_of = jnp.where((thin_row % ROWS == done) & (thin_row // ROWS >= t), k, take_of)
    column = iota(take_of.shape, 1)
    same_step = column // len(slots) == iota(take_of.shape, 0) // ROWS
    take = ((take_of == column % len(slots)) & same_step).astype(BF16)

    for i in range(N_DP):
        if PLANE[i] != (0, 0):
            back(i).wait_recv()
    for k, (t, j) in enumerate(slots):
        rf[k * GROUPS * 8 : (k + 1) * GROUPS * 8] = rrcv[own_ref[t, j, me_d]].astype(F32)
    slot_row = iota((len(slots), 128), 0)
    slot_readouts, slot_packed = recurrence(
        slot_get,
        lambda g, k: rf[pl.ds(g * 8 + k, len(slots), stride=GROUPS * 8), :],
        [slot_row // REPLACED == t for t in range(STEPS)],
    )
    ssqbuf[me_v] = slot_packed
    ssq_sends, ssq_arrivals = exchange(lambda slot: ssqbuf.at[slot], lambda i: sqs.at[i], lambda i: sqr.at[i])
    for copy in ssq_sends:
        copy.start()
    readouts_b, sq_sends_b, sq_arrivals_b = first_half(LAST, part_of_b)
    silu_gain(readouts_a, row_get(FIRST))
    l_o.wait()
    scaled(FIRST, readouts_a, sq_arrivals_a)
    sum_over_cores(FIRST)
    silu_gain(readouts_b, row_get(LAST))
    silu_gain(slot_readouts, slot_get)
    sum_along_x(FIRST)
    scaled(LAST, readouts_b, sq_arrivals_b)

    for copy in ssq_arrivals:
        copy.wait_recv()
    slot_scales = scalings(jnp.sum(ssqbuf[...], axis=0))
    gat_s[LAST, SUMMED[FIRST] : SUMMED[LAST]] = jnp.concatenate(
        [
            jnp.concatenate([slot_readouts[t][g] * slot_scales[t] for g in range(GROUPS)], axis=1)
            for t in range(STEPS)
        ],
        axis=0,
    ).astype(BF16)

    sum_over_cores(LAST)
    sum_along_x(LAST)

    totals = [summed(FIRST), summed(LAST)]
    chosen = dot(take, totals[LAST][SUMMED[FIRST] :].astype(BF16))
    for half in range(PIECE // 128):
        lanes = slice(half * 128, (half + 1) * 128)
        for chunk, total in enumerate(totals):
            for t in range(STEPS):
                rows = slice(t * ROWS + BASE[chunk], t * ROWS + BASE[chunk] + CHUNK)
                own = total[t * CHUNK : (t + 1) * CHUNK, lanes]
                out_ref[rows, lanes] = jnp.where(slot_of[rows] >= 0, chosen[rows, lanes], own).astype(BF16)

    for j in range(N_X):
        foreign_all(j).wait_send()
        foreign_forward(j).wait_send()
    for i in range(N_DP):
        if PLANE[i] != (0, 0):
            back(i).wait_send()
    for chunk in range(2):
        for j in range(N_X):
            along(chunk, j).wait_send()
        for j in range(1, N_X):
            forward(chunk, j).wait_send()
        for k in range(N_X):
            first_copy(chunk, k).wait_send()
        for k in range(N_X - 1):
            second_copy(chunk, k).wait_send()
    for copy in sq_sends_a + sq_sends_b + ssq_sends:
        copy.wait_send()


def on_device(
    inputs,
    qk_weight,
    value_weight,
    output_gate_weight,
    rate_weight,
    log_decay,
    decay_bias,
    norm_gain,
    out_weight,
    states,
    prefilled,
    finished,
    new_owner,
    new_slot,
):
    hbm = pl.BlockSpec(memory_space=pl.ANY)
    dma = pltpu.SemaphoreType.DMA
    produced = pl.pallas_call(
        kernel,
        out_shape=pltpu.VMEM((STEPS * ROWS, PIECE), BF16),
        in_specs=[hbm] * 14,
        out_specs=pl.BlockSpec(memory_space=pltpu.VMEM),
        scratch_shapes=[
            pltpu.SMEM((STEPS, REPLACED, N_DP), jnp.int32),
            pltpu.SMEM((STEPS, REPLACED, N_DP), jnp.int32),
            pltpu.SMEM((STEPS, REPLACED, N_DP), jnp.int32),
            pltpu.SMEM((H,), F32),
            pltpu.SMEM((H,), F32),
            pltpu.SMEM((DV // N_VALUE,), F32),
            pltpu.VMEM((STEPS, ROWS, WIDTH), BF16),
            pltpu.VMEM((WIDTH, COLS), BF16),
            pltpu.VMEM((WIDTH, COLS), BF16),
            pltpu.VMEM((WIDTH, COLS), BF16),
            pltpu.VMEM((2 * H, WIDTH), BF16),
            pltpu.VMEM((COLS, WIDTH), BF16),
            pltpu.VMEM((ROWS, 16, H, DK), F32),
            pltpu.VMEM((16, 16, H, DK), F32),
            pltpu.VMEM((TILE * BLOCKS, DK), F32),
            pltpu.VMEM((N_DP, TILE, DK), BF16),
            pltpu.VMEM((N_VALUE, BLOCKS, TILE, DK), BF16),
            pltpu.VMEM((GROUPS + 1, ROWS * 8, 128), F32),
            pltpu.VMEM((N_DP, GROUPS * 8, 128), BF16),
            pltpu.VMEM((N_DP, GROUPS * 8, 128), BF16),
            pltpu.VMEM((STEPS * REPLACED * GROUPS * 8, 128), F32),
            pltpu.VMEM((QUANTITIES * ROWS, 128), F32),
            pltpu.VMEM((STEPS * REPLACED * QUANTITIES, 128), F32),
            pltpu.VMEM((2, SUMMED[LAST], COLS), BF16),
            pltpu.VMEM((2, N_VALUE, CHUNK, 128), BF16),
            pltpu.VMEM((N_VALUE, STEPS * REPLACED, 128), F32),
            pltpu.VMEM((2, N_X, SUMMED[LAST], PIECE), BF16),
            pltpu.VMEM((2, N_X, SUMMED[LAST], PIECE), BF16),
            pltpu.VMEM((2, N_X, SUMMED[LAST], PIECE), F32),
            pltpu.VMEM((2, N_X - 1, SUMMED[LAST], PIECE), BF16),
            pltpu.VMEM((2, N_X - 1, SUMMED[LAST], PIECE), BF16),
            dma((15 + QK_PIECES,)),
            dma((2, 2 * N_X - 1)),
            dma((2, 2 * N_X - 1)),
            dma((N_X,)),
            dma((N_X,)),
            dma((N_X,)),
            dma((N_X,)),
            dma((N_DP,)),
            dma((N_DP,)),
            dma((2, N_VALUE)),
            dma((2, N_VALUE)),
            dma((2, N_X)),
            dma((2, N_X)),
            dma((2, N_X - 1)),
            dma((2, N_X - 1)),
            dma((N_VALUE,)),
            dma((N_VALUE,)),
        ],
        compiler_params=pltpu.CompilerParams(
            collective_id=0, has_side_effects=True, vmem_limit_bytes=56 * 2**20
        ),
        name="delta_steps",
    )(
        finished.transpose(0, 2, 1),
        new_owner.transpose(0, 2, 1),
        new_slot.transpose(0, 2, 1),
        log_decay,
        decay_bias,
        norm_gain,
        inputs,
        qk_weight,
        value_weight,
        output_gate_weight,
        rate_weight.T,
        out_weight,
        states,
        prefilled,
    )
    return produced.reshape(STEPS, ROWS, PIECE)


def solution(mesh):
    return jax.shard_map(
        on_device,
        mesh=mesh,
        in_specs=(
            P(None, "dp", None),
            P(None, "value"),
            P(None, "value"),
            P(None, "value"),
            P(),
            P(),
            P(),
            P("value"),
            P("value", None),
            P("dp", "value", None, None),
            P("dp", "value", None, None),
            P(),
            P(),
            P(),
        ),
        out_specs=P(None, "dp", "value"),
        check_vma=False,
    )
```

```python
import functools

import jax
import jax.numpy as jnp
from jax import lax
from jax.experimental import pallas as pl
from jax.experimental.pallas import tpu as pltpu
from jax.sharding import PartitionSpec as P

F32 = jnp.float32
BF16 = jnp.bfloat16
MESH = pl.DeviceIdType.MESH

STEPS = 4
REPLACED = 2
N_DP = 16
N_VALUE = 8
N_X = 4
ROWS = 32
H = 32
DK = 128
DV = 128
WIDTH = 2048
COLS = 512
PIECE = 256
BLOCKS = ROWS + N_DP
HEADS = 4
TILE = HEADS * STEPS
GROUPS = COLS // 128
ALL = STEPS * ROWS

PAIRS = [(s, t) for t in range(STEPS) for s in range(t + 1)]
VALUES, GATING = 0, GROUPS * ALL
RETAIN = 2 * GROUPS * ALL
STRENGTH, INV_K, INV_Q = RETAIN + ALL, RETAIN + 2 * ALL, RETAIN + 3 * ALL
KEY_KEY = RETAIN + 4 * ALL
KEY_QUERY = KEY_KEY + len(PAIRS) * ROWS
QUANTITIES = KEY_QUERY // ROWS + len(PAIRS)

FIRST, LAST = 0, 1
BASE = (0, 16)
CHUNK = 16
SLOT_ROWS = STEPS * STEPS * REPLACED
SUMMED = (STEPS * CHUNK, STEPS * CHUNK + SLOT_ROWS)
QK_PIECES = 4
UNROLL = 16


def ring(k):
    return min(k, N_X - k)


PLANE = sorted(((a, b) for a in range(N_X) for b in range(N_X)), key=lambda o: -ring(o[0]) - ring(o[1]))
SPACE = sorted(((i, j) for i in range(N_DP) for j in range(N_X)), key=lambda o: -sum(map(ring, (*PLANE[o[0]], o[1]))))


def iota(shape, dim):
    return lax.broadcasted_iota(jnp.int32, shape, dim)


def dot(a, b, **kw):
    return jnp.dot(a, b, preferred_element_type=F32, **kw)


def dot_t(a, b):
    return lax.dot_general(a, b, (((1,), (1,)), ((), ())), preferred_element_type=F32)


def kernel(
    fin_hbm,
    own_hbm,
    slot_hbm,
    logd_hbm,
    bias_hbm,
    gain_hbm,
    x_hbm,
    wqk_hbm,
    wv_hbm,
    wg_hbm,
    wr_hbm,
    wo_hbm,
    st_hbm,
    pf_hbm,
    out_ref,
    fin_ref,
    own_ref,
    slot_ref,
    logd_ref,
    bias_ref,
    gain_ref,
    x_v,
    wqk_v,
    wv_v,
    wg_v,
    wr_v,
    wo_v,
    st_v,
    pf_v,
    zf,
    snd_f,
    gbuf,
    msc,
    rsnd,
    rrcv,
    rf,
    rowq,
    slotq,
    gat_s,
    sqbuf,
    ssqbuf,
    r1_snd,
    r1_rcv,
    part,
    r2_snd,
    r2_rcv,
    loc,
    ag_s,
    ag_r,
    fs,
    fr,
    fps,
    fpr,
    bs,
    br,
    qs,
    qr,
    r1s,
    r1r,
    r2s,
    r2r,
    sqs,
    sqr,
):
    me_d = lax.axis_index("dp")
    me_v = lax.axis_index("value")
    x = me_v // 2
    c = me_v % 2

    def vid(xx, cc):
        return xx * 2 + cc

    partner = vid(x, 1 - c)

    def peer(i):
        dz, dy = PLANE[i]
        return ((me_d // N_X + dz) % N_X) * N_X + (me_d % N_X + dy) % N_X

    def load(src, dst, k):
        cp = pltpu.make_async_copy(src, dst, loc.at[k])
        cp.start()
        return cp

    scalars = (
        (fin_hbm, fin_ref),
        (own_hbm, own_ref),
        (slot_hbm, slot_ref),
        (logd_hbm, logd_ref),
        (bias_hbm, bias_ref),
        (gain_hbm, gain_ref),
    )
    l_scalars = [load(src, dst, 9 + k) for k, (src, dst) in enumerate(scalars)]
    l_x = load(x_hbm, x_v, 0)
    pieces = [pl.ds(k * (WIDTH // QK_PIECES), WIDTH // QK_PIECES) for k in range(QK_PIECES)]
    l_qk = [load(wqk_hbm.at[piece], wqk_v.at[piece], 15 + k) for k, piece in enumerate(pieces)]

    barrier = pltpu.get_barrier_semaphore()
    greeted = 0
    for i, j in SPACE:
        if PLANE[i] != (0, 0) or j:
            to = (peer(i), vid((x + j) % N_X, c))
            pl.semaphore_signal(barrier, inc=1, device_id=to, device_id_type=MESH)
            greeted += 1
    for j in range(N_X):
        to = (me_d, vid((x + j) % N_X, 1 - c))
        pl.semaphore_signal(barrier, inc=1, device_id=to, device_id_type=MESH)
        greeted += 1

    l_r = load(wr_hbm, wr_v, 2)
    l_v = load(wv_hbm, wv_v, 3)
    l_g = load(wg_hbm, wg_v, 4)
    l_p = load(pf_hbm, pf_v, 5)
    l_s = load(st_hbm, st_v, 6)
    l_o = load(wo_hbm, wo_v, 8)

    for copy in l_scalars:
        copy.wait()
    pick = jnp.zeros((N_DP, ROWS), F32)
    for t in range(STEPS):
        for j in range(REPLACED):
            hit = (iota((N_DP, ROWS), 0) == own_ref[t, j, me_d]) & (iota((N_DP, ROWS), 1) == fin_ref[t, j, me_d])
            pick = jnp.where(hit, 1.0, pick)
    pick = pick.astype(BF16)

    l_x.wait()
    xin = x_v[...].reshape(STEPS * ROWS, WIDTH)
    joined = jnp.zeros((ALL, COLS), F32)
    for k, piece in enumerate(pieces):
        l_qk[k].wait()
        deep = slice(k * (WIDTH // QK_PIECES), (k + 1) * (WIDTH // QK_PIECES))
        joined = joined + dot(xin[:, deep], wqk_v[piece])
    joined = joined.astype(BF16)
    joined_f = joined.astype(F32)
    for t in range(STEPS):
        chosen = dot(pick, joined[t * ROWS : (t + 1) * ROWS])
        for h in range(HEADS):
            at = (h * STEPS + t) * BLOCKS
            zf[at : at + ROWS] = joined_f[t * ROWS : (t + 1) * ROWS, h * 128 : (h + 1) * 128]
            zf[at + ROWS : at + BLOCKS] = chosen[:, h * 128 : (h + 1) * 128]

    def block_of(r):
        return zf[pl.ds(r, TILE, stride=BLOCKS), :].astype(BF16)

    for o in range(N_DP):
        snd_f[o] = block_of(ROWS + o)
    pl.semaphore_wait(barrier, greeted)

    def foreign(i, j):
        dst = peer(i)
        return pltpu.make_async_remote_copy(
            src_ref=snd_f.at[dst],
            dst_ref=gbuf.at[me_v, ROWS + me_d],
            send_sem=fs.at[j],
            recv_sem=fr.at[j],
            device_id=(dst, vid((x + j) % N_X, c)),
            device_id_type=MESH,
        )

    def foreign_all(j):
        slot = vid((x + N_X - j) % N_X, c)
        first = 1 if j == 0 else 0
        rows = pl.ds(ROWS, N_DP - first)
        return pltpu.make_async_remote_copy(
            src_ref=gbuf.at[slot, rows],
            dst_ref=gbuf.at[slot, rows],
            send_sem=fs.at[j],
            recv_sem=fr.at[j],
            device_id=(me_d, partner),
            device_id_type=MESH,
        )

    def foreign_forward(j):
        slot = vid((x + N_X - j) % N_X, c)
        rows = pl.ds(ROWS, N_DP)
        return pltpu.make_async_remote_copy(
            src_ref=gbuf.at[slot, rows],
            dst_ref=gbuf.at[slot, rows],
            send_sem=fps.at[j],
            recv_sem=fpr.at[j],
            device_id=(me_d, partner),
            device_id_type=MESH,
        )

    def foreign_forwarded(j):
        slot = vid((x + N_X - j) % N_X, 1 - c)
        rows = pl.ds(ROWS, N_DP)
        pltpu.make_async_remote_copy(
            src_ref=gbuf.at[slot, rows],
            dst_ref=gbuf.at[slot, rows],
            send_sem=fps.at[j],
            recv_sem=fpr.at[j],
            device_id=(me_d, partner),
            device_id_type=MESH,
        ).wait_recv()

    for i, j in SPACE:
        if PLANE[i] != (0, 0) or j:
            foreign(i, j).start()
    gbuf[me_v, ROWS + me_d] = snd_f[me_d]
    for r in range(CHUNK):
        gbuf[me_v, r] = block_of(r)

    def gather(chunk, k, slot, to):
        rows = pl.ds(BASE[chunk], CHUNK)
        return pltpu.make_async_remote_copy(
            src_ref=gbuf.at[slot, rows],
            dst_ref=gbuf.at[slot, rows],
            send_sem=ag_s.at[chunk, k],
            recv_sem=ag_r.at[chunk, k],
            device_id=(me_d, to),
            device_id_type=MESH,
        )

    def along(chunk, j):
        return gather(chunk, j, me_v, vid((x + j) % N_X, c) if j else partner)

    def arrived(chunk, j):
        gather(chunk, j, vid((x + N_X - j) % N_X, c) if j else partner, partner).wait_recv()

    def forward(chunk, j):
        return gather(chunk, N_X - 1 + j, vid((x + N_X - j) % N_X, c), partner)

    def forwarded(chunk, j):
        gather(chunk, N_X - 1 + j, vid((x + N_X - j) % N_X, 1 - c), partner).wait_recv()

    def send_own(chunk):
        for j in (2, 1, 3, 0):
            along(chunk, j).start()

    def pass_on(chunk):
        for j in (1, 3, 2):
            arrived(chunk, j)
            forward(chunk, j).start()

    def all_here(chunk):
        arrived(chunk, 0)
        for j in (1, 3, 2):
            forwarded(chunk, j)

    send_own(FIRST)
    for r in range(CHUNK, 2 * CHUNK):
        gbuf[me_v, r] = block_of(r)
    send_own(LAST)

    seg = iota((1, 128), 1) // H
    in_seg = iota((1, 128), 1) % H
    l_r.wait()
    rates = dot_t(xin, wr_v[...])
    decay = jnp.zeros((1, 128), F32)
    bias = jnp.zeros((1, 128), F32)
    for h in range(H):
        decay = jnp.where(in_seg == h, logd_ref[h], decay)
        bias = jnp.where(in_seg == h, bias_ref[h], bias)
    wide = jnp.concatenate([rates, rates], axis=1)
    turned = pltpu.roll(wide, H, 1)
    odd = seg % 2 == 1
    rowq[RETAIN : RETAIN + ALL] = jnp.exp(-jnp.exp(decay) * jax.nn.softplus(jnp.where(odd, wide, turned) + bias))
    rowq[STRENGTH : STRENGTH + ALL] = jax.nn.sigmoid(jnp.where(odd, turned, wide))
    l_v.wait()
    values = dot(xin, wv_v[...])
    for g in range(GROUPS):
        rowq[VALUES + g * ALL : VALUES + (g + 1) * ALL] = values[:, g * 128 : (g + 1) * 128]
    l_g.wait()
    gating = dot(xin, wg_v[...])
    for g in range(GROUPS):
        rowq[GATING + g * ALL : GATING + (g + 1) * ALL] = gating[:, g * 128 : (g + 1) * 128]
    chosen_slots = []
    for i in range(N_DP):
        d = peer(i)
        slot = jnp.int32(0)
        for t in range(STEPS):
            for j in range(REPLACED):
                slot = jnp.where(own_ref[t, j, d] == me_d, slot_ref[t, j, d], slot)
        chosen_slots.append(slot)
    for j in (0, 1, 3, 2):
        foreign_all(j).wait_recv()
        foreign_forward(j).start()

    lane = iota((8, 128), 1)
    sub = iota((8, 128), 0)
    state_masks = [(lane % H) // 2 == 2 * i + sub // 4 for i in range(8)]
    gram_masks = [(lane % 64) // 4 == 2 * i + sub // 4 for i in range(8)]

    def diagonal(full, masks):
        sums = []
        for kind in range(2):
            acc = jnp.zeros((8, 128), F32)
            for i in range(8):
                at = kind * 64 + i * 8
                acc = jnp.where(masks[i], full[at : at + 8], acc)
            sums.append(acc + pltpu.roll(acc, 4, 0))
        return jnp.where(sub < 4, sums[0], sums[1])

    def contract(qk, state):
        full = dot_t(qk, state.reshape(COLS, DK).astype(BF16))
        return [diagonal(full[:, g * 128 : (g + 1) * 128], state_masks) for g in range(GROUPS)]

    def own_rows(first, count):
        def one(r):
            qk = gbuf[:, r].reshape(N_VALUE * TILE, DK)
            at = pl.multiple_of(r * 8, 8)
            for g, block in enumerate(contract(qk, st_v[r])):
                msc[g, pl.ds(at, 8)] = block
            msc[GROUPS, pl.ds(at, 8)] = diagonal(dot_t(qk, qk), gram_masks)

        def some(i, _):
            for k in range(UNROLL):
                one(first + UNROLL * i + k)
            return 0

        if count == UNROLL:
            some(0, 0)
        else:
            lax.fori_loop(0, count // UNROLL, some, 0)

    def foreign_rows(first, end):
        for i in range(first, end):
            d = peer(i)
            qk = gbuf[:, ROWS + d].reshape(N_VALUE * TILE, DK)
            blocks = contract(qk, pf_v[chosen_slots[i]])
            rsnd[d] = jnp.concatenate(blocks, axis=0).astype(BF16)

    def back(i):
        dst = peer(i)
        return pltpu.make_async_remote_copy(
            src_ref=rsnd.at[dst],
            dst_ref=rrcv.at[me_d],
            send_sem=bs.at[i],
            recv_sem=br.at[i],
            device_id=(dst, me_v),
            device_id_type=MESH,
        )

    l_p.wait()
    for j in (0, 1, 3, 2):
        foreign_forwarded(j)
    for first in range(0, N_DP, N_DP // 2):
        foreign_rows(first, first + N_DP // 2)
        for i in range(first, first + N_DP // 2):
            if PLANE[i] != (0, 0):
                back(i).start()
    rrcv[me_d] = rsnd[me_d]

    def row_get(chunk):
        def get(at):
            return rowq[at + BASE[chunk] : at + BASE[chunk] + CHUNK]

        return get

    src = iota((DK, 128), 0)
    head = (iota((DK, 128), 1) % H) // 2
    spread = [src == 64 + head * 4 + s for s in range(STEPS)] + [src == head * 4 + t for t in range(STEPS)]
    spread = jnp.concatenate([entry.astype(F32) for entry in spread], axis=1).astype(BF16)

    def contractions(chunk):
        def part_of(g, k):
            return msc[g, pl.ds(BASE[chunk] * 8 + k, CHUNK, stride=8), :]

        all_here(chunk)
        own_rows(BASE[chunk], CHUNK)
        gram = [part_of(GROUPS, k) for k in range(2 * STEPS)]
        gram = jnp.concatenate(gram, axis=0)
        high = gram.astype(BF16)
        low = (gram - high.astype(F32)).astype(BF16)
        copied = dot(jnp.concatenate([high, low], axis=0), spread)
        copied = copied[: 2 * STEPS * CHUNK] + copied[2 * STEPS * CHUNK :]

        def entry(k, s):
            return copied[k * CHUNK : (k + 1) * CHUNK, s * 128 : (s + 1) * 128]

        def put(at, what):
            rowq[at + BASE[chunk] : at + BASE[chunk] + CHUNK] = what

        inv_k, inv_q = [], []
        for t in range(STEPS):
            inv_k.append(lax.rsqrt(entry(STEPS + t, t) + 1e-06))
            inv_q.append(lax.rsqrt(entry(t, STEPS + t) + 1e-06) * DK ** (-0.5))
            put(INV_K + t * ROWS, inv_k[t])
            put(INV_Q + t * ROWS, inv_q[t])
        for s, t in PAIRS:
            at = PAIRS.index((s, t)) * ROWS
            if s < t:
                put(KEY_KEY + at, entry(STEPS + t, s) * (inv_k[s] * inv_k[t]))
            put(KEY_QUERY + at, entry(t, s) * (inv_k[s] * inv_q[t]))
        return part_of

    def recurrence(get, contracted, fresh):
        readouts = [[None] * GROUPS for _ in range(STEPS)]
        squares = [None] * STEPS
        for g in range(GROUPS):
            written = []
            kept = None
            for t in range(STEPS):
                a, b = get(RETAIN + t * ROWS), get(STRENGTH + t * ROWS)
                kept = a if kept is None else kept * a
                written = [w * a for w in written]
                if fresh is not None:
                    kept = jnp.where(fresh[t], a, kept)
                    written = [jnp.where(fresh[t], 0.0, w) for w in written]
                memory = kept * contracted(g, STEPS + t) * get(INV_K + t * ROWS)
                readout = kept * contracted(g, t) * get(INV_Q + t * ROWS)
                for s, w in enumerate(written):
                    at = PAIRS.index((s, t)) * ROWS
                    memory = memory + w * get(KEY_KEY + at)
                    readout = readout + w * get(KEY_QUERY + at)
                update = (get(VALUES + g * ALL + t * ROWS) - memory) * b
                readout = readout + update * get(KEY_QUERY + PAIRS.index((t, t)) * ROWS)
                written.append(update)
                readouts[t][g] = readout
                square = readout * readout
                squares[t] = square if g == 0 else squares[t] + square
        packed = jnp.zeros_like(squares[0])
        for t in range(STEPS):
            total = squares[t] + pltpu.roll(squares[t], 64, 1)
            total = total + pltpu.roll(total, 32, 1)
            packed = jnp.where(seg == t, total, packed)
        return readouts, packed

    def silu_gain(readouts, get):
        for g in range(GROUPS):
            gain = jnp.zeros((1, 128), F32)
            for e in range(4):
                gain = jnp.where(seg == e, gain_ref[g * 4 + e], gain)
            for t in range(STEPS):
                gate = get(GATING + g * ALL + t * ROWS)
                readouts[t][g] = readouts[t][g] * gain * (gate * jax.nn.sigmoid(gate))

    def scalings(summed):
        out = []
        for t in range(STEPS):
            total = jnp.where(seg == t, summed, 0.0)
            total = total + pltpu.roll(total, 64, 1)
            total = total + pltpu.roll(total, 32, 1)
            out.append(lax.rsqrt(total * (1.0 / DV) + 1e-06))
        return out

    def exchange(place, s_sem, r_sem):
        def one(i, slot):
            return pltpu.make_async_remote_copy(
                src_ref=place(slot),
                dst_ref=place(slot),
                send_sem=s_sem(i),
                recv_sem=r_sem(i),
                device_id=(me_d, (me_v + i) % N_VALUE),
                device_id_type=MESH,
            )

        sends = [one(i, me_v) for i in range(1, N_VALUE)]
        arrivals = [one(i, (me_v + N_VALUE - i) % N_VALUE) for i in range(1, N_VALUE)]
        return sends, arrivals

    def first_half(chunk, part_of):
        readouts, packed = recurrence(row_get(chunk), part_of, None)
        sqbuf[chunk, me_v] = packed.astype(BF16)
        sends, arrivals = exchange(
            lambda slot: sqbuf.at[chunk, slot], lambda i: qs.at[chunk, i], lambda i: qr.at[chunk, i]
        )
        for copy in sends:
            copy.start()
        return readouts, sends, arrivals

    def scaled(chunk, readouts, arrivals):
        for copy in arrivals:
            copy.wait_recv()
        scales = scalings(jnp.sum(sqbuf[chunk].astype(F32), axis=0))
        for t in range(STEPS):
            for g in range(GROUPS):
                rows = slice(t * CHUNK, (t + 1) * CHUNK)
                gat_s[chunk, rows, g * 128 : (g + 1) * 128] = (readouts[t][g] * scales[t]).astype(BF16)

    order = [(x + j) % N_X for j in (2, 1, 3, 0)]

    def project(what, to):
        at = pl.multiple_of(to * PIECE, PIECE)
        return dot(what, wo_v[:, pl.ds(at, PIECE)])

    def first_copy(chunk, k):
        return pltpu.make_async_remote_copy(
            src_ref=r1_snd.at[chunk, k, pl.ds(0, SUMMED[chunk])],
            dst_ref=r1_rcv.at[chunk, k, pl.ds(0, SUMMED[chunk])],
            send_sem=r1s.at[chunk, k],
            recv_sem=r1r.at[chunk, k],
            device_id=(me_d, partner),
            device_id_type=MESH,
        )

    def second_copy(chunk, k):
        return pltpu.make_async_remote_copy(
            src_ref=r2_snd.at[chunk, k, pl.ds(0, SUMMED[chunk])],
            dst_ref=r2_rcv.at[chunk, k, pl.ds(0, SUMMED[chunk])],
            send_sem=r2s.at[chunk, k],
            recv_sem=r2r.at[chunk, k],
            device_id=(me_d, vid(order[k], c)),
            device_id_type=MESH,
        )

    def sum_over_cores(chunk):
        n = SUMMED[chunk]
        gated = gat_s[chunk, :n]
        for k in range(N_X):
            r1_snd[chunk, k, :n] = project(gated, vid(order[k], 1 - c)).astype(BF16)
            first_copy(chunk, k).start()
        for k in range(N_X):
            part[chunk, k, :n] = project(gated, vid(order[k], c))

    def sum_along_x(chunk):
        n = SUMMED[chunk]
        for k in range(N_X - 1):
            first_copy(chunk, k).wait_recv()
            r2_snd[chunk, k, :n] = (part[chunk, k, :n] + r1_rcv[chunk, k, :n].astype(F32)).astype(BF16)
            second_copy(chunk, k).start()

    def sums_left(chunk):
        for k in range(N_X):
            first_copy(chunk, k).wait_send()
        for k in range(N_X - 1):
            second_copy(chunk, k).wait_send()

    def summed(chunk):
        n = SUMMED[chunk]
        first_copy(chunk, 3).wait_recv()
        total = part[chunk, 3, :n] + r1_rcv[chunk, 3, :n].astype(F32)
        for k in (1, 2, 0):
            second_copy(chunk, k).wait_recv()
            total = total + r2_rcv[chunk, k, :n].astype(F32)
        return total

    l_s.wait()
    pass_on(FIRST)
    pass_on(LAST)
    readouts_a, sq_sends_a, sq_arrivals_a = first_half(FIRST, contractions(FIRST))
    part_of_b = contractions(LAST)
    slots = [(t, j) for t in range(STEPS) for j in range(REPLACED)]
    for k, (t, j) in enumerate(slots):
        slotq[k * QUANTITIES : (k + 1) * QUANTITIES] = rowq[pl.ds(fin_ref[t, j, me_d], QUANTITIES, stride=ROWS), :]

    def slot_get(at):
        return slotq[pl.ds(at // ROWS, len(slots), stride=QUANTITIES), :]

    slot_of = jnp.full((ALL, 128), -1, jnp.int32)
    take_of = jnp.full((ALL, len(slots) * STEPS), -1, jnp.int32)
    for k, (t, j) in enumerate(slots):
        done = fin_ref[t, j, me_d]
        wide_row, thin_row = iota(slot_of.shape, 0), iota(take_of.shape, 0)
        slot_of = jnp.where((wide_row % ROWS == done) & (wide_row // ROWS >= t), k, slot_of)
        take_of = jnp.where((thin_row % ROWS == done) & (thin_row // ROWS >= t), k, take_of)
    column = iota(take_of.shape, 1)
    same_step = column // len(slots) == iota(take_of.shape, 0) // ROWS
    take = ((take_of == column % len(slots)) & same_step).astype(BF16)

    for i in range(N_DP):
        if PLANE[i] != (0, 0):
            back(i).wait_recv()
    for k, (t, j) in enumerate(slots):
        rf[k * GROUPS * 8 : (k + 1) * GROUPS * 8] = rrcv[own_ref[t, j, me_d]].astype(F32)
    slot_row = iota((len(slots), 128), 0)
    slot_readouts, slot_packed = recurrence(
        slot_get,
        lambda g, k: rf[pl.ds(g * 8 + k, len(slots), stride=GROUPS * 8), :],
        [slot_row // REPLACED == t for t in range(STEPS)],
    )
    ssqbuf[me_v] = slot_packed
    ssq_sends, ssq_arrivals = exchange(lambda slot: ssqbuf.at[slot], lambda i: sqs.at[i], lambda i: sqr.at[i])
    for copy in ssq_sends:
        copy.start()
    readouts_b, sq_sends_b, sq_arrivals_b = first_half(LAST, part_of_b)
    silu_gain(readouts_a, row_get(FIRST))
    l_o.wait()
    scaled(FIRST, readouts_a, sq_arrivals_a)
    sum_over_cores(FIRST)
    silu_gain(readouts_b, row_get(LAST))
    silu_gain(slot_readouts, slot_get)
    sum_along_x(FIRST)
    for j in range(N_X):
        foreign_all(j).wait_send()
        foreign_forward(j).wait_send()
    for i in range(N_DP):
        if PLANE[i] != (0, 0):
            back(i).wait_send()
    for chunk in (FIRST, LAST):
        for j in range(N_X):
            along(chunk, j).wait_send()
        for j in range(1, N_X):
            forward(chunk, j).wait_send()
    for copy in sq_sends_a:
        copy.wait_send()
    scaled(LAST, readouts_b, sq_arrivals_b)

    for copy in ssq_arrivals:
        copy.wait_recv()
    slot_scales = scalings(jnp.sum(ssqbuf[...], axis=0))
    gat_s[LAST, SUMMED[FIRST] : SUMMED[LAST]] = jnp.concatenate(
        [
            jnp.concatenate([slot_readouts[t][g] * slot_scales[t] for g in range(GROUPS)], axis=1)
            for t in range(STEPS)
        ],
        axis=0,
    ).astype(BF16)

    sum_over_cores(LAST)
    sum_along_x(LAST)

    for copy in sq_sends_b + ssq_sends:
        copy.wait_send()
    first_total = summed(FIRST)
    sums_left(FIRST)
    totals = [first_total, summed(LAST)]
    chosen = dot(take, totals[LAST][SUMMED[FIRST] :].astype(BF16))
    for half in range(PIECE // 128):
        lanes = slice(half * 128, (half + 1) * 128)
        for chunk, total in enumerate(totals):
            for t in range(STEPS):
                rows = slice(t * ROWS + BASE[chunk], t * ROWS + BASE[chunk] + CHUNK)
                own = total[t * CHUNK : (t + 1) * CHUNK, lanes]
                out_ref[rows, lanes] = jnp.where(slot_of[rows] >= 0, chosen[rows, lanes], own).astype(BF16)

    sums_left(LAST)


def on_device(
    inputs,
    qk_weight,
    value_weight,
    output_gate_weight,
    rate_weight,
    log_decay,
    decay_bias,
    norm_gain,
    out_weight,
    states,
    prefilled,
    finished,
    new_owner,
    new_slot,
):
    hbm = pl.BlockSpec(memory_space=pl.ANY)
    dma = pltpu.SemaphoreType.DMA
    produced = pl.pallas_call(
        kernel,
        out_shape=pltpu.VMEM((STEPS * ROWS, PIECE), BF16),
        in_specs=[hbm] * 14,
        out_specs=pl.BlockSpec(memory_space=pltpu.VMEM),
        scratch_shapes=[
            pltpu.SMEM((STEPS, REPLACED, N_DP), jnp.int32),
            pltpu.SMEM((STEPS, REPLACED, N_DP), jnp.int32),
            pltpu.SMEM((STEPS, REPLACED, N_DP), jnp.int32),
            pltpu.SMEM((H,), F32),
            pltpu.SMEM((H,), F32),
            pltpu.SMEM((DV // N_VALUE,), F32),
            pltpu.VMEM((STEPS, ROWS, WIDTH), BF16),
            pltpu.VMEM((WIDTH, COLS), BF16),
            pltpu.VMEM((WIDTH, COLS), BF16),
            pltpu.VMEM((WIDTH, COLS), BF16),
            pltpu.VMEM((2 * H, WIDTH), BF16),
            pltpu.VMEM((COLS, WIDTH), BF16),
            pltpu.VMEM((ROWS, 16, H, DK), F32),
            pltpu.VMEM((16, 16, H, DK), F32),
            pltpu.VMEM(((TILE + 1) * BLOCKS, DK), F32),
            pltpu.VMEM((N_DP, TILE, DK), BF16),
            pltpu.VMEM((N_VALUE, BLOCKS, TILE, DK), BF16),
            pltpu.VMEM((GROUPS + 1, (ROWS + 1) * 8, 128), F32),
            pltpu.VMEM((N_DP, GROUPS * 8, 128), BF16),
            pltpu.VMEM((N_DP, GROUPS * 8, 128), BF16),
            pltpu.VMEM(((STEPS * REPLACED + 1) * GROUPS * 8, 128), F32),
            pltpu.VMEM(((QUANTITIES + 1) * ROWS, 128), F32),
            pltpu.VMEM(((STEPS * REPLACED + 1) * QUANTITIES, 128), F32),
            pltpu.VMEM((2, SUMMED[LAST], COLS), BF16),
            pltpu.VMEM((2, N_VALUE, CHUNK, 128), BF16),
            pltpu.VMEM((N_VALUE, STEPS * REPLACED, 128), F32),
            pltpu.VMEM((2, N_X, SUMMED[LAST], PIECE), BF16),
            pltpu.VMEM((2, N_X, SUMMED[LAST], PIECE), BF16),
            pltpu.VMEM((2, N_X, SUMMED[LAST], PIECE), F32),
            pltpu.VMEM((2, N_X - 1, SUMMED[LAST], PIECE), BF16),
            pltpu.VMEM((2, N_X - 1, SUMMED[LAST], PIECE), BF16),
            dma((15 + QK_PIECES,)),
            dma((2, 2 * N_X - 1)),
            dma((2, 2 * N_X - 1)),
            dma((N_X,)),
            dma((N_X,)),
            dma((N_X,)),
            dma((N_X,)),
            dma((N_DP,)),
            dma((N_DP,)),
            dma((2, N_VALUE)),
            dma((2, N_VALUE)),
            dma((2, N_X)),
            dma((2, N_X)),
            dma((2, N_X - 1)),
            dma((2, N_X - 1)),
            dma((N_VALUE,)),
            dma((N_VALUE,)),
        ],
        compiler_params=pltpu.CompilerParams(
            collective_id=0, has_side_effects=True, vmem_limit_bytes=56 * 2**20
        ),
        name="delta_steps",
    )(
        finished.transpose(0, 2, 1),
        new_owner.transpose(0, 2, 1),
        new_slot.transpose(0, 2, 1),
        log_decay,
        decay_bias,
        norm_gain,
        inputs,
        qk_weight,
        value_weight,
        output_gate_weight,
        rate_weight.T,
        out_weight,
        states,
        prefilled,
    )
    return produced.reshape(STEPS, ROWS, PIECE)


def solution(mesh):
    return jax.shard_map(
        on_device,
        mesh=mesh,
        in_specs=(
            P(None, "dp", None),
            P(None, "value"),
            P(None, "value"),
            P(None, "value"),
            P(),
            P(),
            P(),
            P("value"),
            P("value", None),
            P("dp", "value", None, None),
            P("dp", "value", None, None),
            P(),
            P(),
            P(),
        ),
        out_specs=P(None, "dp", "value"),
        check_vma=False,
    )
```
